256 devices in a mesh: lat: 8 (over y_hi, x), lon: 32 (over z, y_lo, core).
Axes of the slice: x: 4, y: 4 (y_hi: 2, y_lo: 2; y = y_hi * 2 + y_lo), z: 8, core: 2. Of those that a mesh axis runs over, the one named last changes fastest.
Arguments:
- tokens: bfloat16 [48, 384, 4, 512], P('lat', 'lon'), may hold values from -6 to 6
- region: int32 [48, 384], P('lat', 'lon'), may hold values from 1 to 3
- w_qkv: bfloat16 [512, 1536], replicated, as said below
- w_proj: bfloat16 [512, 512], replicated, may hold values from -0.25 to 0.25
- w_merge: bfloat16 [2048, 1024], replicated, may hold values from -0.125 to 0.125
- cotangent: bfloat16 [24, 192, 4, 1024], P('lat', 'lon'), may hold values from -6 to 6
Outputs:
- merged: bfloat16 [24, 192, 4, 1024], P('lat', 'lon')
- grad_tokens: bfloat16 [48, 384, 4, 512], P('lat', 'lon')
- grad_qkv: float32 [512, 1536], P('lat', 'lon')
- grad_proj: float32 [512, 512], P('lat', 'lon')
- grad_merge: float32 [2048, 1024], P('lat', 'lon')
The draws below stay inside these ranges and needn't reach their ends.
Inputs may be any that keep to these rules, and one draw needn't show every extreme that they name: `region`: a surface class per cell; attention joins only cells of one class. `w_qkv`: query, key and value columns side by side in that order.
All inputs are finite; a program needn't handle non-finite values.
Results may differ from the reference program's by a relative error of at most 0.038.
Values may be sent and summed in bfloat16 or wider, within the bound.
A program may use at most 64 MiB of HBM per device.

```python
import jax
import jax.numpy as jnp
from jax import lax

D = 512
D2 = 1024
HEADS = 8
WIN_LEV = 2
WIN_LAT = 6
WIN_LON = 12
LEV = 4
HEAD_DIM = 64
SHIFT_LAT = 3
SHIFT_LON = 6
NLAT = 48
NLON = 384
N_LAT = 8
N_LON = 32


def draw_w_qkv(key, part):
    key = jax.random.fold_in(key, 11)
    first = jax.random.fold_in(key, 0)
    base = jax.random.normal(first, (D, 3 * D), jnp.float32) * D ** (-0.5)
    return base.astype(jnp.bfloat16)


def touch_ends(array, stream_key, smallest, largest):
    spot = [jax.random.randint(jax.random.fold_in(stream_key, axis), (), 0, length) for axis, length in enumerate(array.shape)]
    longest = array.shape.index(max(array.shape))
    next_to = spot[:longest] + [(spot[longest] + 1) % array.shape[longest]] + spot[longest + 1:]
    return array.at[tuple(spot)].set(smallest).at[tuple(next_to)].set(largest)


def shard_levels(key, shape, cuts, smallest, largest):
    factor_of = 1.0
    for axis_at, shards_of in cuts:
        draws = jax.random.uniform(jax.random.fold_in(jax.random.fold_in(key, 6), axis_at), (shards_of,), jnp.float32, smallest / len(cuts), largest / len(cuts))
        factor_of = factor_of * jnp.repeat(jnp.exp(draws), shape[axis_at] // shards_of).reshape((-1,) + (1,) * (len(shape) - 1 - axis_at))
    return factor_of


def normal_values(rng, dims, scale, limit, cuts=(), held_as=jnp.bfloat16):
    entries = jax.random.normal(rng, dims, jnp.float32) * scale
    if len(cuts) > 0:
        entries = shard_levels(rng, dims, cuts, -0.22, 0.18) * entries
    return jnp.clip(entries, min=-limit, max=limit).astype(held_as)


def setup_inputs(seed: int = 0) -> dict:
    streams_of = jax.random.split(jax.random.key(seed), 7)
    tokens = normal_values(streams_of[0], (NLAT, NLON, LEV, D), 1.0, 6.0, ((0, 8), (1, 32)))
    region = touch_ends(jax.random.randint(streams_of[1], (NLAT, NLON), 1, 4), jax.random.fold_in(streams_of[1], 1), 1, 3).astype(jnp.int32)
    w_qkv = draw_w_qkv(jax.random.fold_in(streams_of[6], 71), 0)
    w_proj = normal_values(streams_of[3], (D, D), D ** -0.5, 0.25)
    w_merge = normal_values(streams_of[4], (4 * D, D2), (4 * D) ** -0.5, 0.125)
    cotangent = normal_values(streams_of[5], (NLAT // 2, NLON // 2, LEV, D2), 1.0, 6.0, ((0, 8), (1, 32)))
    return dict(tokens=tokens, region=region, w_qkv=w_qkv, w_proj=w_proj, w_merge=w_merge, cotangent=cotangent)


epsilon = 1e-05

def to_windows(block):
    h, w, l, c = block.shape
    parts = block.reshape(h // WIN_LAT, WIN_LAT, w // WIN_LON, WIN_LON, l // WIN_LEV, WIN_LEV, c)
    return parts.transpose(0, 2, 4, 1, 3, 5, 6).reshape(-1, WIN_LAT * WIN_LON * WIN_LEV, c)

def from_windows(windows, shape):
    h, w, l, c = shape
    parts = windows.reshape(h // WIN_LAT, w // WIN_LON, l // WIN_LEV, WIN_LAT, WIN_LON, WIN_LEV, c)
    return parts.transpose(0, 3, 1, 4, 2, 5, 6).reshape(h, w, l, c)

def window_labels(rolled_ids, first_row, total_rows, levels):
    rows = (first_row + jnp.arange(rolled_ids.shape[0], dtype=jnp.int32) + SHIFT_LAT) % total_rows
    wrapped = (rows < SHIFT_LAT).astype(jnp.int32)
    labels = rolled_ids * 2 + wrapped[:, None]
    full = jnp.broadcast_to(labels[:, :, None, None], (labels.shape[0], labels.shape[1], levels, 1))
    return to_windows(full)[..., 0]

def normalize(values):
    valf = values.astype(jnp.float32)
    mean_removed_input = valf - lax.optimization_barrier(jnp.mean(valf, axis=-1, keepdims=True))
    var = lax.optimization_barrier(jnp.mean(mean_removed_input * mean_removed_input, axis=-1, keepdims=True))
    return (mean_removed_input * lax.rsqrt(var + epsilon)).astype(jnp.bfloat16)

def norm_back(values, weight_gradients):
    valf = values.astype(jnp.float32)
    mean_removed_input = valf - lax.optimization_barrier(jnp.mean(valf, axis=-1, keepdims=True))
    inverse_norm_scale = lax.rsqrt(lax.optimization_barrier(jnp.mean(mean_removed_input * mean_removed_input, axis=-1, keepdims=True)) + epsilon)
    normalized_input = mean_removed_input * inverse_norm_scale
    return inverse_norm_scale * (weight_gradients - lax.optimization_barrier(jnp.mean(weight_gradients, axis=-1, keepdims=True)) - normalized_input * lax.optimization_barrier(jnp.mean(weight_gradients * normalized_input, axis=-1, keepdims=True)))

def split_heads(qkv):
    nwin, wtok, _ = qkv.shape
    query = qkv[..., :D].reshape(nwin, wtok, HEADS, HEAD_DIM).astype(jnp.float32)
    keys = qkv[..., D:2 * D].reshape(nwin, wtok, HEADS, HEAD_DIM).astype(jnp.float32)
    values = qkv[..., 2 * D:].reshape(nwin, wtok, HEADS, HEAD_DIM).astype(jnp.float32)
    return (query, keys, values)

def probabilities(query, keys, labels):
    scale = HEAD_DIM ** (-0.5)
    scores = jnp.einsum('wqhd,wkhd->whqk', query, keys) * scale
    allowed = labels[:, None, :, None] == labels[:, None, None, :]
    scores = jnp.where(allowed, scores, -1e+30)
    scores = scores - lax.optimization_barrier(jnp.max(scores, axis=-1, keepdims=True))
    expo = jnp.exp(scores)
    return expo / lax.optimization_barrier(jnp.sum(expo, axis=-1, keepdims=True))

def rounded(values):
    return lax.optimization_barrier(values.astype(jnp.bfloat16)).astype(jnp.float32)

def attend_forward(qkv, labels):
    query, keys, values = split_heads(qkv)
    probs = probabilities(query, keys, labels)
    out = jnp.einsum('whqk,wkhd->wqhd', rounded(probs), values)
    return out.astype(jnp.bfloat16).reshape(qkv.shape[0], qkv.shape[1], D)

def attend_backward(qkv, labels, d_attn):
    query, keys, values = split_heads(qkv)
    probs = probabilities(query, keys, labels)
    grad_out = d_attn.reshape(query.shape).astype(jnp.float32)
    d_probs = jnp.einsum('wqhd,wkhd->whqk', grad_out, values)
    value_gradient = jnp.einsum('whqk,wqhd->wkhd', rounded(probs), grad_out).astype(jnp.bfloat16)
    d_scores = probs * (d_probs - lax.optimization_barrier(jnp.sum(d_probs * probs, axis=-1, keepdims=True))) * HEAD_DIM ** (-0.5)
    d_scores = rounded(d_scores)
    d_query = jnp.einsum('whqk,wkhd->wqhd', d_scores, keys).astype(jnp.bfloat16)
    d_keys = jnp.einsum('whqk,wqhd->wkhd', d_scores, query).astype(jnp.bfloat16)
    joined = jnp.concatenate([d_query, d_keys, value_gradient], axis=-1)
    return joined.reshape(qkv.shape[0], qkv.shape[1], HEADS, 3, HEAD_DIM).transpose(0, 1, 3, 2, 4).reshape(qkv.shape)

def merge_tokens(level):
    h, w, l, c = level.shape
    return level.reshape(h // 2, 2, w // 2, 2, l, c).transpose(0, 2, 4, 1, 3, 5).reshape(h // 2, w // 2, l, 4 * c)

def split_tokens(stacked):
    h, w, l, c = stacked.shape
    return stacked.reshape(h, w, l, 2, 2, c // 4).transpose(0, 3, 1, 4, 2, 5).reshape(2 * h, 2 * w, l, c // 4)

def reference(tokens, region, w_qkv, w_proj, w_merge, cotangent):
    rolled = jnp.roll(tokens, (-SHIFT_LAT, -SHIFT_LON), (0, 1))
    rolled_ids = jnp.roll(region, (-SHIFT_LAT, -SHIFT_LON), (0, 1))
    labels = window_labels(rolled_ids, 0, NLAT, LEV)
    windows = to_windows(rolled)
    block_list = N_LAT * N_LON
    wtok = WIN_LAT * WIN_LON * WIN_LEV
    win_blocks = windows.reshape(block_list, -1, wtok, D)
    lab_blocks = labels.reshape(block_list, -1, wtok)

    def project(block):
        normed = normalize(block).reshape(-1, D)
        qkv = jnp.dot(normed, w_qkv, preferred_element_type=jnp.float32).astype(jnp.bfloat16)
        return (normed, qkv.reshape(block.shape[0], block.shape[1], 3 * D))

    def block_forward_pass(item):
        block, labs = item
        normed, qkv = project(block)
        attn = attend_forward(qkv, labs).reshape(-1, D)
        branch = jnp.dot(attn, w_proj, preferred_element_type=jnp.float32).reshape(block.shape)
        return (block.astype(jnp.float32) + branch).astype(jnp.bfloat16)
    hidden_blocks = lax.map(block_forward_pass, (win_blocks, lab_blocks))
    hidden = from_windows(hidden_blocks.reshape(-1, wtok, D), rolled.shape)
    level_one = jnp.roll(hidden, (SHIFT_LAT, SHIFT_LON), (0, 1))
    stacked = merge_tokens(level_one)
    flat_stacked = stacked.reshape(-1, 4 * D)
    merge_in = normalize(flat_stacked)
    merged = jnp.dot(merge_in, w_merge, preferred_element_type=jnp.float32).astype(jnp.bfloat16)
    merged = merged.reshape(stacked.shape[0], stacked.shape[1], LEV, D2)
    flat_cot = cotangent.reshape(-1, D2)
    grad_merge = jnp.dot(merge_in.T, flat_cot, preferred_element_type=jnp.float32)
    d_merge_in = jnp.dot(flat_cot, w_merge.T, preferred_element_type=jnp.float32).astype(jnp.bfloat16)
    d_stacked = norm_back(flat_stacked, d_merge_in.astype(jnp.float32)).astype(jnp.bfloat16)
    d_level = split_tokens(d_stacked.reshape(stacked.shape))
    d_hidden = jnp.roll(d_level, (-SHIFT_LAT, -SHIFT_LON), (0, 1))
    dh_blocks = to_windows(d_hidden).reshape(block_list, -1, wtok, D)

    def backward_block(carry, item):
        acc_qkv, acc_proj = carry
        block, labs, d_block = item
        normed, qkv = project(block)
        attn = attend_forward(qkv, labs).reshape(-1, D)
        flat_dh = d_block.reshape(-1, D)
        acc_proj = acc_proj + jnp.dot(attn.T, flat_dh, preferred_element_type=jnp.float32)
        d_attn = jnp.dot(flat_dh, w_proj.T, preferred_element_type=jnp.float32).astype(jnp.bfloat16)
        d_qkv = attend_backward(qkv, labs, d_attn.reshape(block.shape)).reshape(-1, 3 * D)
        acc_qkv = acc_qkv + jnp.dot(normed.T, d_qkv, preferred_element_type=jnp.float32)
        d_normed = jnp.dot(d_qkv, w_qkv.T, preferred_element_type=jnp.float32)
        d_in = flat_dh.astype(jnp.float32) + norm_back(block.reshape(-1, D), d_normed)
        return ((acc_qkv, acc_proj), d_in.astype(jnp.bfloat16).reshape(block.shape))
    start = (jnp.zeros((D, 3 * D), jnp.float32), jnp.zeros((D, D), jnp.float32))
    (grad_qkv, grad_proj), din_blocks = lax.scan(backward_block, start, (win_blocks, lab_blocks, dh_blocks))
    d_rolled = from_windows(din_blocks.reshape(-1, wtok, D), rolled.shape)
    grad_tokens = jnp.roll(d_rolled, (SHIFT_LAT, SHIFT_LON), (0, 1))
    return (merged, grad_tokens, grad_qkv, grad_proj, grad_merge)
```

```python
import jax
import jax.numpy as jnp
from jax import lax
from jax.experimental import pallas as pl
from jax.experimental.pallas import tpu as pltpu
from jax.sharding import PartitionSpec as P

MESH = pl.DeviceIdType.MESH

D = 512
HEADS = 8
WIN_LEV = 2
WIN_LAT = 6
WIN_LON = 12
HEAD_DIM = 64
SHIFT_LAT = 3
SHIFT_LON = 6


epsilon = 1e-05


def for_sending(x):

    def short(part):
        return part.astype(jnp.bfloat16) if part.dtype == jnp.float32 else part

    return jax.tree.map(short, x)


def from_behind(value, axis, steps):
    count = lax.axis_size(axis)
    pairs = [(source, (source + steps) % count) for source in range(count)]
    return lax.ppermute(value, axis, pairs)


def to_windows(block):
    h, w, l, c = block.shape
    parts = block.reshape(h // WIN_LAT, WIN_LAT, w // WIN_LON, WIN_LON, l // WIN_LEV, WIN_LEV, c)
    return parts.transpose(0, 2, 4, 1, 3, 5, 6).reshape(-1, WIN_LAT * WIN_LON * WIN_LEV, c)


def from_windows(windows, shape):
    h, w, l, c = shape
    parts = windows.reshape(h // WIN_LAT, w // WIN_LON, l // WIN_LEV, WIN_LAT, WIN_LON, WIN_LEV, c)
    return parts.transpose(0, 3, 1, 4, 2, 5, 6).reshape(h, w, l, c)


def window_labels(rolled_ids, first_row, total_rows, levels):
    rows = (first_row + jnp.arange(rolled_ids.shape[0], dtype=jnp.int32) + SHIFT_LAT) % total_rows
    wrapped = (rows < SHIFT_LAT).astype(jnp.int32)
    labels = rolled_ids * 2 + wrapped[:, None]
    full = jnp.broadcast_to(labels[:, :, None, None], (labels.shape[0], labels.shape[1], levels, 1))
    return to_windows(full)[..., 0]


def normalize(values):
    valf = values.astype(jnp.float32)
    mean_removed_input = valf - jnp.mean(valf, axis=-1, keepdims=True)
    var = jnp.mean(mean_removed_input * mean_removed_input, axis=-1, keepdims=True)
    return (mean_removed_input * lax.rsqrt(var + epsilon)).astype(jnp.bfloat16)


def norm_back(values, weight_gradients):
    valf = values.astype(jnp.float32)
    mean_removed_input = valf - jnp.mean(valf, axis=-1, keepdims=True)
    inverse_norm_scale = lax.rsqrt(
        jnp.mean(mean_removed_input * mean_removed_input, axis=-1, keepdims=True) + epsilon
    )
    normalized_input = mean_removed_input * inverse_norm_scale
    return inverse_norm_scale * (
        weight_gradients
        - jnp.mean(weight_gradients, axis=-1, keepdims=True)
        - normalized_input * jnp.mean(weight_gradients * normalized_input, axis=-1, keepdims=True)
    )


def split_heads(qkv):
    nwin, wtok, _ = qkv.shape
    query = qkv[..., :D].reshape(nwin, wtok, HEADS, HEAD_DIM)
    keys = qkv[..., D : 2 * D].reshape(nwin, wtok, HEADS, HEAD_DIM)
    values = qkv[..., 2 * D :].reshape(nwin, wtok, HEADS, HEAD_DIM)
    return (query, keys, values)


def probabilities(query, keys, labels):
    scale = HEAD_DIM ** (-0.5)
    scores = jnp.einsum("wqhd,wkhd->whqk", query, keys, preferred_element_type=jnp.float32) * scale
    allowed = labels[:, None, :, None] == labels[:, None, None, :]
    scores = jnp.where(allowed, scores, -1e30)
    scores = scores - jnp.max(scores, axis=-1, keepdims=True)
    expo = jnp.exp(scores)
    return expo / jnp.sum(expo, axis=-1, keepdims=True)


def attend_forward(qkv, labels):
    query, keys, values = split_heads(qkv)
    probs = probabilities(query, keys, labels).astype(jnp.bfloat16)
    out = jnp.einsum("whqk,wkhd->wqhd", probs, values, preferred_element_type=jnp.float32)
    return out.astype(jnp.bfloat16).reshape(qkv.shape[0], qkv.shape[1], D)


def attend_backward(qkv, labels, d_attn):
    query, keys, values = split_heads(qkv)
    probs = probabilities(query, keys, labels)
    grad_out = d_attn.reshape(query.shape)
    d_probs = jnp.einsum("wqhd,wkhd->whqk", grad_out, values, preferred_element_type=jnp.float32)
    value_gradient = jnp.einsum(
        "whqk,wqhd->wkhd", probs.astype(jnp.bfloat16), grad_out, preferred_element_type=jnp.float32
    ).astype(jnp.bfloat16)
    d_scores = (
        probs * (d_probs - jnp.sum(d_probs * probs, axis=-1, keepdims=True)) * HEAD_DIM ** (-0.5)
    )
    d_scores = d_scores.astype(jnp.bfloat16)
    d_query = jnp.einsum(
        "whqk,wkhd->wqhd", d_scores, keys, preferred_element_type=jnp.float32
    ).astype(jnp.bfloat16)
    d_keys = jnp.einsum(
        "whqk,wqhd->wkhd", d_scores, query, preferred_element_type=jnp.float32
    ).astype(jnp.bfloat16)
    joined = jnp.concatenate([d_query, d_keys, value_gradient], axis=-1)
    return (
        joined.reshape(qkv.shape[0], qkv.shape[1], HEADS, 3, HEAD_DIM)
        .transpose(0, 1, 3, 2, 4)
        .reshape(qkv.shape)
    )


def merge_tokens(level):
    h, w, l, c = level.shape
    return (
        level.reshape(h // 2, 2, w // 2, 2, l, c)
        .transpose(0, 2, 4, 1, 3, 5)
        .reshape(h // 2, w // 2, l, 4 * c)
    )


def split_tokens(stacked):
    h, w, l, c = stacked.shape
    return (
        stacked.reshape(h, w, l, 2, 2, c // 4)
        .transpose(0, 3, 1, 4, 2, 5)
        .reshape(2 * h, 2 * w, l, c // 4)
    )


def lat_in(block, cell_ids):
    rims = from_behind((block[:SHIFT_LAT], for_sending(cell_ids[:SHIFT_LAT])), "lat", -1)
    return (
        jnp.concatenate([block[SHIFT_LAT:], rims[0]], axis=0),
        jnp.concatenate([cell_ids[SHIFT_LAT:], rims[1]], axis=0),
    )


def lon_in(block, cell_ids):
    rims = from_behind((block[:, :SHIFT_LON], cell_ids[:, :SHIFT_LON]), "lon", -1)
    return (
        jnp.concatenate([block[:, SHIFT_LON:], rims[0]], axis=1),
        jnp.concatenate([cell_ids[:, SHIFT_LON:], rims[1]], axis=1),
    )


def roll_in(block, cell_ids):
    block, cell_ids = lon_in(block, cell_ids)
    return lat_in(block, cell_ids)


def roll_out(block):
    rows = block.shape[0]
    cols = block.shape[1]
    rim_cols = from_behind(block[:, cols - SHIFT_LON :], "lon", 1)
    block = jnp.concatenate([rim_cols, block[:, : cols - SHIFT_LON]], axis=1)
    rim_rows = from_behind(block[rows - SHIFT_LAT :], "lat", 1)
    return jnp.concatenate([rim_rows, block[: rows - SHIFT_LAT]], axis=0)


def place():
    lat = lax.axis_index("lat")
    lon = lax.axis_index("lon")
    return lat // 4, lat % 4, lon // 4, (lon // 2) % 2, lon % 2


def device(y_hi, x, z, y_lo, core):
    return (y_hi * 4 + x, z * 4 + y_lo * 2 + core)


def remote(src, dst, send, recv, target):
    copy = pltpu.make_async_remote_copy(
        src_ref=src, dst_ref=dst, send_sem=send, recv_sem=recv, device_id=target, device_id_type=MESH
    )
    copy.start()
    return copy


def f32(x):
    return x.astype(jnp.float32)


def sum_kernel(small, large, out_small, out_large, *scratch):
    y_hi, x, z, y_lo, core = place()
    y = y_hi * 2 + y_lo
    ys = [(y + k) % 4 for k in range(1, 4)]
    zs = [(z + k) % 8 for k in range(1, 8)]
    xs = [(x + k) % 4 for k in range(1, 4)]
    partners = [device(y_hi, x, z, y_lo, 1 - core)]
    partners += [device(t // 2, x, z, t % 2, core) for t in ys]
    partners += [device(y_hi, x, t, y_lo, core) for t in zs]
    partners += [device(y_hi, t, z, y_lo, core) for t in xs]
    barrier = pltpu.get_barrier_semaphore()
    for target in partners:
        pl.semaphore_signal(barrier, inc=1, device_id=target, device_id_type=MESH)
    pl.semaphore_wait(barrier, len(partners))

    jobs = []
    for index, (src, out) in enumerate(((small, out_small), (large, out_large))):
        jobs.append((src, out) + scratch[index * 9 : index * 9 + 9])
    pending = []
    for src, out, r1, a1, r2, a2, r3, a3, r4, send, recv in jobs:
        pending.append([remote(src.at[:, :, 1 - core], r1, send.at[0], recv.at[0], partners[0])])
    for index, (src, out, r1, a1, r2, a2, r3, a3, r4, send, recv) in enumerate(jobs):
        for copy in pending[index]:
            copy.wait()
        half = a1.shape[-1] // 2

        @pl.loop(0, 8)
        def _(step):
            for row in range(2):
                a1[step, row] = (f32(src[step, row, core]) + f32(r1[step, row])).astype(jnp.bfloat16)

        pending[index] = [
            remote(
                a1.at[:, t % 2, :, pl.ds(pl.multiple_of((t // 2) * half, half), half)],
                r2.at[k],
                send.at[1 + k],
                recv.at[1 + k],
                partners[1 + k],
            )
            for k, t in enumerate(ys)
        ]
    for index, (src, out, r1, a1, r2, a2, r3, a3, r4, send, recv) in enumerate(jobs):
        for copy in pending[index]:
            copy.wait()
        half = a1.shape[-1] // 2

        @pl.loop(0, 8)
        def _(step):
            own = f32(a1[step, y_lo, :, pl.ds(pl.multiple_of(y_hi * half, half), half)])
            a2[step] = (own + f32(r2[0, step]) + f32(r2[1, step]) + f32(r2[2, step])).astype(jnp.bfloat16)

        pending[index] = [
            remote(a2.at[t], r3.at[k], send.at[4 + k], recv.at[4 + k], partners[4 + k]) for k, t in enumerate(zs)
        ]
    for index, (src, out, r1, a1, r2, a2, r3, a3, r4, send, recv) in enumerate(jobs):
        for copy in pending[index]:
            copy.wait()
        total = f32(a2[z])
        for k in range(7):
            total = total + f32(r3[k])
        a3[...] = total.astype(jnp.bfloat16)
        width = r4.shape[-1]
        share = 4 // (a3.shape[-1] // width)
        pending[index] = [
            remote(
                a3.at[:, pl.ds(pl.multiple_of((t // share) * width, width), width)],
                r4.at[k],
                send.at[11 + k],
                recv.at[11 + k],
                partners[11 + k],
            )
            for k, t in enumerate(xs)
        ]
    for index, (src, out, r1, a1, r2, a2, r3, a3, r4, send, recv) in enumerate(jobs):
        for copy in pending[index]:
            copy.wait()
        width = r4.shape[-1]
        share = 4 // (a3.shape[-1] // width)
        total = f32(a3[:, pl.ds(pl.multiple_of((x // share) * width, width), width)])
        for k in range(3):
            total = total + f32(r4[k])
        out[...] = total


def reduce_weight_gradients(grad_qkv, grad_proj, grad_merge):
    small = jnp.concatenate(
        [grad_qkv.reshape(32, 48, D), grad_proj.reshape(32, 16, D)], axis=1
    ).reshape(8, 2, 2, 64, D)
    large = grad_merge.reshape(8, 2, 2, 32, 4 * D)
    scratch = []
    for rows, lanes, width in ((64, D, 128), (32, 4 * D, 256)):
        half = lanes // 2
        scratch += [
            pltpu.VMEM((8, 2, rows, lanes), jnp.bfloat16),
            pltpu.VMEM((8, 2, rows, lanes), jnp.bfloat16),
            pltpu.VMEM((3, 8, rows, half), jnp.bfloat16),
            pltpu.VMEM((8, rows, half), jnp.bfloat16),
            pltpu.VMEM((7, rows, half), jnp.bfloat16),
            pltpu.VMEM((rows, half), jnp.bfloat16),
            pltpu.VMEM((3, rows, width), jnp.bfloat16),
            pltpu.SemaphoreType.DMA((14,)),
            pltpu.SemaphoreType.DMA((14,)),
        ]
    vmem = pl.BlockSpec(memory_space=pltpu.VMEM)
    out_small, out_large = pl.pallas_call(
        sum_kernel,
        out_shape=(
            jax.ShapeDtypeStruct((64, 128), jnp.float32),
            jax.ShapeDtypeStruct((32, 256), jnp.float32),
        ),
        in_specs=[vmem, vmem],
        out_specs=(vmem, vmem),
        scratch_shapes=scratch,
        compiler_params=pltpu.CompilerParams(
            collective_id=0, has_side_effects=True, vmem_limit_bytes=48 * 1024 * 1024
        ),
    )(small, large)
    odd = lax.axis_index("lat") % 2 == 1
    mine = jnp.where(odd, out_small[:, 64:], out_small[:, :64])
    return (mine[:48].T, mine[48:].T, out_large.T)


def shards(tokens, region, w_qkv, w_proj, w_merge, cotangent):
    lat_rows = tokens.shape[0]
    levels = tokens.shape[2]
    first_row = lax.axis_index("lat") * lat_rows
    total_rows = lax.axis_size("lat") * lat_rows
    rolled, rolled_ids = roll_in(tokens, region)
    labels = window_labels(rolled_ids, first_row, total_rows, levels)
    windows = to_windows(rolled)
    flat_norm = normalize(windows).reshape(-1, D)
    qkv = jnp.dot(flat_norm, w_qkv, preferred_element_type=jnp.float32).astype(jnp.bfloat16)
    qkv = qkv.reshape(windows.shape[0], windows.shape[1], 3 * D)
    flat_attn = attend_forward(qkv, labels).reshape(-1, D)
    branch = jnp.dot(flat_attn, w_proj, preferred_element_type=jnp.float32).reshape(windows.shape)
    hidden = from_windows((windows.astype(jnp.float32) + branch).astype(jnp.bfloat16), rolled.shape)
    level_one = roll_out(hidden)
    stacked = merge_tokens(level_one)
    flat_stacked = stacked.reshape(-1, 4 * D)
    merge_in = normalize(flat_stacked)
    merged = jnp.dot(merge_in, w_merge, preferred_element_type=jnp.float32).astype(jnp.bfloat16)
    merged = merged.reshape(stacked.shape[0], stacked.shape[1], levels, w_merge.shape[1])
    flat_cot = cotangent.reshape(-1, w_merge.shape[1])
    grad_merge = jnp.dot(flat_cot.T, merge_in, preferred_element_type=jnp.float32).astype(jnp.bfloat16)
    d_merge_in = jnp.dot(flat_cot, w_merge.T, preferred_element_type=jnp.float32).astype(
        jnp.bfloat16
    )
    d_stacked = norm_back(flat_stacked, d_merge_in.astype(jnp.float32)).astype(jnp.bfloat16)
    d_level = split_tokens(d_stacked.reshape(stacked.shape))
    d_hidden, back_ids = roll_in(d_level, region)
    back_labels = window_labels(back_ids, first_row, total_rows, levels)
    flat_dh = to_windows(d_hidden).reshape(-1, D)
    grad_proj = jnp.dot(flat_dh.T, flat_attn, preferred_element_type=jnp.float32).astype(jnp.bfloat16)
    d_attn = jnp.dot(flat_dh, w_proj.T, preferred_element_type=jnp.float32).astype(jnp.bfloat16)
    d_qkv = attend_backward(qkv, back_labels, d_attn.reshape(windows.shape)).reshape(-1, 3 * D)
    grad_qkv = jnp.dot(d_qkv.T, flat_norm, preferred_element_type=jnp.float32).astype(jnp.bfloat16)
    d_normed = jnp.dot(d_qkv, w_qkv.T, preferred_element_type=jnp.float32)
    d_in = (flat_dh.astype(jnp.float32) + norm_back(windows.reshape(-1, D), d_normed)).astype(
        jnp.bfloat16
    )
    grad_tokens = roll_out(from_windows(d_in.reshape(windows.shape), rolled.shape))
    summed = reduce_weight_gradients(grad_qkv, grad_proj, grad_merge)
    return (merged, grad_tokens, summed[0], summed[1], summed[2])


def solution(mesh):
    return jax.shard_map(
        shards,
        mesh=mesh,
        in_specs=(
            P("lat", "lon", None, None),
            P("lat", "lon"),
            P(),
            P(),
            P(),
            P("lat", "lon", None, None),
        ),
        out_specs=(
            P("lat", "lon", None, None),
            P("lat", "lon", None, None),
            P("lat", "lon"),
            P("lat", "lon"),
            P("lat", "lon"),
        ),
        check_vma=False,
    )
```

```python
import jax
import jax.numpy as jnp
import numpy as np
from jax import lax
from jax.experimental import pallas as pl
from jax.experimental.pallas import tpu as pltpu
from jax.sharding import PartitionSpec as P

MESH = pl.DeviceIdType.MESH
BF = jnp.bfloat16
F32 = jnp.float32
D = 512
D2 = 1024
TOK = 288
WTOK = 144
MTOK = 72
MPAD = 80
RIM = 48
EPS = 1e-05


def f32(x):
    return x.astype(F32)


def nn(a, b):
    return jnp.dot(a, b, preferred_element_type=F32)


def nt(a, b):
    return lax.dot_general(a, b, (((1,), (1,)), ((), ())), preferred_element_type=F32)


def tn(a, b):
    return lax.dot_general(a, b, (((0,), (0,)), ((), ())), preferred_element_type=F32)


def one_hot_moves():
    into = np.zeros((TOK, TOK))
    part = np.zeros((TOK, TOK))
    rim = np.zeros((RIM, TOK))
    late = np.zeros((WTOK, RIM))
    for r in range(6):
        for c in range(12):
            for l in range(4):
                natural = ((r // 3) * 2 + c // 6) * 72 + (r % 3) * 24 + (c % 6) * 4 + l
                window = (l // 2) * WTOK + r * 24 + c * 2 + l % 2
                into[window, natural] = 1
                if r == 0:
                    rim[c * 4 + l, window] = 1
                else:
                    part[(((r - 1) % 2) * 2 + c % 2) * 72 + ((r - 1) // 2) * 24 + (c // 2) * 4 + l, window] = 1
    for c in range(12):
        for l in range(4):
            late[(c % 2) * 72 + 48 + (c // 2) * 4 + l, c * 4 + l] = 1
    rows = [into, into.T, part, part.T, rim, late.T, late, rim.T]
    rows = [np.pad(m, ((0, 0), (0, TOK - m.shape[1]))) for m in rows]
    return np.concatenate(rows, axis=0).astype(jnp.bfloat16)


SCRATCH = dict(
    moves=pltpu.VMEM((1680, TOK), BF),
    w_qkv=pltpu.VMEM((D, 3 * D), BF),
    w_proj=pltpu.VMEM((D, D), BF),
    w_merge=pltpu.VMEM((4 * D, D2), BF),
    halo=pltpu.VMEM((4, 3, 6, 4, D), BF),
    classes=pltpu.VMEM((3, 6, 12), jnp.int32),
    cot=pltpu.VMEM((3, 6, 4, D2), BF),
    normed=pltpu.VMEM((TOK, D), BF),
    rolled=pltpu.VMEM((TOK, D), BF),
    xhat=pltpu.VMEM((TOK, D), F32),
    qkv=pltpu.VMEM((TOK, 3 * D), BF),
    probs=pltpu.VMEM((16, WTOK, WTOK), F32),
    attn=pltpu.VMEM((TOK, D), BF),
    rim_out=pltpu.VMEM((RIM, D), BF),
    rim_in=pltpu.VMEM((RIM, D), BF),
    drim_out=pltpu.VMEM((RIM, D), BF),
    drim_in=pltpu.VMEM((RIM, D), BF),
    merge_in=pltpu.VMEM((MPAD, 4 * D), BF),
    merged=pltpu.VMEM((3, 6, 4, D2), BF),
    cots=pltpu.VMEM((8, MPAD, D2), BF),
    merges=pltpu.VMEM((8, MPAD, 256), BF),
    d_hidden=pltpu.VMEM((TOK, D), BF),
    d_attn=pltpu.VMEM((TOK, D), BF),
    d_qkv=pltpu.VMEM((TOK, 3 * D), BF),
    d_tokens=pltpu.VMEM((4, 3, 6, 4, D), BF),
    c0=pltpu.VMEM((8, 2, 2, 64, D), BF),
    c0_in=pltpu.VMEM((8, 2, 64, D), BF),
    c1=pltpu.VMEM((8, 2, 64, D), BF),
    c1_in=pltpu.VMEM((3, 8, 64, D // 2), BF),
    c2=pltpu.VMEM((8, 64, D // 2), BF),
    c2_in=pltpu.VMEM((7, 64, D // 2), BF),
    c3=pltpu.VMEM((64, D // 2), BF),
    c3_in=pltpu.VMEM((3, 64, 128), BF),
    m0=pltpu.VMEM((8, 2, 2, 32, 256), BF),
    m0_in=pltpu.VMEM((8, 2, 32, 256), BF),
    m1=pltpu.VMEM((8, 2, 32, 256), BF),
    m1_in=pltpu.VMEM((8, 32, 256), BF),
    m2=pltpu.VMEM((8, 32, 256), BF),
    m2_in=pltpu.VMEM((7, 32, 256), BF),
    local=pltpu.SemaphoreType.DMA((10,)),
    send=pltpu.SemaphoreType.DMA((64,)),
    recv=pltpu.SemaphoreType.DMA((64,)),
)


class Scratch:
    def __init__(self, refs):
        for name, ref in zip(SCRATCH, refs, strict=True):
            setattr(self, name, ref)


def norm_back(xhat, inverse, g):
    mean_g = jnp.mean(g, axis=-1, keepdims=True)
    mean_gx = jnp.mean(g * xhat, axis=-1, keepdims=True)
    return inverse * (g - mean_g - xhat * mean_gx)


def same_class(region, classes, lat):
    cell = lax.broadcasted_iota(jnp.int32, (12, WTOK), 1)
    column = (cell % 24) // 2
    source = lax.broadcasted_iota(jnp.int32, (12, WTOK), 0)
    from_west = f32((column + 6 == source)).astype(BF)
    from_east = f32((column - 6 == source)).astype(BF)
    row = lax.broadcasted_iota(jnp.int32, (6, WTOK), 1) // 24
    line = lax.broadcasted_iota(jnp.int32, (6, WTOK), 0)
    top = f32(row + 3 == line)
    bottom = f32(row - 3 == line)
    blocks = [f32(region[...]).astype(BF)] + [f32(classes[k]).astype(BF) for k in range(3)]
    own = (nn(blocks[0], from_west) + nn(blocks[1], from_east)) * top
    below = (nn(blocks[2], from_west) + nn(blocks[3], from_east)) * bottom
    label = 2.0 * jnp.sum(own + below, axis=0, keepdims=True)
    wraps = jnp.where(lat == 7, 1.0, 0.0)
    label = label + wraps * f32(lax.broadcasted_iota(jnp.int32, (1, WTOK), 1) >= 72)
    spread = jnp.broadcast_to(label, (8, WTOK)).astype(BF)
    down = tn(spread, jnp.full((8, WTOK), 0.125, BF))
    return down == label


def kernel(
    tokens, region, w_qkv, w_proj, w_merge, cotangent, moves,
    merged_out, tokens_out, qkv_out, proj_out, merge_out, *scratch
):
    s = Scratch(scratch)
    lat = lax.axis_index("lat")
    lon = lax.axis_index("lon")
    y_hi, x, z, y_lo, core = lat // 4, lat % 4, lon // 4, (lon // 2) % 2, lon % 2
    y = y_hi * 2 + y_lo
    south, north = (lat + 1) % 8, (lat + 7) % 8
    east, west = (lon + 1) % 32, (lon + 31) % 32

    def chip(y_hi, x, z, y_lo, core):
        return (y_hi * 4 + x, z * 4 + y_lo * 2 + core)

    back = [(lat, west), (north, lon), (north, west)]
    ahead = [(lat, east), (south, lon), (south, east)]
    ys = [(y + k) % 4 for k in range(1, 4)]
    zs = [(z + k) % 8 for k in range(1, 8)]
    xs = [(x + k) % 4 for k in range(1, 4)]
    lats = [(lat + k) % 8 for k in range(1, 8)]
    other_core = chip(y_hi, x, z, y_lo, 1 - core)
    y_chips = [chip(t // 2, x, z, t % 2, core) for t in ys]
    z_chips = [chip(y_hi, x, t, y_lo, core) for t in zs]
    x_chips = [chip(y_hi, t, z, y_lo, core) for t in xs]
    lat_chips = [(t, lon) for t in lats]
    y_lo_chip = chip(y_hi, x, z, 1 - y_lo, core)
    partners = back + ahead + [other_core] + y_chips + z_chips + x_chips + lat_chips

    used = iter(range(64))

    def push(src, dst, target):
        at = next(used)
        copy = pltpu.make_async_remote_copy(
            src_ref=src,
            dst_ref=dst,
            send_sem=s.send.at[at],
            recv_sem=s.recv.at[at],
            device_id=target,
            device_id_type=MESH,
        )
        copy.start()
        return copy

    held = iter(range(10))

    def fetch(src, dst):
        copy = pltpu.make_async_copy(src, dst, s.local.at[next(held)])
        copy.start()
        return copy

    def wait(copies):
        for copy in copies:
            copy.wait()

    barrier = pltpu.get_barrier_semaphore()
    for target in partners:
        pl.semaphore_signal(barrier, inc=1, device_id=target, device_id_type=MESH)
    own_tokens = fetch(tokens.at[3:6, 6:12], s.halo.at[0])
    own_moves = fetch(moves, s.moves)
    own_qkv = fetch(w_qkv, s.w_qkv)
    own_proj = fetch(w_proj, s.w_proj)
    own_cot = fetch(cotangent.at[2:3, 3:6], s.cot.at[0:1, 0:3])
    own_merge = fetch(w_merge, s.w_merge)
    pl.semaphore_wait(barrier, len(partners))
    halos = [
        push(tokens.at[3:6, 0:6], s.halo.at[1], back[0]),
        push(tokens.at[0:3, 6:12], s.halo.at[2], back[1]),
        push(tokens.at[0:3, 0:6], s.halo.at[3], back[2]),
    ]
    class_halos = [push(region, s.classes.at[k], back[k]) for k in range(3)]
    cot_halos = [
        push(cotangent.at[2:3, 0:3], s.cot.at[0:1, 3:6], back[0]),
        push(cotangent.at[0:2, 3:6], s.cot.at[1:3, 0:3], back[1]),
        push(cotangent.at[0:2, 0:3], s.cot.at[1:3, 3:6], back[2]),
    ]
    wait([own_moves, own_tokens] + class_halos + halos)

    same = same_class(region, s.classes, lat)
    rolled = nn(s.moves[0:288], s.halo[...].reshape(TOK, D))
    s.rolled[...] = rolled.astype(BF)
    centred = rolled - jnp.mean(rolled, axis=-1, keepdims=True)
    inverse = lax.rsqrt(jnp.mean(centred * centred, axis=-1, keepdims=True) + EPS)
    xhat = centred * inverse
    s.xhat[...] = xhat
    s.normed[...] = xhat.astype(BF)
    wait([own_qkv])
    normed = s.normed[...]
    for part in range(3):
        cols = slice(part * D, part * D + D)
        made = nn(normed, s.w_qkv[:, cols]).astype(BF)
        s.qkv[:, cols] = made * jnp.asarray(0.125, BF) if part == 0 else made

    wait([own_cot] + cot_halos)
    cot_rows = jnp.concatenate([f32(s.cot[...].reshape(MTOK, D2)), jnp.zeros((MPAD - MTOK, D2), F32)], axis=0)
    s.cots[0] = cot_rows.astype(BF)
    cot_sends = [push(s.cots.at[0], s.cots.at[k + 1], lat_chips[k]) for k in range(7)]

    lane = lax.broadcasted_iota(jnp.int32, (1, 128), 1)
    halves = [f32(lane < 64).astype(BF), f32(lane >= 64).astype(BF)]
    low = lax.broadcasted_iota(jnp.int32, (WTOK, 128), 1) < 64

    for w in range(2):
        rows = slice(w * WTOK, w * WTOK + WTOK)
        for pair in range(4):
            lo = pair * 128
            query = s.qkv[rows, lo : lo + 128]
            keys = s.qkv[rows, D + lo : D + lo + 128]
            values = s.qkv[rows, 2 * D + lo : 2 * D + lo + 128]
            out = []
            for half in range(2):
                scores = jnp.where(same, nt(keys, query * halves[half]), -1e30)
                expo = jnp.exp(scores - jnp.max(scores, axis=0, keepdims=True))
                probs = expo * (1.0 / jnp.sum(expo, axis=0, keepdims=True))
                s.probs[w * 8 + pair * 2 + half] = probs
                out.append(tn(probs.astype(BF), values))
            s.attn[rows, lo : lo + 128] = jnp.where(low, out[0], out[1]).astype(BF)

    wait([own_proj])
    hidden = (f32(s.rolled[...]) + nn(s.attn[...], s.w_proj[...])).astype(BF)
    s.rim_out[...] = nn(s.moves[1152:1200], hidden).astype(BF)
    rim_copy = push(s.rim_out, s.rim_in, back[1])

    parts = nn(s.moves[576:864], hidden)
    wait([own_merge])
    cot_own = s.cots[0]
    d_merge_in = [nt(cot_own, s.w_merge[r * D : r * D + D, :]).astype(BF) for r in range(4)]
    wait([rim_copy])
    arrived = nn(s.moves[1248:1392, 0:RIM], s.rim_in[...])
    corner = [parts[r * MTOK : r * MTOK + MTOK] for r in range(4)]
    corner = [corner[0], corner[1], corner[2] + arrived[:MTOK], corner[3] + arrived[MTOK:]]
    mean = sum(jnp.sum(c, axis=-1, keepdims=True) for c in corner) * (1.0 / 2048)
    corner = [c - mean for c in corner]
    var = sum(jnp.sum(c * c, axis=-1, keepdims=True) for c in corner) * (1.0 / 2048)
    m_inverse = lax.rsqrt(var + EPS)
    corner = [c * m_inverse for c in corner]
    for r in range(4):
        block = jnp.concatenate([corner[r], jnp.zeros((MPAD - MTOK, D), F32)], axis=0)
        s.merge_in[:, r * D : r * D + D] = block.astype(BF)
    merge_sends = [
        push(s.merge_in.at[:, pl.ds(pl.multiple_of(lats[k] * 256, 256), 256)], s.merges.at[k + 1], lat_chips[k])
        for k in range(7)
    ]
    s.merges[0] = s.merge_in[:, pl.ds(pl.multiple_of(lat * 256, 256), 256)]

    g = [f32(d)[:MTOK] for d in d_merge_in]
    mean_g = sum(jnp.sum(d, axis=-1, keepdims=True) for d in g) * (1.0 / 2048)
    mean_gx = sum(jnp.sum(d * c, axis=-1, keepdims=True) for d, c in zip(g, corner)) * (1.0 / 2048)
    d_corner = jnp.concatenate([m_inverse * (d - mean_g - c * mean_gx) for d, c in zip(g, corner)], axis=0).astype(BF)
    s.drim_out[...] = nn(s.moves[1200:1248, 0:WTOK], d_corner[WTOK:]).astype(BF)
    drim_copy = push(s.drim_out, s.drim_in, ahead[1])
    d_hidden = nn(s.moves[864:1152], d_corner)
    for part in range(2):
        cols = slice(part * D, part * D + D)
        made = nn(s.merge_in[...], s.w_merge[:, cols])[:MTOK].astype(BF)
        s.merged[:, :, :, cols] = made.reshape(3, 6, 4, D)
    merged_sends = [
        push(s.merged.at[0:1, 3:6], merged_out.at[2:3, 0:3], ahead[0]),
        push(s.merged.at[1:3, 0:3], merged_out.at[0:2, 3:6], ahead[1]),
        push(s.merged.at[1:3, 3:6], merged_out.at[0:2, 0:3], ahead[2]),
        fetch(s.merged.at[0:1, 0:3], merged_out.at[2:3, 3:6]),
    ]
    wait([drim_copy])
    d_hidden = (d_hidden + nn(s.moves[1392:1680, 0:RIM], s.drim_in[...])).astype(BF)
    s.d_hidden[...] = d_hidden

    s.d_attn[...] = nt(d_hidden, s.w_proj[...]).astype(BF)
    for w in range(2):
        rows = slice(w * WTOK, w * WTOK + WTOK)
        for pair in range(4):
            lo = pair * 128
            query = s.qkv[rows, lo : lo + 128]
            keys = s.qkv[rows, D + lo : D + lo + 128]
            values = s.qkv[rows, 2 * D + lo : 2 * D + lo + 128]
            grad = s.d_attn[rows, lo : lo + 128]
            d_query, d_keys, d_values = [], [], []
            for half in range(2):
                probs = s.probs[w * 8 + pair * 2 + half]
                d_probs = nt(values, grad * halves[half])
                d_scores = (probs * (d_probs - jnp.sum(d_probs * probs, axis=0, keepdims=True))).astype(BF)
                d_values.append(nn(probs.astype(BF), grad))
                d_query.append(tn(d_scores, keys))
                d_keys.append(nn(d_scores, query))
            s.d_qkv[rows, lo : lo + 128] = (jnp.where(low, d_query[0], d_query[1]) * 0.125).astype(BF)
            s.d_qkv[rows, D + lo : D + lo + 128] = jnp.where(low, d_keys[0], d_keys[1]).astype(BF)
            s.d_qkv[rows, 2 * D + lo : 2 * D + lo + 128] = jnp.where(low, d_values[0], d_values[1]).astype(BF)

    grad_proj = tn(s.d_hidden[...], s.attn[...]).astype(BF)
    for j in range(32):
        s.c0[j // 4, (j // 2) % 2, j % 2, 48:64] = grad_proj[16 * j : 16 * j + 16]
    normed = s.normed[...]
    for part in range(3):
        made = tn(s.d_qkv[:, part * D : part * D + D], normed).astype(BF)
        at = part * D
        while at < part * D + D:
            j, off = at // 48, at % 48
            n = min(48 - off, part * D + D - at)
            s.c0[j // 4, (j // 2) % 2, j % 2, off : off + n] = made[at - part * D : at - part * D + n]
            at += n
    c_copy = push(s.c0.at[:, :, 1 - core], s.c0_in, other_core)

    wait(cot_sends + merge_sends)
    merges = s.merges[...].reshape(8 * MPAD, 256)
    for part in range(4):
        cots = s.cots[:, :, part * 256 : part * 256 + 256].reshape(8 * MPAD, 256)
        made = tn(cots, merges).astype(BF)
        s.m0[2 * part : 2 * part + 2] = made.reshape(2, 2, 2, 32, 256)
    m_copy = push(s.m0.at[:, :, 1 - core], s.m0_in, other_core)

    d_normed = nt(s.d_qkv[:, 0:D], s.w_qkv[:, 0:D])
    for part in range(1, 3):
        cols = slice(part * D, part * D + D)
        d_normed = d_normed + nt(s.d_qkv[:, cols], s.w_qkv[:, cols])
    d_tokens = (f32(s.d_hidden[...]) + norm_back(s.xhat[...], inverse, d_normed)).astype(BF)
    s.d_tokens[...] = nn(s.moves[288:576], d_tokens).astype(BF).reshape(4, 3, 6, 4, D)
    token_sends = [
        push(s.d_tokens.at[1], tokens_out.at[3:6, 0:6], ahead[0]),
        push(s.d_tokens.at[2], tokens_out.at[0:3, 6:12], ahead[1]),
        push(s.d_tokens.at[3], tokens_out.at[0:3, 0:6], ahead[2]),
        fetch(s.d_tokens.at[0], tokens_out.at[3:6, 6:12]),
    ]

    wait([c_copy])

    @pl.loop(0, 8)
    def _(step):
        for row in range(2):
            s.c1[step, row] = (f32(s.c0[step, row, core]) + f32(s.c0_in[step, row])).astype(BF)

    c_copies = [
        push(
            s.c1.at[:, t % 2, :, pl.ds(pl.multiple_of((t // 2) * 256, 256), 256)], s.c1_in.at[k], y_chips[k]
        )
        for k, t in enumerate(ys)
    ]
    wait([m_copy])

    @pl.loop(0, 8)
    def _(step):
        for row in range(2):
            s.m1[step, row] = (f32(s.m0[step, row, core]) + f32(s.m0_in[step, row])).astype(BF)

    m_copy = push(s.m1.at[:, 1 - y_lo], s.m1_in, y_lo_chip)
    wait([m_copy])

    @pl.loop(0, 8)
    def _(step):
        s.m2[step] = (f32(s.m1[step, y_lo]) + f32(s.m1_in[step])).astype(BF)

    m_copies = [push(s.m2.at[t], s.m2_in.at[k], z_chips[k]) for k, t in enumerate(zs)]
    wait(c_copies)

    @pl.loop(0, 8)
    def _(step):
        total = f32(s.c1[step, y_lo, :, pl.ds(pl.multiple_of(y_hi * 256, 256), 256)])
        for k in range(3):
            total = total + f32(s.c1_in[k, step])
        s.c2[step] = total.astype(BF)

    c_copies = [push(s.c2.at[t], s.c2_in.at[k], z_chips[k]) for k, t in enumerate(zs)]
    wait(m_copies)
    total = f32(s.m2[z])
    for k in range(7):
        total = total + f32(s.m2_in[k])
    merge_out[...] = total
    wait(c_copies)
    total = f32(s.c2[z])
    for k in range(7):
        total = total + f32(s.c2_in[k])
    s.c3[...] = total.astype(BF)
    c_copies = [
        push(s.c3.at[:, pl.ds(pl.multiple_of((t // 2) * 128, 128), 128)], s.c3_in.at[k], x_chips[k])
        for k, t in enumerate(xs)
    ]
    wait(merged_sends + token_sends + c_copies)
    total = f32(s.c3[:, pl.ds(pl.multiple_of((x // 2) * 128, 128), 128)])
    for k in range(3):
        total = total + f32(s.c3_in[k])
    mine = jnp.where(x % 2 == 1, total[:, 64:], total[:, :64])
    qkv_out[...] = mine[:48]
    proj_out[...] = mine[48:]


def shards(tokens, region, w_qkv, w_proj, w_merge, cotangent):
    hbm = pl.BlockSpec(memory_space=pltpu.HBM)
    vmem = pl.BlockSpec(memory_space=pltpu.VMEM)
    merged, grad_tokens, grad_qkv, grad_proj, grad_merge = pl.pallas_call(
        kernel,
        out_shape=(
            jax.ShapeDtypeStruct((3, 6, 4, D2), BF),
            jax.ShapeDtypeStruct((6, 12, 4, D), BF),
            jax.ShapeDtypeStruct((48, 64), F32),
            jax.ShapeDtypeStruct((16, 64), F32),
            jax.ShapeDtypeStruct((32, 256), F32),
        ),
        in_specs=[hbm, vmem, hbm, hbm, hbm, hbm, hbm],
        out_specs=(hbm, hbm, vmem, vmem, vmem),
        scratch_shapes=list(SCRATCH.values()),
        compiler_params=pltpu.CompilerParams(
            collective_id=0, has_side_effects=True, vmem_limit_bytes=56 * 1024 * 1024
        ),
    )(tokens, region, w_qkv, w_proj, w_merge, cotangent, jnp.asarray(one_hot_moves()))
    return (merged, grad_tokens, grad_qkv.T, grad_proj.T, grad_merge.T)


def solution(mesh):
    return jax.shard_map(
        shards,
        mesh=mesh,
        in_specs=(
            P("lat", "lon", None, None),
            P("lat", "lon"),
            P(),
            P(),
            P(),
            P("lat", "lon", None, None),
        ),
        out_specs=(
            P("lat", "lon", None, None),
            P("lat", "lon", None, None),
            P("lat", "lon"),
            P("lat", "lon"),
            P("lat", "lon"),
        ),
        check_vma=False,
    )
```

```python
import jax
import jax.numpy as jnp
import numpy as np
from jax import lax
from jax.experimental import pallas as pl
from jax.experimental.pallas import tpu as pltpu
from jax.sharding import PartitionSpec as P

MESH = pl.DeviceIdType.MESH
BF = jnp.bfloat16
F32 = jnp.float32
D = 512
D2 = 1024
TOK = 288
WTOK = 144
MTOK = 72
MPAD = 80
MALL = 96
RIM = 48
EPS = 1e-05


def f32(x):
    return x.astype(F32)


def nn(a, b):
    return jnp.dot(a, b, preferred_element_type=F32)


def nt(a, b):
    return lax.dot_general(a, b, (((1,), (1,)), ((), ())), preferred_element_type=F32)


def tn(a, b):
    return lax.dot_general(a, b, (((0,), (0,)), ((), ())), preferred_element_type=F32)


def one_hot_moves():
    into = np.zeros((TOK, TOK))
    part = np.zeros((4 * MALL, TOK))
    first = np.zeros((RIM, TOK))
    last = np.zeros((RIM, TOK))
    late = np.zeros((2 * MALL, RIM))
    early = np.zeros((2 * MALL, RIM))
    for c in range(12):
        for l in range(4):
            patch = (c // 2) * 4 + l
            for r in range(6):
                natural = ((r // 3) * 2 + c // 6) * 72 + (r % 3) * 24 + (c % 6) * 4 + l
                window = (l // 2) * WTOK + r * 24 + c * 2 + l % 2
                into[window, natural] = 1
                a = (r - 1) // 2 if r > 0 else 3
                part[(((r - 1) % 2) * 2 + c % 2) * MALL + a * 24 + patch, window] = 1
                if r == 0:
                    first[c * 4 + l, window] = 1
                if r == 5:
                    last[c * 4 + l, window] = 1
            late[(c % 2) * MALL + 48 + patch, c * 4 + l] = 1
            early[(c % 2) * MALL + 72 + patch, c * 4 + l] = 1
    rows = [into, into.T, part, part.T, first, last, late, early]
    rows = [np.pad(m, ((0, 0), (0, 4 * MALL - m.shape[1]))) for m in rows]
    return np.concatenate(rows, axis=0).astype(jnp.bfloat16)


SCRATCH = dict(
    moves=pltpu.VMEM((1728, 4 * MALL), BF),
    w_qkv=pltpu.VMEM((D, 3 * D), BF),
    w_proj=pltpu.VMEM((D, D), BF),
    w_merge=pltpu.VMEM((4 * D, D2), BF),
    halo=pltpu.VMEM((4, 3, 6, 4, D), BF),
    classes=pltpu.VMEM((3, 6, 12), jnp.int32),
    cot=pltpu.VMEM((8, 3, 6, 4, D2), BF),
    normed=pltpu.VMEM((TOK, D), BF),
    rolled=pltpu.VMEM((TOK, D), BF),
    xhat=pltpu.VMEM((TOK, D), F32),
    qkv=pltpu.VMEM((TOK, 3 * D), BF),
    probs=pltpu.VMEM((16, WTOK, WTOK), F32),
    attn=pltpu.VMEM((TOK, D), BF),
    first_out=pltpu.VMEM((RIM, D), BF),
    first_in=pltpu.VMEM((RIM, D), BF),
    last_out=pltpu.VMEM((RIM, D), BF),
    last_in=pltpu.VMEM((RIM, D), BF),
    merge_in=pltpu.VMEM((MALL, 4 * D), BF),
    merged=pltpu.VMEM((3, 6, 4, D2), BF),
    cots=pltpu.VMEM((8, MPAD, D2), BF),
    merges=pltpu.VMEM((8, MPAD, 256), BF),
    d_hidden=pltpu.VMEM((TOK, D), BF),
    d_attn=pltpu.VMEM((TOK, D), BF),
    d_qkv=pltpu.VMEM((TOK, 3 * D), BF),
    d_tokens=pltpu.VMEM((4, 3, 6, 4, D), BF),
    c0=pltpu.VMEM((8, 2, 2, 64, D), BF),
    c0_in=pltpu.VMEM((8, 2, 64, D), BF),
    c1=pltpu.VMEM((8, 2, 64, D), BF),
    a1_in=pltpu.VMEM((3, 8, 32, 256), BF),
    a2=pltpu.VMEM((8, 32, 256), BF),
    a2_in=pltpu.VMEM((3, 8, 32, 128), BF),
    b1_in=pltpu.VMEM((3, 8, 2, 32, 128), BF),
    b2=pltpu.VMEM((8, 2, 32, 128), BF),
    b2_in=pltpu.VMEM((3, 8, 32, 128), BF),
    c3=pltpu.VMEM((8, 32, 128), BF),
    c3_in=pltpu.VMEM((7, 32, 128), BF),
    m0=pltpu.VMEM((8, 2, 2, 32, 256), BF),
    m0_in=pltpu.VMEM((8, 2, 32, 256), BF),
    m1=pltpu.VMEM((8, 2, 32, 256), BF),
    m1_in=pltpu.VMEM((8, 32, 256), BF),
    m2=pltpu.VMEM((8, 32, 256), BF),
    m2_in=pltpu.VMEM((7, 32, 256), BF),
    local=pltpu.SemaphoreType.DMA((10,)),
    send=pltpu.SemaphoreType.DMA((80,)),
    recv=pltpu.SemaphoreType.DMA((80,)),
)


class Scratch:
    def __init__(self, refs):
        for name, ref in zip(SCRATCH, refs, strict=True):
            setattr(self, name, ref)


def norm_back(xhat, inverse, g):
    mean_g = jnp.mean(g, axis=-1, keepdims=True)
    mean_gx = jnp.mean(g * xhat, axis=-1, keepdims=True)
    return inverse * (g - mean_g - xhat * mean_gx)


def by_x(rows):
    low = lax.broadcasted_iota(jnp.int32, (rows.shape[0], 128), 1) < 64
    tiles = []
    for t in range(4):
        one = rows[:, (t // 2) * 128 : (t // 2) * 128 + 128]
        two = rows[:, 256 + (t // 2) * 128 : 256 + (t // 2) * 128 + 128]
        if t % 2 == 0:
            tiles.append(jnp.where(low, one, pltpu.roll(two, 64, 1)))
        else:
            tiles.append(jnp.where(low, pltpu.roll(one, 64, 1), two))
    return jnp.concatenate(tiles, axis=1)


def same_class(region, classes, lat):
    cell = lax.broadcasted_iota(jnp.int32, (12, WTOK), 1)
    column = (cell % 24) // 2
    source = lax.broadcasted_iota(jnp.int32, (12, WTOK), 0)
    from_west = f32((column + 6 == source)).astype(BF)
    from_east = f32((column - 6 == source)).astype(BF)
    row = lax.broadcasted_iota(jnp.int32, (6, WTOK), 1) // 24
    line = lax.broadcasted_iota(jnp.int32, (6, WTOK), 0)
    top = f32(row + 3 == line)
    bottom = f32(row - 3 == line)
    blocks = [f32(region[...]).astype(BF)] + [f32(classes[k]).astype(BF) for k in range(3)]
    own = (nn(blocks[0], from_west) + nn(blocks[1], from_east)) * top
    below = (nn(blocks[2], from_west) + nn(blocks[3], from_east)) * bottom
    label = 2.0 * jnp.sum(own + below, axis=0, keepdims=True)
    wraps = jnp.where(lat == 7, 1.0, 0.0)
    label = label + wraps * f32(lax.broadcasted_iota(jnp.int32, (1, WTOK), 1) >= 72)
    spread = jnp.broadcast_to(label, (8, WTOK)).astype(BF)
    down = tn(spread, jnp.full((8, WTOK), 0.125, BF))
    return down == label


def kernel(
    tokens, region, w_qkv, w_proj, w_merge, cotangent, moves,
    merged_out, tokens_out, qkv_out, proj_out, merge_out, *scratch
):
    s = Scratch(scratch)
    lat = lax.axis_index("lat")
    lon = lax.axis_index("lon")
    y_hi, x, z, y_lo, core = lat // 4, lat % 4, lon // 4, (lon // 2) % 2, lon % 2
    y = y_hi * 2 + y_lo
    south, north = (lat + 1) % 8, (lat + 7) % 8
    east, west = (lon + 1) % 32, (lon + 31) % 32

    def chip(y_hi, x, z, y_lo, core):
        return (y_hi * 4 + x, z * 4 + y_lo * 2 + core)

    back = [(lat, west), (north, lon), (north, west)]
    ahead = [(lat, east), (south, lon), (south, east)]
    ys = [(y + k) % 4 for k in range(1, 4)]
    zs = [(z + k) % 8 for k in range(1, 8)]
    xs = [(x + k) % 4 for k in range(1, 4)]
    lats = [(lat + k) % 8 for k in range(1, 8)]
    other_core = chip(y_hi, x, z, y_lo, 1 - core)
    y_chips = [chip(t // 2, x, z, t % 2, core) for t in ys]
    z_chips = [chip(y_hi, x, t, y_lo, core) for t in zs]
    x_chips = [chip(y_hi, t, z, y_lo, core) for t in xs]
    lat_chips = [(t, lon) for t in lats]
    y_lo_chip = chip(y_hi, x, z, 1 - y_lo, core)
    partners = back + ahead + [other_core] + y_chips + z_chips + x_chips + lat_chips

    used = iter(range(80))

    def push(src, dst, target):
        at = next(used)
        copy = pltpu.make_async_remote_copy(
            src_ref=src,
            dst_ref=dst,
            send_sem=s.send.at[at],
            recv_sem=s.recv.at[at],
            device_id=target,
            device_id_type=MESH,
        )
        copy.start()
        return copy

    held = iter(range(10))

    def fetch(src, dst):
        copy = pltpu.make_async_copy(src, dst, s.local.at[next(held)])
        copy.start()
        return copy

    def wait(copies):
        for copy in copies:
            copy.wait()

    barrier = pltpu.get_barrier_semaphore()
    for target in partners:
        pl.semaphore_signal(barrier, inc=1, device_id=target, device_id_type=MESH)
    own_tokens = fetch(tokens.at[3:6, 6:12], s.halo.at[0])
    own_moves = fetch(moves, s.moves)
    own_qkv = fetch(w_qkv, s.w_qkv)
    own_proj = fetch(w_proj, s.w_proj)
    own_cot = [
        fetch(cotangent.at[2:3, 3:6], s.cot.at[lat, 0:1, 0:3]),
        fetch(cotangent.at[0:2, 3:6], s.cot.at[north, 1:3, 0:3]),
    ]
    own_merge = fetch(w_merge, s.w_merge)
    pl.semaphore_wait(barrier, len(partners))
    class_halos = [push(region, s.classes.at[k], back[k]) for k in range(3)]
    halos = [
        push(tokens.at[0:3, 6:12], s.halo.at[2], back[1]),
        push(tokens.at[0:3, 0:6], s.halo.at[3], back[2]),
        push(tokens.at[3:6, 0:6], s.halo.at[1], back[0]),
    ]
    cot_halos = [
        push(cotangent.at[2:3, 0:3], s.cot.at[lat, 0:1, 3:6], back[0]),
        push(cotangent.at[0:2, 0:3], s.cot.at[north, 1:3, 3:6], back[0]),
    ]
    wait(own_cot + cot_halos)

    def gather_cot(offset):
        chip_at = lat_chips[offset - 1]
        return [
            push(s.cot.at[north, 1:3], s.cot.at[north, 1:3], chip_at),
            push(s.cot.at[lat, 0:1], s.cot.at[lat, 0:1], chip_at),
        ]

    to_north = gather_cot(7)
    cot_sends = gather_cot(1) + gather_cot(4)
    wait([own_moves, own_tokens] + class_halos + halos)

    same = same_class(region, s.classes, lat)
    rolled = nn(s.moves[0:288, 0:TOK], s.halo[...].reshape(TOK, D))
    s.rolled[...] = rolled.astype(BF)
    centred = rolled - jnp.mean(rolled, axis=-1, keepdims=True)
    inverse = lax.rsqrt(jnp.mean(centred * centred, axis=-1, keepdims=True) + EPS)
    xhat = centred * inverse
    s.xhat[...] = xhat
    s.normed[...] = xhat.astype(BF)
    wait([own_qkv])
    normed = s.normed[...]
    for part in range(3):
        cols = slice(part * D, part * D + D)
        made = nn(normed, s.w_qkv[:, cols]).astype(BF)
        s.qkv[:, cols] = made * jnp.asarray(0.125, BF) if part == 0 else made

    lane = lax.broadcasted_iota(jnp.int32, (1, 128), 1)
    halves = [f32(lane < 64).astype(BF), f32(lane >= 64).astype(BF)]
    low = lax.broadcasted_iota(jnp.int32, (WTOK, 128), 1) < 64

    for w in range(2):
        rows = slice(w * WTOK, w * WTOK + WTOK)
        for pair in range(4):
            lo = pair * 128
            query = s.qkv[rows, lo : lo + 128]
            keys = s.qkv[rows, D + lo : D + lo + 128]
            values = s.qkv[rows, 2 * D + lo : 2 * D + lo + 128]
            out = []
            for half in range(2):
                scores = jnp.where(same, nt(keys, query * halves[half]), -1e30)
                expo = jnp.exp(scores - jnp.max(scores, axis=0, keepdims=True))
                probs = expo * (1.0 / jnp.sum(expo, axis=0, keepdims=True))
                s.probs[w * 8 + pair * 2 + half] = probs
                out.append(tn(probs.astype(BF), values))
            s.attn[rows, lo : lo + 128] = jnp.where(low, out[0], out[1]).astype(BF)

    wait([own_proj])
    hidden = (f32(s.rolled[...]) + nn(s.attn[...], s.w_proj[...])).astype(BF)
    s.first_out[...] = nn(s.moves[1248:1296, 0:TOK], hidden).astype(BF)
    s.last_out[...] = nn(s.moves[1296:1344, 0:TOK], hidden).astype(BF)
    rims = [push(s.first_out, s.first_in, back[1]), push(s.last_out, s.last_in, ahead[1])]

    parts = nn(s.moves[576:960, 0:TOK], hidden)
    wait([own_merge] + to_north)
    cot_own = jnp.concatenate([s.cot[lat], s.cot[north, 2:3]], axis=0).reshape(MALL, D2)
    g = [f32(nt(cot_own, s.w_merge[r * D : r * D + D, :]).astype(BF)) for r in range(4)]
    wait(rims)
    cot_sends += gather_cot(2) + gather_cot(6) + gather_cot(3) + gather_cot(5)
    above = nn(s.moves[1536:1728, 0:RIM], s.last_in[...])
    below = nn(s.moves[1344:1536, 0:RIM], s.first_in[...])
    corner = [parts[r * MALL : r * MALL + MALL] for r in range(4)]
    corner = [corner[0] + above[:MALL], corner[1] + above[MALL:], corner[2] + below[:MALL], corner[3] + below[MALL:]]
    mean = sum(jnp.sum(c, axis=-1, keepdims=True) for c in corner) * (1.0 / 2048)
    corner = [c - mean for c in corner]
    var = sum(jnp.sum(c * c, axis=-1, keepdims=True) for c in corner) * (1.0 / 2048)
    m_inverse = lax.rsqrt(var + EPS)
    corner = [c * m_inverse for c in corner]
    for r in range(4):
        s.merge_in[:, r * D : r * D + D] = corner[r].astype(BF)
    merge_sends = [
        push(
            s.merge_in.at[0:MPAD, pl.ds(pl.multiple_of(lats[k] * 256, 256), 256)], s.merges.at[lat], lat_chips[k]
        )
        for k in range(7)
    ]
    s.merges[lat] = s.merge_in[0:MPAD, pl.ds(pl.multiple_of(lat * 256, 256), 256)]

    mean_g = sum(jnp.sum(d, axis=-1, keepdims=True) for d in g) * (1.0 / 2048)
    mean_gx = sum(jnp.sum(d * c, axis=-1, keepdims=True) for d, c in zip(g, corner)) * (1.0 / 2048)
    d_corner = jnp.concatenate([m_inverse * (d - mean_g - c * mean_gx) for d, c in zip(g, corner)], axis=0).astype(BF)
    d_hidden = nn(s.moves[960:1248], d_corner).astype(BF)
    s.d_hidden[...] = d_hidden

    s.d_attn[...] = nt(d_hidden, s.w_proj[...]).astype(BF)
    for w in range(2):
        rows = slice(w * WTOK, w * WTOK + WTOK)
        for pair in range(4):
            lo = pair * 128
            query = s.qkv[rows, lo : lo + 128]
            keys = s.qkv[rows, D + lo : D + lo + 128]
            values = s.qkv[rows, 2 * D + lo : 2 * D + lo + 128]
            grad = s.d_attn[rows, lo : lo + 128]
            d_query, d_keys, d_values = [], [], []
            for half in range(2):
                probs = s.probs[w * 8 + pair * 2 + half]
                d_probs = nt(values, grad * halves[half])
                d_scores = (probs * (d_probs - jnp.sum(d_probs * probs, axis=0, keepdims=True))).astype(BF)
                d_values.append(nn(probs.astype(BF), grad))
                d_query.append(tn(d_scores, keys))
                d_keys.append(nn(d_scores, query))
            s.d_qkv[rows, lo : lo + 128] = (jnp.where(low, d_query[0], d_query[1]) * 0.125).astype(BF)
            s.d_qkv[rows, D + lo : D + lo + 128] = jnp.where(low, d_keys[0], d_keys[1]).astype(BF)
            s.d_qkv[rows, 2 * D + lo : 2 * D + lo + 128] = jnp.where(low, d_values[0], d_values[1]).astype(BF)

    grad_proj = by_x(tn(s.d_hidden[...], s.attn[...])).astype(BF)
    for j in range(32):
        s.c0[j // 4, (j // 2) % 2, j % 2, 48:64] = grad_proj[16 * j : 16 * j + 16]
    normed = s.normed[...]
    for part in range(3):
        made = tn(s.d_qkv[:, part * D : part * D + D], normed)
        moved = by_x(made).astype(BF)
        made = made.astype(BF)
        for block in range(part * 32, part * 32 + 32):
            j, third = block // 3, block % 3
            rows = (moved if third == 2 else made)[16 * block - part * D : 16 * block - part * D + 16]
            s.c0[j // 4, (j // 2) % 2, j % 2, 16 * third : 16 * third + 16] = rows
    c_copy = push(s.c0.at[:, :, 1 - core], s.c0_in, other_core)

    for part in range(2):
        cols = slice(part * D, part * D + D)
        made = nn(s.merge_in[0:MPAD], s.w_merge[:, cols])[:MTOK].astype(BF)
        s.merged[:, :, :, cols] = made.reshape(3, 6, 4, D)

    wait([c_copy])

    @pl.loop(0, 8)
    def _(step):
        for row in range(2):
            s.c1[step, row] = (f32(s.c0[step, row, core]) + f32(s.c0_in[step, row])).astype(BF)

    a_copies = [
        push(
            s.c1.at[:, t % 2, 0:32, pl.ds(pl.multiple_of((t // 2) * 256, 256), 256)], s.a1_in.at[k], y_chips[k]
        )
        for k, t in enumerate(ys)
    ]
    b_copies = [
        push(s.c1.at[:, :, 32:64, pl.ds(pl.multiple_of(t * 128, 128), 128)], s.b1_in.at[k], x_chips[k])
        for k, t in enumerate(xs)
    ]

    d_normed = nt(s.d_qkv[:, 0:D], s.w_qkv[:, 0:D])
    for part in range(1, 3):
        cols = slice(part * D, part * D + D)
        d_normed = d_normed + nt(s.d_qkv[:, cols], s.w_qkv[:, cols])
    d_tokens = (f32(s.d_hidden[...]) + norm_back(s.xhat[...], inverse, d_normed)).astype(BF)
    s.d_tokens[...] = nn(s.moves[288:576, 0:TOK], d_tokens).astype(BF).reshape(4, 3, 6, 4, D)

    wait(cot_sends + merge_sends)
    for slot in range(8):
        rows = [f32(s.cot[slot].reshape(MTOK, D2)), jnp.zeros((MPAD - MTOK, D2), F32)]
        s.cots[slot] = jnp.concatenate(rows, axis=0).astype(BF)
    merges = s.merges[...].reshape(8 * MPAD, 256)
    for part in range(4):
        cots = s.cots[:, :, part * 256 : part * 256 + 256].reshape(8 * MPAD, 256)
        made = tn(cots, merges).astype(BF)
        s.m0[2 * part : 2 * part + 2] = made.reshape(2, 2, 2, 32, 256)
    m_copy = push(s.m0.at[:, :, 1 - core], s.m0_in, other_core)

    wait(a_copies + b_copies)

    @pl.loop(0, 8)
    def _(step):
        total = f32(s.c1[step, y_lo, 0:32, pl.ds(pl.multiple_of(y_hi * 256, 256), 256)])
        for k in range(3):
            total = total + f32(s.a1_in[k, step])
        s.a2[step] = total.astype(BF)
        for row in range(2):
            total = f32(s.c1[step, row, 32:64, pl.ds(pl.multiple_of(x * 128, 128), 128)])
            for k in range(3):
                total = total + f32(s.b1_in[k, step, row])
            s.b2[step, row] = total.astype(BF)

    a_copies = [
        push(s.a2.at[:, :, pl.ds(pl.multiple_of((t // 2) * 128, 128), 128)], s.a2_in.at[k], x_chips[k])
        for k, t in enumerate(xs)
    ]
    b_copies = [push(s.b2.at[:, t % 2], s.b2_in.at[k], y_chips[k]) for k, t in enumerate(ys)]
    last_sends = [
        push(s.merged.at[0:1, 3:6], merged_out.at[2:3, 0:3], ahead[0]),
        push(s.merged.at[1:3, 0:3], merged_out.at[0:2, 3:6], ahead[1]),
        push(s.merged.at[1:3, 3:6], merged_out.at[0:2, 0:3], ahead[2]),
        fetch(s.merged.at[0:1, 0:3], merged_out.at[2:3, 3:6]),
        push(s.d_tokens.at[1], tokens_out.at[3:6, 0:6], ahead[0]),
        push(s.d_tokens.at[2], tokens_out.at[0:3, 6:12], ahead[1]),
        push(s.d_tokens.at[3], tokens_out.at[0:3, 0:6], ahead[2]),
        fetch(s.d_tokens.at[0], tokens_out.at[3:6, 6:12]),
    ]
    wait([m_copy])

    @pl.loop(0, 8)
    def _(step):
        for row in range(2):
            s.m1[step, row] = (f32(s.m0[step, row, core]) + f32(s.m0_in[step, row])).astype(BF)

    m_copy = push(s.m1.at[:, 1 - y_lo], s.m1_in, y_lo_chip)
    wait(a_copies + b_copies)
    left = lax.broadcasted_iota(jnp.int32, (32, 128), 1) < 64

    @pl.loop(0, 8)
    def _(step):
        one = f32(s.a2[step, :, pl.ds(pl.multiple_of((x // 2) * 128, 128), 128)])
        two = f32(s.b2[step, y_lo])
        for k in range(3):
            one = one + f32(s.a2_in[k, step])
            two = two + f32(s.b2_in[k, step])
        one = jnp.where(x % 2 == 1, pltpu.roll(one, 64, 1), one)
        two = jnp.where(y_hi == 0, pltpu.roll(two, 64, 1), two)
        s.c3[step] = jnp.where(left, one, two).astype(BF)

    c_copies = [push(s.c3.at[t], s.c3_in.at[k], z_chips[k]) for k, t in enumerate(zs)]
    wait([m_copy])

    @pl.loop(0, 8)
    def _(step):
        s.m2[step] = (f32(s.m1[step, y_lo]) + f32(s.m1_in[step])).astype(BF)

    m_copies = [push(s.m2.at[t], s.m2_in.at[k], z_chips[k]) for k, t in enumerate(zs)]
    wait(c_copies)
    total = f32(s.c3[z])
    for k in range(7):
        total = total + f32(s.c3_in[k])
    qkv_out[0:32] = total[:, :64]
    qkv_out[32:48] = total[:16, 64:]
    proj_out[...] = total[16:, 64:]
    wait(m_copies)
    total = f32(s.m2[z])
    for k in range(7):
        total = total + f32(s.m2_in[k])
    merge_out[...] = total
    wait(last_sends)


def hand_over(*refs):
    done = refs[10]
    copies = [pltpu.make_async_copy(refs[k], refs[5 + k], done.at[k]) for k in range(5)]
    for copy in copies:
        copy.start()
    for copy in copies:
        copy.wait()


def shards(tokens, region, w_qkv, w_proj, w_merge, cotangent):
    hbm = pl.BlockSpec(memory_space=pltpu.HBM)
    vmem = pl.BlockSpec(memory_space=pltpu.VMEM)
    made = pl.pallas_call(
        kernel,
        out_shape=(
            jax.ShapeDtypeStruct((3, 6, 4, D2), BF),
            jax.ShapeDtypeStruct((6, 12, 4, D), BF),
            jax.ShapeDtypeStruct((48, 64), F32),
            jax.ShapeDtypeStruct((16, 64), F32),
            jax.ShapeDtypeStruct((32, 256), F32),
        ),
        in_specs=[hbm, vmem, hbm, hbm, hbm, hbm, hbm],
        out_specs=(hbm, hbm, vmem, vmem, vmem),
        scratch_shapes=list(SCRATCH.values()),
        compiler_params=pltpu.CompilerParams(
            collective_id=0, has_side_effects=True, vmem_limit_bytes=56 * 1024 * 1024
        ),
    )(tokens, region, w_qkv, w_proj, w_merge, cotangent, jnp.asarray(one_hot_moves()))
    merged, grad_tokens, grad_qkv, grad_proj, grad_merge = pl.pallas_call(
        hand_over,
        out_shape=tuple(jax.ShapeDtypeStruct(a.shape, a.dtype) for a in made),
        in_specs=[hbm] * 5,
        out_specs=(hbm,) * 5,
        scratch_shapes=[pltpu.SemaphoreType.DMA((5,))],
        compiler_params=pltpu.CompilerParams(vmem_limit_bytes=56 * 1024 * 1024),
    )(*made)
    return (merged, grad_tokens, grad_qkv.T, grad_proj.T, grad_merge.T)


def solution(mesh):
    return jax.shard_map(
        shards,
        mesh=mesh,
        in_specs=(
            P("lat", "lon", None, None),
            P("lat", "lon"),
            P(),
            P(),
            P(),
            P("lat", "lon", None, None),
        ),
        out_specs=(
            P("lat", "lon", None, None),
            P("lat", "lon", None, None),
            P("lat", "lon"),
            P("lat", "lon"),
            P("lat", "lon"),
        ),
        check_vma=False,
    )
```

```python
import jax
import jax.numpy as jnp
import numpy as np
from jax import lax
from jax.experimental import pallas as pl
from jax.experimental.pallas import tpu as pltpu
from jax.sharding import PartitionSpec as P

MESH = pl.DeviceIdType.MESH
BF = jnp.bfloat16
F32 = jnp.float32
D = 512
D2 = 1024
TOK = 288
WTOK = 144
MTOK = 72
MPAD = 80
MALL = 96
RIM = 48
EPS = 1e-05


def f32(x):
    return x.astype(F32)


def nn(a, b):
    return jnp.dot(a, b, preferred_element_type=F32)


def nt(a, b):
    return lax.dot_general(a, b, (((1,), (1,)), ((), ())), preferred_element_type=F32)


def tn(a, b):
    return lax.dot_general(a, b, (((0,), (0,)), ((), ())), preferred_element_type=F32)


def one_hot_moves():
    into = np.zeros((TOK, TOK))
    part = np.zeros((4 * MALL, TOK))
    first = np.zeros((RIM, TOK))
    last = np.zeros((RIM, TOK))
    late = np.zeros((2 * MALL, RIM))
    early = np.zeros((2 * MALL, RIM))
    for c in range(12):
        for l in range(4):
            patch = (c // 2) * 4 + l
            for r in range(6):
                natural = ((r // 3) * 2 + c // 6) * 72 + (r % 3) * 24 + (c % 6) * 4 + l
                window = (l // 2) * WTOK + r * 24 + c * 2 + l % 2
                into[window, natural] = 1
                a = (r - 1) // 2 if r > 0 else 3
                part[(((r - 1) % 2) * 2 + c % 2) * MALL + a * 24 + patch, window] = 1
                if r == 0:
                    first[c * 4 + l, window] = 1
                if r == 5:
                    last[c * 4 + l, window] = 1
            late[(c % 2) * MALL + 48 + patch, c * 4 + l] = 1
            early[(c % 2) * MALL + 72 + patch, c * 4 + l] = 1
    rows = [into, into.T, part, part.T, first, last, late, early]
    rows = [np.pad(m, ((0, 0), (0, 4 * MALL - m.shape[1]))) for m in rows]
    return np.concatenate(rows, axis=0).astype(jnp.bfloat16)


SCRATCH = dict(
    moves=pltpu.VMEM((1728, 4 * MALL), BF),
    w_qkv=pltpu.VMEM((D, 3 * D), BF),
    w_proj=pltpu.VMEM((D, D), BF),
    w_merge=pltpu.VMEM((4 * D, D2), BF),
    halo=pltpu.VMEM((4, 3, 6, 4, D), BF),
    classes=pltpu.VMEM((3, 6, 12), jnp.int32),
    cot=pltpu.VMEM((8, 3, 6, 4, D2), BF),
    normed=pltpu.VMEM((TOK, D), BF),
    rolled=pltpu.VMEM((TOK, D), BF),
    xhat=pltpu.VMEM((TOK, D), F32),
    qkv=pltpu.VMEM((TOK, 3 * D), BF),
    probs=pltpu.VMEM((16, WTOK, WTOK), F32),
    attn=pltpu.VMEM((TOK, D), BF),
    first_out=pltpu.VMEM((RIM, D), BF),
    first_in=pltpu.VMEM((RIM, D), BF),
    last_out=pltpu.VMEM((RIM, D), BF),
    last_in=pltpu.VMEM((RIM, D), BF),
    merge_in=pltpu.VMEM((MALL, 4 * D), BF),
    merged=pltpu.VMEM((3, 6, 4, D2), BF),
    cots=pltpu.VMEM((8, MPAD, D2), BF),
    merges=pltpu.VMEM((8, MPAD, 256), BF),
    d_hidden=pltpu.VMEM((TOK, D), BF),
    d_attn=pltpu.VMEM((TOK, D), BF),
    d_qkv=pltpu.VMEM((TOK, 3 * D), BF),
    d_tokens=pltpu.VMEM((4, 3, 6, 4, D), BF),
    c0=pltpu.VMEM((8, 2, 2, 64, D), BF),
    c0_in=pltpu.VMEM((8, 2, 64, D), BF),
    c1=pltpu.VMEM((8, 2, 64, D), BF),
    a1_in=pltpu.VMEM((3, 8, 32, 256), BF),
    a2=pltpu.VMEM((8, 32, 256), BF),
    a2_in=pltpu.VMEM((3, 8, 32, 128), BF),
    b1_in=pltpu.VMEM((3, 8, 2, 32, 128), BF),
    b2=pltpu.VMEM((8, 2, 32, 128), BF),
    b2_in=pltpu.VMEM((3, 8, 32, 128), BF),
    c3=pltpu.VMEM((8, 32, 128), BF),
    c3_in=pltpu.VMEM((7, 32, 128), BF),
    m0=pltpu.VMEM((8, 2, 2, 32, 256), BF),
    m0_in=pltpu.VMEM((8, 2, 32, 256), BF),
    m1=pltpu.VMEM((8, 2, 32, 256), BF),
    m1_in=pltpu.VMEM((8, 32, 256), BF),
    m2=pltpu.VMEM((8, 32, 256), BF),
    m2_in=pltpu.VMEM((7, 32, 256), BF),
    local=pltpu.SemaphoreType.DMA((10,)),
    send=pltpu.SemaphoreType.DMA((80,)),
    recv=pltpu.SemaphoreType.DMA((80,)),
)


class Scratch:
    def __init__(self, refs):
        for name, ref in zip(SCRATCH, refs, strict=True):
            setattr(self, name, ref)


def norm_back(xhat, inverse, g):
    mean_g = jnp.mean(g, axis=-1, keepdims=True)
    mean_gx = jnp.mean(g * xhat, axis=-1, keepdims=True)
    return inverse * (g - mean_g - xhat * mean_gx)


def by_x(rows):
    low = lax.broadcasted_iota(jnp.int32, (rows.shape[0], 128), 1) < 64
    tiles = []
    for t in range(4):
        one = rows[:, (t // 2) * 128 : (t // 2) * 128 + 128]
        two = rows[:, 256 + (t // 2) * 128 : 256 + (t // 2) * 128 + 128]
        if t % 2 == 0:
            tiles.append(jnp.where(low, one, pltpu.roll(two, 64, 1)))
        else:
            tiles.append(jnp.where(low, pltpu.roll(one, 64, 1), two))
    return jnp.concatenate(tiles, axis=1)


def same_class(region, classes, lat):
    cell = lax.broadcasted_iota(jnp.int32, (12, WTOK), 1)
    column = (cell % 24) // 2
    source = lax.broadcasted_iota(jnp.int32, (12, WTOK), 0)
    from_west = f32((column + 6 == source)).astype(BF)
    from_east = f32((column - 6 == source)).astype(BF)
    row = lax.broadcasted_iota(jnp.int32, (6, WTOK), 1) // 24
    line = lax.broadcasted_iota(jnp.int32, (6, WTOK), 0)
    top = f32(row + 3 == line)
    bottom = f32(row - 3 == line)
    blocks = [f32(region[...]).astype(BF)] + [f32(classes[k]).astype(BF) for k in range(3)]
    own = (nn(blocks[0], from_west) + nn(blocks[1], from_east)) * top
    below = (nn(blocks[2], from_west) + nn(blocks[3], from_east)) * bottom
    label = 2.0 * jnp.sum(own + below, axis=0, keepdims=True)
    wraps = jnp.where(lat == 7, 1.0, 0.0)
    label = label + wraps * f32(lax.broadcasted_iota(jnp.int32, (1, WTOK), 1) >= 72)
    spread = jnp.broadcast_to(label, (8, WTOK)).astype(BF)
    down = tn(spread, jnp.full((8, WTOK), 0.125, BF))
    return down == label


def kernel(
    tokens, region, w_qkv, w_proj, w_merge, cotangent, moves,
    merged_out, tokens_out, qkv_out, proj_out, merge_out, *scratch
):
    s = Scratch(scratch)
    lat = lax.axis_index("lat")
    lon = lax.axis_index("lon")
    y_hi, x, z, y_lo, core = lat // 4, lat % 4, lon // 4, (lon // 2) % 2, lon % 2
    y = y_hi * 2 + y_lo
    south, north = (lat + 1) % 8, (lat + 7) % 8
    east, west = (lon + 1) % 32, (lon + 31) % 32

    def chip(y_hi, x, z, y_lo, core):
        return (y_hi * 4 + x, z * 4 + y_lo * 2 + core)

    back = [(lat, west), (north, lon), (north, west)]
    ahead = [(lat, east), (south, lon), (south, east)]
    ys = [(y + k) % 4 for k in range(1, 4)]
    zs = [(z + k) % 8 for k in range(1, 8)]
    xs = [(x + k) % 4 for k in range(1, 4)]
    lats = [(lat + k) % 8 for k in range(1, 8)]
    other_core = chip(y_hi, x, z, y_lo, 1 - core)
    y_chips = [chip(t // 2, x, z, t % 2, core) for t in ys]
    z_chips = [chip(y_hi, x, t, y_lo, core) for t in zs]
    x_chips = [chip(y_hi, t, z, y_lo, core) for t in xs]
    lat_chips = [(t, lon) for t in lats]
    y_lo_chip = chip(y_hi, x, z, 1 - y_lo, core)
    partners = lat_chips + [back[0], ahead[0], back[2], ahead[2], other_core, y_chips[0], y_chips[2]] + z_chips

    used = iter(range(80))

    def push(src, dst, target):
        at = next(used)
        copy = pltpu.make_async_remote_copy(
            src_ref=src,
            dst_ref=dst,
            send_sem=s.send.at[at],
            recv_sem=s.recv.at[at],
            device_id=target,
            device_id_type=MESH,
        )
        copy.start()
        return copy

    held = iter(range(10))

    def fetch(src, dst):
        copy = pltpu.make_async_copy(src, dst, s.local.at[next(held)])
        copy.start()
        return copy

    def wait(copies):
        for copy in copies:
            copy.wait()

    barrier = pltpu.get_barrier_semaphore()
    for target in partners:
        pl.semaphore_signal(barrier, inc=1, device_id=target, device_id_type=MESH)
    own_tokens = fetch(tokens.at[3:6, 6:12], s.halo.at[0])
    own_moves = fetch(moves, s.moves)
    own_cot = [
        fetch(cotangent.at[2:3, 3:6], s.cot.at[lat, 0:1, 0:3]),
        fetch(cotangent.at[0:2, 3:6], s.cot.at[north, 1:3, 0:3]),
    ]
    pl.semaphore_wait(barrier, len(partners))
    class_halos = [push(region, s.classes.at[k], back[k]) for k in range(3)]
    halos = [
        push(tokens.at[0:3, 6:12], s.halo.at[2], back[1]),
        push(tokens.at[0:3, 0:6], s.halo.at[3], back[2]),
        push(tokens.at[3:6, 0:6], s.halo.at[1], back[0]),
    ]
    cot_halos = [
        push(cotangent.at[2:3, 0:3], s.cot.at[lat, 0:1, 3:6], back[0]),
        push(cotangent.at[0:2, 0:3], s.cot.at[north, 1:3, 3:6], back[0]),
    ]
    own_qkv = fetch(w_qkv, s.w_qkv)
    own_proj = fetch(w_proj, s.w_proj)
    own_merge = fetch(w_merge, s.w_merge)
    wait(own_cot + cot_halos)

    def gather_cot(offset):
        chip_at = lat_chips[offset - 1]
        return [
            push(s.cot.at[north, 1:3], s.cot.at[north, 1:3], chip_at),
            push(s.cot.at[lat, 0:1], s.cot.at[lat, 0:1], chip_at),
        ]

    to_north = gather_cot(7)
    cot_sends = gather_cot(1) + gather_cot(4)
    wait([own_moves, own_tokens] + class_halos + halos)

    same = same_class(region, s.classes, lat)
    rolled = nn(s.moves[0:288, 0:TOK], s.halo[...].reshape(TOK, D))
    s.rolled[...] = rolled.astype(BF)
    centred = rolled - jnp.mean(rolled, axis=-1, keepdims=True)
    inverse = lax.rsqrt(jnp.mean(centred * centred, axis=-1, keepdims=True) + EPS)
    xhat = centred * inverse
    s.xhat[...] = xhat
    s.normed[...] = xhat.astype(BF)
    wait([own_qkv])
    normed = s.normed[...]
    for part in range(3):
        cols = slice(part * D, part * D + D)
        made = nn(normed, s.w_qkv[:, cols]).astype(BF)
        s.qkv[:, cols] = made * jnp.asarray(0.125, BF) if part == 0 else made

    lane = lax.broadcasted_iota(jnp.int32, (1, 128), 1)
    halves = [f32(lane < 64).astype(BF), f32(lane >= 64).astype(BF)]
    low = lax.broadcasted_iota(jnp.int32, (WTOK, 128), 1) < 64

    for w in range(2):
        rows = slice(w * WTOK, w * WTOK + WTOK)
        for pair in range(4):
            lo = pair * 128
            query = s.qkv[rows, lo : lo + 128]
            keys = s.qkv[rows, D + lo : D + lo + 128]
            values = s.qkv[rows, 2 * D + lo : 2 * D + lo + 128]
            out = []
            for half in range(2):
                scores = jnp.where(same, nt(keys, query * halves[half]), -1e30)
                expo = jnp.exp(scores - jnp.max(scores, axis=0, keepdims=True))
                probs = expo * (1.0 / jnp.sum(expo, axis=0, keepdims=True))
                s.probs[w * 8 + pair * 2 + half] = probs
                out.append(tn(probs.astype(BF), values))
            s.attn[rows, lo : lo + 128] = jnp.where(low, out[0], out[1]).astype(BF)

    wait([own_proj])
    hidden = (f32(s.rolled[...]) + nn(s.attn[...], s.w_proj[...])).astype(BF)
    s.first_out[...] = nn(s.moves[1248:1296, 0:TOK], hidden).astype(BF)
    s.last_out[...] = nn(s.moves[1296:1344, 0:TOK], hidden).astype(BF)
    rims = [push(s.first_out, s.first_in, back[1]), push(s.last_out, s.last_in, ahead[1])]

    parts = nn(s.moves[576:960, 0:TOK], hidden)
    wait([own_merge] + to_north)
    cot_own = jnp.concatenate([s.cot[lat], s.cot[north, 2:3]], axis=0).reshape(MALL, D2)
    g = [f32(nt(cot_own, s.w_merge[r * D : r * D + D, :]).astype(BF)) for r in range(4)]
    wait(rims)
    cot_sends += gather_cot(2) + gather_cot(6) + gather_cot(3) + gather_cot(5)
    above = nn(s.moves[1536:1728, 0:RIM], s.last_in[...])
    below = nn(s.moves[1344:1536, 0:RIM], s.first_in[...])
    corner = [parts[r * MALL : r * MALL + MALL] for r in range(4)]
    corner = [corner[0] + above[:MALL], corner[1] + above[MALL:], corner[2] + below[:MALL], corner[3] + below[MALL:]]
    mean = sum(jnp.sum(c, axis=-1, keepdims=True) for c in corner) * (1.0 / 2048)
    corner = [c - mean for c in corner]
    var = sum(jnp.sum(c * c, axis=-1, keepdims=True) for c in corner) * (1.0 / 2048)
    m_inverse = lax.rsqrt(var + EPS)
    corner = [c * m_inverse for c in corner]
    for r in range(4):
        s.merge_in[:, r * D : r * D + D] = corner[r].astype(BF)
    merge_sends = [
        push(
            s.merge_in.at[0:MPAD, pl.ds(pl.multiple_of(lats[k] * 256, 256), 256)], s.merges.at[lat], lat_chips[k]
        )
        for k in range(7)
    ]
    s.merges[lat] = s.merge_in[0:MPAD, pl.ds(pl.multiple_of(lat * 256, 256), 256)]

    mean_g = sum(jnp.sum(d, axis=-1, keepdims=True) for d in g) * (1.0 / 2048)
    mean_gx = sum(jnp.sum(d * c, axis=-1, keepdims=True) for d, c in zip(g, corner)) * (1.0 / 2048)
    d_corner = jnp.concatenate([m_inverse * (d - mean_g - c * mean_gx) for d, c in zip(g, corner)], axis=0).astype(BF)
    d_hidden = nn(s.moves[960:1248], d_corner).astype(BF)
    s.d_hidden[...] = d_hidden

    s.d_attn[...] = nt(d_hidden, s.w_proj[...]).astype(BF)
    for w in range(2):
        rows = slice(w * WTOK, w * WTOK + WTOK)
        for pair in range(4):
            lo = pair * 128
            query = s.qkv[rows, lo : lo + 128]
            keys = s.qkv[rows, D + lo : D + lo + 128]
            values = s.qkv[rows, 2 * D + lo : 2 * D + lo + 128]
            grad = s.d_attn[rows, lo : lo + 128]
            d_query, d_keys, d_values = [], [], []
            for half in range(2):
                probs = s.probs[w * 8 + pair * 2 + half]
                d_probs = nt(values, grad * halves[half])
                d_scores = (probs * (d_probs - jnp.sum(d_probs * probs, axis=0, keepdims=True))).astype(BF)
                d_values.append(nn(probs.astype(BF), grad))
                d_query.append(tn(d_scores, keys))
                d_keys.append(nn(d_scores, query))
            s.d_qkv[rows, lo : lo + 128] = (jnp.where(low, d_query[0], d_query[1]) * 0.125).astype(BF)
            s.d_qkv[rows, D + lo : D + lo + 128] = jnp.where(low, d_keys[0], d_keys[1]).astype(BF)
            s.d_qkv[rows, 2 * D + lo : 2 * D + lo + 128] = jnp.where(low, d_values[0], d_values[1]).astype(BF)

    grad_proj = by_x(tn(s.d_hidden[...], s.attn[...])).astype(BF)
    for j in range(32):
        s.c0[j // 4, (j // 2) % 2, j % 2, 48:64] = grad_proj[16 * j : 16 * j + 16]
    normed = s.normed[...]
    for part in range(3):
        made = tn(s.d_qkv[:, part * D : part * D + D], normed)
        moved = by_x(made).astype(BF)
        made = made.astype(BF)
        for block in range(part * 32, part * 32 + 32):
            j, third = block // 3, block % 3
            rows = (moved if third == 2 else made)[16 * block - part * D : 16 * block - part * D + 16]
            s.c0[j // 4, (j // 2) % 2, j % 2, 16 * third : 16 * third + 16] = rows
    c_copy = push(s.c0.at[:, :, 1 - core], s.c0_in, other_core)

    for part in range(2):
        cols = slice(part * D, part * D + D)
        made = nn(s.merge_in[0:MPAD], s.w_merge[:, cols])[:MTOK].astype(BF)
        s.merged[:, :, :, cols] = made.reshape(3, 6, 4, D)

    wait([c_copy])

    @pl.loop(0, 8)
    def _(step):
        for row in range(2):
            s.c1[step, row] = (f32(s.c0[step, row, core]) + f32(s.c0_in[step, row])).astype(BF)

    a_copies = [
        push(
            s.c1.at[:, t % 2, 0:32, pl.ds(pl.multiple_of((t // 2) * 256, 256), 256)], s.a1_in.at[k], y_chips[k]
        )
        for k, t in enumerate(ys)
    ]
    b_copies = [
        push(s.c1.at[:, :, 32:64, pl.ds(pl.multiple_of(t * 128, 128), 128)], s.b1_in.at[k], x_chips[k])
        for k, t in enumerate(xs)
    ]

    d_normed = nt(s.d_qkv[:, 0:D], s.w_qkv[:, 0:D])
    for part in range(1, 3):
        cols = slice(part * D, part * D + D)
        d_normed = d_normed + nt(s.d_qkv[:, cols], s.w_qkv[:, cols])
    d_tokens = (f32(s.d_hidden[...]) + norm_back(s.xhat[...], inverse, d_normed)).astype(BF)
    s.d_tokens[...] = nn(s.moves[288:576, 0:TOK], d_tokens).astype(BF).reshape(4, 3, 6, 4, D)

    wait(cot_sends + merge_sends)
    for slot in range(8):
        rows = [f32(s.cot[slot].reshape(MTOK, D2)), jnp.zeros((MPAD - MTOK, D2), F32)]
        s.cots[slot] = jnp.concatenate(rows, axis=0).astype(BF)
    merges = s.merges[...].reshape(8 * MPAD, 256)
    for part in range(4):
        cots = s.cots[:, :, part * 256 : part * 256 + 256].reshape(8 * MPAD, 256)
        made = tn(cots, merges).astype(BF)
        s.m0[2 * part : 2 * part + 2] = made.reshape(2, 2, 2, 32, 256)
    m_copy = push(s.m0.at[:, :, 1 - core], s.m0_in, other_core)

    wait([m_copy])

    @pl.loop(0, 8)
    def _(step):
        for row in range(2):
            s.m1[step, row] = (f32(s.m0[step, row, core]) + f32(s.m0_in[step, row])).astype(BF)

    m_copy = push(s.m1.at[:, 1 - y_lo], s.m1_in, y_lo_chip)
    wait(a_copies + b_copies)

    @pl.loop(0, 8)
    def _(step):
        total = f32(s.c1[step, y_lo, 0:32, pl.ds(pl.multiple_of(y_hi * 256, 256), 256)])
        for k in range(3):
            total = total + f32(s.a1_in[k, step])
        s.a2[step] = total.astype(BF)
        for row in range(2):
            total = f32(s.c1[step, row, 32:64, pl.ds(pl.multiple_of(x * 128, 128), 128)])
            for k in range(3):
                total = total + f32(s.b1_in[k, step, row])
            s.b2[step, row] = total.astype(BF)

    a_copies = [
        push(s.a2.at[:, :, pl.ds(pl.multiple_of((t // 2) * 128, 128), 128)], s.a2_in.at[k], x_chips[k])
        for k, t in enumerate(xs)
    ]
    b_copies = [push(s.b2.at[:, t % 2], s.b2_in.at[k], y_chips[k]) for k, t in enumerate(ys)]
    last_sends = [
        push(s.merged.at[0:1, 3:6], merged_out.at[2:3, 0:3], ahead[0]),
        push(s.merged.at[1:3, 0:3], merged_out.at[0:2, 3:6], ahead[1]),
        push(s.merged.at[1:3, 3:6], merged_out.at[0:2, 0:3], ahead[2]),
        fetch(s.merged.at[0:1, 0:3], merged_out.at[2:3, 3:6]),
        push(s.d_tokens.at[1], tokens_out.at[3:6, 0:6], ahead[0]),
        push(s.d_tokens.at[2], tokens_out.at[0:3, 6:12], ahead[1]),
        push(s.d_tokens.at[3], tokens_out.at[0:3, 0:6], ahead[2]),
        fetch(s.d_tokens.at[0], tokens_out.at[3:6, 6:12]),
    ]
    wait([m_copy])

    @pl.loop(0, 8)
    def _(step):
        s.m2[step] = (f32(s.m1[step, y_lo]) + f32(s.m1_in[step])).astype(BF)

    m_copies = [push(s.m2.at[t], s.m2_in.at[k], z_chips[k]) for k, t in enumerate(zs)]
    wait(a_copies + b_copies)
    left = lax.broadcasted_iota(jnp.int32, (32, 128), 1) < 64

    @pl.loop(0, 8)
    def _(step):
        one = f32(s.a2[step, :, pl.ds(pl.multiple_of((x // 2) * 128, 128), 128)])
        two = f32(s.b2[step, y_lo])
        for k in range(3):
            one = one + f32(s.a2_in[k, step])
            two = two + f32(s.b2_in[k, step])
        one = jnp.where(x % 2 == 1, pltpu.roll(one, 64, 1), one)
        two = jnp.where(y_hi == 0, pltpu.roll(two, 64, 1), two)
        s.c3[step] = jnp.where(left, one, two).astype(BF)

    c_copies = [push(s.c3.at[t], s.c3_in.at[k], z_chips[k]) for k, t in enumerate(zs)]
    wait(c_copies)
    total = f32(s.c3[z])
    for k in range(7):
        total = total + f32(s.c3_in[k])
    qkv_out[0:32] = total[:, :64]
    qkv_out[32:48] = total[:16, 64:]
    proj_out[...] = total[16:, 64:]
    wait(m_copies)
    total = f32(s.m2[z])
    for k in range(7):
        total = total + f32(s.m2_in[k])
    merge_out[...] = total
    wait(last_sends)


def hand_over(*refs):
    held, done = refs[10:15], refs[15]
    into = [pltpu.make_async_copy(refs[k], held[k], done.at[k]) for k in range(5)]
    out = [pltpu.make_async_copy(held[k], refs[5 + k], done.at[5 + k]) for k in range(5)]
    for copy in into:
        copy.start()
    for one, two in zip(into, out):
        one.wait()
        two.start()
    for copy in out:
        copy.wait()


def shards(tokens, region, w_qkv, w_proj, w_merge, cotangent):
    hbm = pl.BlockSpec(memory_space=pltpu.HBM)
    vmem = pl.BlockSpec(memory_space=pltpu.VMEM)
    made = pl.pallas_call(
        kernel,
        out_shape=(
            jax.ShapeDtypeStruct((3, 6, 4, D2), BF),
            jax.ShapeDtypeStruct((6, 12, 4, D), BF),
            jax.ShapeDtypeStruct((48, 64), F32),
            jax.ShapeDtypeStruct((16, 64), F32),
            jax.ShapeDtypeStruct((32, 256), F32),
        ),
        in_specs=[hbm, vmem, hbm, hbm, hbm, hbm, hbm],
        out_specs=(hbm, hbm, vmem, vmem, vmem),
        scratch_shapes=list(SCRATCH.values()),
        compiler_params=pltpu.CompilerParams(
            collective_id=0, has_side_effects=True, vmem_limit_bytes=56 * 1024 * 1024
        ),
    )(tokens, region, w_qkv, w_proj, w_merge, cotangent, jnp.asarray(one_hot_moves()))
    merged, grad_tokens, grad_qkv, grad_proj, grad_merge = pl.pallas_call(
        hand_over,
        out_shape=tuple(jax.ShapeDtypeStruct(a.shape, a.dtype) for a in made),
        in_specs=[hbm] * 5,
        out_specs=(hbm,) * 5,
        scratch_shapes=[pltpu.VMEM(a.shape, a.dtype) for a in made] + [pltpu.SemaphoreType.DMA((10,))],
        compiler_params=pltpu.CompilerParams(vmem_limit_bytes=56 * 1024 * 1024),
    )(*made)
    return (merged, grad_tokens, grad_qkv.T, grad_proj.T, grad_merge.T)


def solution(mesh):
    return jax.shard_map(
        shards,
        mesh=mesh,
        in_specs=(
            P("lat", "lon", None, None),
            P("lat", "lon"),
            P(),
            P(),
            P(),
            P("lat", "lon", None, None),
        ),
        out_specs=(
            P("lat", "lon", None, None),
            P("lat", "lon", None, None),
            P("lat", "lon"),
            P("lat", "lon"),
            P("lat", "lon"),
        ),
        check_vma=False,
    )
```

```python
import jax
import jax.numpy as jnp
import numpy as np
from jax import lax
from jax.experimental import pallas as pl
from jax.experimental.pallas import tpu as pltpu
from jax.sharding import PartitionSpec as P

MESH = pl.DeviceIdType.MESH
BF = jnp.bfloat16
F32 = jnp.float32
D = 512
D2 = 1024
TOK = 288
WTOK = 144
MTOK = 72
MPAD = 80
MALL = 96
RIM = 48
EPS = 1e-05


def f32(x):
    return x.astype(F32)


def nn(a, b):
    return jnp.dot(a, b, preferred_element_type=F32)


def nt(a, b):
    return lax.dot_general(a, b, (((1,), (1,)), ((), ())), preferred_element_type=F32)


def tn(a, b):
    return lax.dot_general(a, b, (((0,), (0,)), ((), ())), preferred_element_type=F32)


def one_hot_moves():
    into = np.zeros((TOK, TOK))
    part = np.zeros((4 * MALL, TOK))
    first = np.zeros((RIM, TOK))
    last = np.zeros((RIM, TOK))
    late = np.zeros((2 * MALL, RIM))
    early = np.zeros((2 * MALL, RIM))
    for c in range(12):
        for l in range(4):
            patch = (c // 2) * 4 + l
            for r in range(6):
                natural = ((r // 3) * 2 + c // 6) * 72 + (r % 3) * 24 + (c % 6) * 4 + l
                window = (l // 2) * WTOK + r * 24 + c * 2 + l % 2
                into[window, natural] = 1
                a = (r + 1) // 2
                part[(((r - 1) % 2) * 2 + c % 2) * MALL + a * 24 + patch, window] = 1
                if r == 0:
                    first[c * 4 + l, window] = 1
                if r == 5:
                    last[c * 4 + l, window] = 1
            late[(c % 2) * MALL + 72 + patch, c * 4 + l] = 1
            early[(c % 2) * MALL + patch, c * 4 + l] = 1
    rows = [into, into.T, part, part.T, first, last, late, early]
    rows = [np.pad(m, ((0, 0), (0, 4 * MALL - m.shape[1]))) for m in rows]
    return np.concatenate(rows, axis=0).astype(jnp.bfloat16)


SCRATCH = dict(
    moves=pltpu.VMEM((1728, 4 * MALL), BF),
    w_qkv=pltpu.VMEM((D, 3 * D), BF),
    w_proj=pltpu.VMEM((D, D), BF),
    w_merge=pltpu.VMEM((4 * D, D2), BF),
    halo=pltpu.VMEM((4, 3, 6, 4, D), BF),
    classes=pltpu.VMEM((3, 6, 12), jnp.int32),
    cot=pltpu.VMEM((8, 3, 6, 4, D2), BF),
    normed=pltpu.VMEM((TOK, D), BF),
    rolled=pltpu.VMEM((TOK, D), BF),
    xhat=pltpu.VMEM((TOK, D), F32),
    qkv=pltpu.VMEM((TOK, 3 * D), BF),
    probs=pltpu.VMEM((16, WTOK, WTOK), F32),
    attn=pltpu.VMEM((TOK, D), BF),
    first_out=pltpu.VMEM((RIM, D), BF),
    first_in=pltpu.VMEM((RIM, D), BF),
    last_out=pltpu.VMEM((RIM, D), BF),
    last_in=pltpu.VMEM((RIM, D), BF),
    merge_in=pltpu.VMEM((MALL, 4 * D), BF),
    merged=pltpu.VMEM((3, 6, 4, D2), BF),
    cots=pltpu.VMEM((8, MPAD, D2), BF),
    merges=pltpu.VMEM((8, MPAD, 256), BF),
    d_hidden=pltpu.VMEM((TOK, D), BF),
    d_attn=pltpu.VMEM((TOK, D), BF),
    d_qkv=pltpu.VMEM((TOK, 3 * D), BF),
    d_tokens=pltpu.VMEM((4, 3, 6, 4, D), BF),
    c0=pltpu.VMEM((8, 2, 2, 64, D), BF),
    c0_in=pltpu.VMEM((8, 2, 64, D), BF),
    c1=pltpu.VMEM((8, 2, 64, D), BF),
    a1_in=pltpu.VMEM((3, 8, 32, 256), BF),
    a2=pltpu.VMEM((8, 32, 256), BF),
    a2_in=pltpu.VMEM((3, 8, 32, 128), BF),
    b1_in=pltpu.VMEM((3, 8, 2, 32, 128), BF),
    b2=pltpu.VMEM((8, 2, 32, 128), BF),
    b2_in=pltpu.VMEM((3, 8, 32, 128), BF),
    c3=pltpu.VMEM((8, 32, 128), BF),
    c3_in=pltpu.VMEM((7, 32, 128), BF),
    m0=pltpu.VMEM((8, 2, 2, 32, 256), BF),
    m0_in=pltpu.VMEM((8, 2, 32, 256), BF),
    m1=pltpu.VMEM((8, 2, 32, 256), BF),
    m1_in=pltpu.VMEM((8, 32, 256), BF),
    m2=pltpu.VMEM((8, 32, 256), BF),
    m2_in=pltpu.VMEM((7, 32, 256), BF),
    local=pltpu.SemaphoreType.DMA((10,)),
    send=pltpu.SemaphoreType.DMA((112,)),
    recv=pltpu.SemaphoreType.DMA((112,)),
)


class Scratch:
    def __init__(self, refs):
        for name, ref in zip(SCRATCH, refs, strict=True):
            setattr(self, name, ref)


def norm_back(xhat, inverse, g):
    mean_g = jnp.mean(g, axis=-1, keepdims=True)
    mean_gx = jnp.mean(g * xhat, axis=-1, keepdims=True)
    return inverse * (g - mean_g - xhat * mean_gx)


def by_x(rows):
    low = lax.broadcasted_iota(jnp.int32, (rows.shape[0], 128), 1) < 64
    tiles = []
    for t in range(4):
        one = rows[:, (t // 2) * 128 : (t // 2) * 128 + 128]
        two = rows[:, 256 + (t // 2) * 128 : 256 + (t // 2) * 128 + 128]
        if t % 2 == 0:
            tiles.append(jnp.where(low, one, pltpu.roll(two, 64, 1)))
        else:
            tiles.append(jnp.where(low, pltpu.roll(one, 64, 1), two))
    return jnp.concatenate(tiles, axis=1)


def same_class(region, classes, lat):
    cell = lax.broadcasted_iota(jnp.int32, (12, WTOK), 1)
    column = (cell % 24) // 2
    source = lax.broadcasted_iota(jnp.int32, (12, WTOK), 0)
    from_west = f32((column + 6 == source)).astype(BF)
    from_east = f32((column - 6 == source)).astype(BF)
    row = lax.broadcasted_iota(jnp.int32, (6, WTOK), 1) // 24
    line = lax.broadcasted_iota(jnp.int32, (6, WTOK), 0)
    top = f32(row + 3 == line)
    bottom = f32(row - 3 == line)
    blocks = [f32(region[...]).astype(BF)] + [f32(classes[k]).astype(BF) for k in range(3)]
    own = (nn(blocks[0], from_west) + nn(blocks[1], from_east)) * top
    below = (nn(blocks[2], from_west) + nn(blocks[3], from_east)) * bottom
    label = 2.0 * jnp.sum(own + below, axis=0, keepdims=True)
    wraps = jnp.where(lat == 7, 1.0, 0.0)
    label = label + wraps * f32(lax.broadcasted_iota(jnp.int32, (1, WTOK), 1) >= 72)
    spread = jnp.broadcast_to(label, (8, WTOK)).astype(BF)
    down = tn(spread, jnp.full((8, WTOK), 0.125, BF))
    return down == label


def kernel(
    tokens, region, w_qkv, w_proj, w_merge, cotangent, moves,
    merged_out, tokens_out, qkv_out, proj_out, merge_out, *scratch
):
    s = Scratch(scratch)
    lat = lax.axis_index("lat")
    lon = lax.axis_index("lon")
    y_hi, x, z, y_lo, core = lat // 4, lat % 4, lon // 4, (lon // 2) % 2, lon % 2
    y = y_hi * 2 + y_lo
    south, north = (lat + 1) % 8, (lat + 7) % 8
    east, west = (lon + 1) % 32, (lon + 31) % 32

    def chip(y_hi, x, z, y_lo, core):
        return (y_hi * 4 + x, z * 4 + y_lo * 2 + core)

    back = [(lat, west), (north, lon), (north, west)]
    ahead = [(lat, east), (south, lon), (south, east)]
    ys = [(y + k) % 4 for k in range(1, 4)]
    zs = [(z + k) % 8 for k in range(1, 8)]
    xs = [(x + k) % 4 for k in range(1, 4)]
    lats = [(lat + k) % 8 for k in range(1, 8)]
    other_core = chip(y_hi, x, z, y_lo, 1 - core)
    y_chips = [chip(t // 2, x, z, t % 2, core) for t in ys]
    z_chips = [chip(y_hi, x, t, y_lo, core) for t in zs]
    x_chips = [chip(y_hi, t, z, y_lo, core) for t in xs]
    lat_chips = [(t, lon) for t in lats]
    y_lo_chip = chip(y_hi, x, z, 1 - y_lo, core)
    partners = lat_chips + [back[0], ahead[0], back[2], ahead[2], other_core, y_chips[0], y_chips[2]] + z_chips

    used = iter(range(112))

    def push(src, dst, target):
        at = next(used)
        copy = pltpu.make_async_remote_copy(
            src_ref=src,
            dst_ref=dst,
            send_sem=s.send.at[at],
            recv_sem=s.recv.at[at],
            device_id=target,
            device_id_type=MESH,
        )
        copy.start()
        return copy

    held = iter(range(10))

    def fetch(src, dst):
        copy = pltpu.make_async_copy(src, dst, s.local.at[next(held)])
        copy.start()
        return copy

    def wait(copies):
        for copy in copies:
            copy.wait()

    barrier = pltpu.get_barrier_semaphore()
    for target in partners:
        pl.semaphore_signal(barrier, inc=1, device_id=target, device_id_type=MESH)
    own_tokens = fetch(tokens.at[3:6, 6:12], s.halo.at[0])
    own_moves = fetch(moves, s.moves)
    own_cot = [
        fetch(cotangent.at[1:3, 3:6], s.cot.at[lat, 0:2, 0:3]),
        fetch(cotangent.at[0:1, 3:6], s.cot.at[north, 2:3, 0:3]),
    ]
    pl.semaphore_wait(barrier, len(partners))
    class_halos = [push(region, s.classes.at[k], back[k]) for k in range(3)]
    halos = [
        push(tokens.at[0:3, 6:12], s.halo.at[2], back[1]),
        push(tokens.at[0:3, 0:6], s.halo.at[3], back[2]),
        push(tokens.at[3:6, 0:6], s.halo.at[1], back[0]),
    ]
    cot_halos = [
        push(cotangent.at[1:3, 0:3], s.cot.at[lat, 0:2, 3:6], back[0]),
        push(cotangent.at[0:1, 0:3], s.cot.at[north, 2:3, 3:6], back[0]),
    ]
    own_qkv = fetch(w_qkv, s.w_qkv)
    own_proj = fetch(w_proj, s.w_proj)
    own_merge = fetch(w_merge, s.w_merge)
    wait(own_cot + cot_halos)

    def gather_cot(offset):
        chip_at = lat_chips[offset - 1]
        return [
            push(s.cot.at[lat, 0:2], s.cot.at[lat, 0:2], chip_at),
            push(s.cot.at[north, 2:3], s.cot.at[north, 2:3], chip_at),
        ]

    to_north = gather_cot(7)
    cot_sends = gather_cot(1) + gather_cot(4)
    wait([own_moves, own_tokens] + class_halos + halos)
    cot_sends += gather_cot(3) + gather_cot(5)

    same = same_class(region, s.classes, lat)
    rolled = nn(s.moves[0:288, 0:TOK], s.halo[...].reshape(TOK, D))
    s.rolled[...] = rolled.astype(BF)
    centred = rolled - jnp.mean(rolled, axis=-1, keepdims=True)
    inverse = lax.rsqrt(jnp.mean(centred * centred, axis=-1, keepdims=True) + EPS)
    xhat = centred * inverse
    s.xhat[...] = xhat
    s.normed[...] = xhat.astype(BF)
    wait([own_qkv])
    normed = s.normed[...]
    for part in range(3):
        cols = slice(part * D, part * D + D)
        made = nn(normed, s.w_qkv[:, cols]).astype(BF)
        s.qkv[:, cols] = made * jnp.asarray(0.125, BF) if part == 0 else made

    lane = lax.broadcasted_iota(jnp.int32, (1, 128), 1)
    halves = [f32(lane < 64).astype(BF), f32(lane >= 64).astype(BF)]
    low = lax.broadcasted_iota(jnp.int32, (WTOK, 128), 1) < 64

    for w in range(2):
        rows = slice(w * WTOK, w * WTOK + WTOK)
        for pair in range(4):
            lo = pair * 128
            query = s.qkv[rows, lo : lo + 128]
            keys = s.qkv[rows, D + lo : D + lo + 128]
            values = s.qkv[rows, 2 * D + lo : 2 * D + lo + 128]
            out = []
            for half in range(2):
                scores = jnp.where(same, nt(keys, query * halves[half]), -1e30)
                expo = jnp.exp(scores - jnp.max(scores, axis=0, keepdims=True))
                probs = expo * (1.0 / jnp.sum(expo, axis=0, keepdims=True))
                s.probs[w * 8 + pair * 2 + half] = probs
                out.append(tn(probs.astype(BF), values))
            s.attn[rows, lo : lo + 128] = jnp.where(low, out[0], out[1]).astype(BF)

    wait([own_proj])
    hidden = (f32(s.rolled[...]) + nn(s.attn[...], s.w_proj[...])).astype(BF)
    s.first_out[...] = nn(s.moves[1248:1296, 0:TOK], hidden).astype(BF)
    s.last_out[...] = nn(s.moves[1296:1344, 0:TOK], hidden).astype(BF)
    rims = [push(s.first_out, s.first_in, back[1]), push(s.last_out, s.last_in, ahead[1])]

    parts = nn(s.moves[576:960, 0:TOK], hidden)
    wait([own_merge] + to_north)
    cot_own = jnp.concatenate([s.cot[lat], s.cot[south, 0:1]], axis=0).reshape(MALL, D2)
    g = [f32(nt(cot_own, s.w_merge[r * D : r * D + D, :]).astype(BF)) for r in range(4)]
    wait(rims)
    cot_sends += gather_cot(2) + gather_cot(6)
    above = nn(s.moves[1536:1728, 0:RIM], s.last_in[...])
    below = nn(s.moves[1344:1536, 0:RIM], s.first_in[...])
    corner = [parts[r * MALL : r * MALL + MALL] for r in range(4)]
    corner = [corner[0] + above[:MALL], corner[1] + above[MALL:], corner[2] + below[:MALL], corner[3] + below[MALL:]]
    mean = sum(jnp.sum(c, axis=-1, keepdims=True) for c in corner) * (1.0 / 2048)
    corner = [c - mean for c in corner]
    var = sum(jnp.sum(c * c, axis=-1, keepdims=True) for c in corner) * (1.0 / 2048)
    m_inverse = lax.rsqrt(var + EPS)
    corner = [c * m_inverse for c in corner]
    for r in range(4):
        s.merge_in[:, r * D : r * D + D] = corner[r].astype(BF)
    merge_sends = [
        push(
            s.merge_in.at[0:MPAD, pl.ds(pl.multiple_of(lats[k] * 256, 256), 256)], s.merges.at[lat], lat_chips[k]
        )
        for k in range(7)
    ]
    s.merges[lat] = s.merge_in[0:MPAD, pl.ds(pl.multiple_of(lat * 256, 256), 256)]

    mean_g = sum(jnp.sum(d, axis=-1, keepdims=True) for d in g) * (1.0 / 2048)
    mean_gx = sum(jnp.sum(d * c, axis=-1, keepdims=True) for d, c in zip(g, corner)) * (1.0 / 2048)
    d_corner = jnp.concatenate([m_inverse * (d - mean_g - c * mean_gx) for d, c in zip(g, corner)], axis=0).astype(BF)
    d_hidden = nn(s.moves[960:1248], d_corner).astype(BF)
    s.d_hidden[...] = d_hidden

    s.d_attn[...] = nt(d_hidden, s.w_proj[...]).astype(BF)
    for w in range(2):
        rows = slice(w * WTOK, w * WTOK + WTOK)
        for pair in range(4):
            lo = pair * 128
            grad = s.d_attn[rows, lo : lo + 128]
            d_values = [nn(s.probs[w * 8 + pair * 2 + half].astype(BF), grad) for half in range(2)]
            s.d_qkv[rows, 2 * D + lo : 2 * D + lo + 128] = jnp.where(low, d_values[0], d_values[1]).astype(BF)

    grad_proj = by_x(tn(s.d_hidden[...], s.attn[...])).astype(BF)
    for j in range(32):
        s.c0[j // 4, (j // 2) % 2, j % 2, 48:64] = grad_proj[16 * j : 16 * j + 16]
    normed = s.normed[...]

    def grad_qkv(part):
        made = tn(s.d_qkv[:, part * D : part * D + D], normed)
        moved = by_x(made).astype(BF)
        made = made.astype(BF)
        for block in range(part * 32, part * 32 + 32):
            j, third = block // 3, block % 3
            rows = (moved if third == 2 else made)[16 * block - part * D : 16 * block - part * D + 16]
            s.c0[j // 4, (j // 2) % 2, j % 2, 16 * third : 16 * third + 16] = rows

    def to_core(span):
        return push(s.c0.at[span, :, 1 - core], s.c0_in.at[span], other_core)

    def to_axes(span, copy):
        copy.wait()

        @pl.loop(span.start, span.stop)
        def _(step):
            for row in range(2):
                s.c1[step, row] = (f32(s.c0[step, row, core]) + f32(s.c0_in[step, row])).astype(BF)

        return [
            push(
                s.c1.at[span, t % 2, 0:32, pl.ds(pl.multiple_of((t // 2) * 256, 256), 256)],
                s.a1_in.at[k, span],
                y_chips[k],
            )
            for k, t in enumerate(ys)
        ] + [
            push(
                s.c1.at[span, :, 32:64, pl.ds(pl.multiple_of(t * 128, 128), 128)], s.b1_in.at[k, span], x_chips[k]
            )
            for k, t in enumerate(xs)
        ]

    def to_other_axes(span, copies):
        wait(copies)

        @pl.loop(span.start, span.stop)
        def _(step):
            total = f32(s.c1[step, y_lo, 0:32, pl.ds(pl.multiple_of(y_hi * 256, 256), 256)])
            for k in range(3):
                total = total + f32(s.a1_in[k, step])
            s.a2[step] = total.astype(BF)
            for row in range(2):
                total = f32(s.c1[step, row, 32:64, pl.ds(pl.multiple_of(x * 128, 128), 128)])
                for k in range(3):
                    total = total + f32(s.b1_in[k, step, row])
                s.b2[step, row] = total.astype(BF)

        return [
            push(
                s.a2.at[span, :, pl.ds(pl.multiple_of((t // 2) * 128, 128), 128)], s.a2_in.at[k, span], x_chips[k]
            )
            for k, t in enumerate(xs)
        ] + [push(s.b2.at[span, t % 2], s.b2_in.at[k, span], y_chips[k]) for k, t in enumerate(ys)]

    chunks = [slice(6, 8), slice(0, 2), slice(2, 6)]
    grad_qkv(2)
    core_copies = [to_core(chunks[0])]
    axis_copies = []

    for w in range(2):
        rows = slice(w * WTOK, w * WTOK + WTOK)
        for pair in range(4):
            lo = pair * 128
            query = s.qkv[rows, lo : lo + 128]
            keys = s.qkv[rows, D + lo : D + lo + 128]
            values = s.qkv[rows, 2 * D + lo : 2 * D + lo + 128]
            grad = s.d_attn[rows, lo : lo + 128]
            d_query, d_keys = [], []
            for half in range(2):
                probs = s.probs[w * 8 + pair * 2 + half]
                d_probs = nt(values, grad * halves[half])
                d_scores = (probs * (d_probs - jnp.sum(d_probs * probs, axis=0, keepdims=True))).astype(BF)
                d_query.append(tn(d_scores, keys))
                d_keys.append(nn(d_scores, query))
            s.d_qkv[rows, lo : lo + 128] = (jnp.where(low, d_query[0], d_query[1]) * 0.125).astype(BF)
            s.d_qkv[rows, D + lo : D + lo + 128] = jnp.where(low, d_keys[0], d_keys[1]).astype(BF)
        if w == 0:
            axis_copies.append(to_axes(chunks[0], core_copies[0]))

    grad_qkv(0)
    core_copies.append(to_core(chunks[1]))
    grad_qkv(1)
    core_copies.append(to_core(chunks[2]))
    axis_copies.append(to_axes(chunks[1], core_copies[1]))

    for part in range(2):
        cols = slice(part * D, part * D + D)
        made = nn(s.merge_in[0:MPAD], s.w_merge[:, cols])[:MTOK].astype(BF)
        s.merged[:, :, :, cols] = made.reshape(3, 6, 4, D)

    axis_copies.append(to_axes(chunks[2], core_copies[2]))
    other_copies = [to_other_axes(chunks[0], axis_copies[0])]

    d_normed = nt(s.d_qkv[:, 0:D], s.w_qkv[:, 0:D])
    for part in range(1, 3):
        cols = slice(part * D, part * D + D)
        d_normed = d_normed + nt(s.d_qkv[:, cols], s.w_qkv[:, cols])
    d_tokens = (f32(s.d_hidden[...]) + norm_back(s.xhat[...], inverse, d_normed)).astype(BF)
    s.d_tokens[...] = nn(s.moves[288:576, 0:TOK], d_tokens).astype(BF).reshape(4, 3, 6, 4, D)

    other_copies.append(to_other_axes(chunks[1], axis_copies[1]))
    wait(cot_sends + merge_sends)
    for slot in range(8):
        rows = [f32(s.cot[slot].reshape(MTOK, D2)), jnp.zeros((MPAD - MTOK, D2), F32)]
        s.cots[slot] = jnp.concatenate(rows, axis=0).astype(BF)
    merges = s.merges[...].reshape(8 * MPAD, 256)
    for part in range(4):
        cots = s.cots[:, :, part * 256 : part * 256 + 256].reshape(8 * MPAD, 256)
        made = tn(cots, merges).astype(BF)
        s.m0[2 * part : 2 * part + 2] = made.reshape(2, 2, 2, 32, 256)
    m_copy = push(s.m0.at[:, :, 1 - core], s.m0_in, other_core)

    wait([m_copy])

    @pl.loop(0, 8)
    def _(step):
        for row in range(2):
            s.m1[step, row] = (f32(s.m0[step, row, core]) + f32(s.m0_in[step, row])).astype(BF)

    m_copy = push(s.m1.at[:, 1 - y_lo], s.m1_in, y_lo_chip)
    other_copies.append(to_other_axes(chunks[2], axis_copies[2]))
    last_sends = [
        push(s.merged.at[0:2, 3:6], merged_out.at[1:3, 0:3], ahead[0]),
        push(s.merged.at[2:3, 0:3], merged_out.at[0:1, 3:6], ahead[1]),
        push(s.merged.at[2:3, 3:6], merged_out.at[0:1, 0:3], ahead[2]),
        fetch(s.merged.at[0:2, 0:3], merged_out.at[1:3, 3:6]),
        push(s.d_tokens.at[1], tokens_out.at[3:6, 0:6], ahead[0]),
        push(s.d_tokens.at[2], tokens_out.at[0:3, 6:12], ahead[1]),
        push(s.d_tokens.at[3], tokens_out.at[0:3, 0:6], ahead[2]),
        fetch(s.d_tokens.at[0], tokens_out.at[3:6, 6:12]),
    ]
    wait([m_copy])

    @pl.loop(0, 8)
    def _(step):
        s.m2[step] = (f32(s.m1[step, y_lo]) + f32(s.m1_in[step])).astype(BF)

    m_copies = [push(s.m2.at[t], s.m2_in.at[k], z_chips[k]) for k, t in enumerate(zs)]
    for copies in other_copies:
        wait(copies)
    left = lax.broadcasted_iota(jnp.int32, (32, 128), 1) < 64

    @pl.loop(0, 8)
    def _(step):
        one = f32(s.a2[step, :, pl.ds(pl.multiple_of((x // 2) * 128, 128), 128)])
        two = f32(s.b2[step, y_lo])
        for k in range(3):
            one = one + f32(s.a2_in[k, step])
            two = two + f32(s.b2_in[k, step])
        one = jnp.where(x % 2 == 1, pltpu.roll(one, 64, 1), one)
        two = jnp.where(y_hi == 0, pltpu.roll(two, 64, 1), two)
        s.c3[step] = jnp.where(left, one, two).astype(BF)

    c_copies = [push(s.c3.at[t], s.c3_in.at[k], z_chips[k]) for k, t in enumerate(zs)]
    wait(c_copies)
    total = f32(s.c3[z])
    for k in range(7):
        total = total + f32(s.c3_in[k])
    qkv_out[0:32] = total[:, :64]
    qkv_out[32:48] = total[:16, 64:]
    proj_out[...] = total[16:, 64:]
    wait(m_copies)
    total = f32(s.m2[z])
    for k in range(7):
        total = total + f32(s.m2_in[k])
    merge_out[...] = total
    wait(last_sends)


def hand_over(*refs):
    held, done = refs[10:15], refs[15]
    into = [pltpu.make_async_copy(refs[k], held[k], done.at[k]) for k in range(5)]
    out = [pltpu.make_async_copy(held[k], refs[5 + k], done.at[5 + k]) for k in range(5)]
    for copy in into:
        copy.start()
    for one, two in zip(into, out):
        one.wait()
        two.start()
    for copy in out:
        copy.wait()


def shards(tokens, region, w_qkv, w_proj, w_merge, cotangent):
    hbm = pl.BlockSpec(memory_space=pltpu.HBM)
    vmem = pl.BlockSpec(memory_space=pltpu.VMEM)
    made = pl.pallas_call(
        kernel,
        out_shape=(
            jax.ShapeDtypeStruct((3, 6, 4, D2), BF),
            jax.ShapeDtypeStruct((6, 12, 4, D), BF),
            jax.ShapeDtypeStruct((48, 64), F32),
            jax.ShapeDtypeStruct((16, 64), F32),
            jax.ShapeDtypeStruct((32, 256), F32),
        ),
        in_specs=[hbm, vmem, hbm, hbm, hbm, hbm, hbm],
        out_specs=(hbm, hbm, vmem, vmem, vmem),
        scratch_shapes=list(SCRATCH.values()),
        compiler_params=pltpu.CompilerParams(
            collective_id=0, has_side_effects=True, vmem_limit_bytes=56 * 1024 * 1024
        ),
    )(tokens, region, w_qkv, w_proj, w_merge, cotangent, jnp.asarray(one_hot_moves()))
    merged, grad_tokens, grad_qkv, grad_proj, grad_merge = pl.pallas_call(
        hand_over,
        out_shape=tuple(jax.ShapeDtypeStruct(a.shape, a.dtype) for a in made),
        in_specs=[hbm] * 5,
        out_specs=(hbm,) * 5,
        scratch_shapes=[pltpu.VMEM(a.shape, a.dtype) for a in made] + [pltpu.SemaphoreType.DMA((10,))],
        compiler_params=pltpu.CompilerParams(vmem_limit_bytes=56 * 1024 * 1024),
    )(*made)
    return (merged, grad_tokens, grad_qkv.T, grad_proj.T, grad_merge.T)


def solution(mesh):
    return jax.shard_map(
        shards,
        mesh=mesh,
        in_specs=(
            P("lat", "lon", None, None),
            P("lat", "lon"),
            P(),
            P(),
            P(),
            P("lat", "lon", None, None),
        ),
        out_specs=(
            P("lat", "lon", None, None),
            P("lat", "lon", None, None),
            P("lat", "lon"),
            P("lat", "lon"),
            P("lat", "lon"),
        ),
        check_vma=False,
    )
```

```python
import jax
import jax.numpy as jnp
import numpy as np
from jax import lax
from jax.experimental import pallas as pl
from jax.experimental.pallas import tpu as pltpu
from jax.sharding import PartitionSpec as P

MESH = pl.DeviceIdType.MESH
BF = jnp.bfloat16
F32 = jnp.float32
D = 512
D2 = 1024
TOK = 288
WTOK = 144
MTOK = 72
MPAD = 80
MALL = 96
RIM = 48
EPS = 1e-05


def f32(x):
    return x.astype(F32)


def nn(a, b):
    return jnp.dot(a, b, preferred_element_type=F32)


def nt(a, b):
    return lax.dot_general(a, b, (((1,), (1,)), ((), ())), preferred_element_type=F32)


def tn(a, b):
    return lax.dot_general(a, b, (((0,), (0,)), ((), ())), preferred_element_type=F32)


def one_hot_moves():
    into = np.zeros((TOK, TOK))
    part = np.zeros((4 * MALL, TOK))
    first = np.zeros((RIM, TOK))
    last = np.zeros((RIM, TOK))
    late = np.zeros((2 * MALL, RIM))
    early = np.zeros((2 * MALL, RIM))
    for c in range(12):
        for l in range(4):
            patch = (c // 2) * 4 + l
            for r in range(6):
                natural = ((r // 3) * 2 + c // 6) * 72 + (r % 3) * 24 + (c % 6) * 4 + l
                window = (l // 2) * WTOK + r * 24 + c * 2 + l % 2
                into[window, natural] = 1
                a = (r + 1) // 2
                part[(((r - 1) % 2) * 2 + c % 2) * MALL + a * 24 + patch, window] = 1
                if r == 0:
                    first[c * 4 + l, window] = 1
                if r == 5:
                    last[c * 4 + l, window] = 1
            late[(c % 2) * MALL + 72 + patch, c * 4 + l] = 1
            early[(c % 2) * MALL + patch, c * 4 + l] = 1
    rows = [into, into.T, part, part.T, first, last, late, early]
    rows = [np.pad(m, ((0, 0), (0, 4 * MALL - m.shape[1]))) for m in rows]
    return np.concatenate(rows, axis=0).astype(jnp.bfloat16)


SCRATCH = dict(
    moves=pltpu.VMEM((1728, 4 * MALL), BF),
    w_qkv=pltpu.VMEM((D, 3 * D), BF),
    w_proj=pltpu.VMEM((D, D), BF),
    w_merge=pltpu.VMEM((4 * D, D2), BF),
    halo=pltpu.VMEM((4, 3, 6, 4, D), BF),
    classes=pltpu.VMEM((3, 6, 12), jnp.int32),
    cot=pltpu.VMEM((8, 3, 6, 4, D2), BF),
    normed=pltpu.VMEM((TOK, D), BF),
    rolled=pltpu.VMEM((TOK, D), BF),
    xhat=pltpu.VMEM((TOK, D), F32),
    qkv=pltpu.VMEM((TOK, 3 * D), BF),
    probs=pltpu.VMEM((16, WTOK, WTOK), F32),
    attn=pltpu.VMEM((TOK, D), BF),
    first_out=pltpu.VMEM((RIM, D), BF),
    first_in=pltpu.VMEM((RIM, D), BF),
    last_out=pltpu.VMEM((RIM, D), BF),
    last_in=pltpu.VMEM((RIM, D), BF),
    merge_in=pltpu.VMEM((MALL, 4 * D), BF),
    merged=pltpu.VMEM((3, 6, 4, D2), BF),
    cots=pltpu.VMEM((8, MPAD, D2), BF),
    merges=pltpu.VMEM((8, MPAD, 256), BF),
    d_hidden=pltpu.VMEM((TOK, D), BF),
    d_attn=pltpu.VMEM((TOK, D), BF),
    d_qkv=pltpu.VMEM((TOK, 3 * D), BF),
    d_tokens=pltpu.VMEM((4, 3, 6, 4, D), BF),
    c0=pltpu.VMEM((8, 2, 2, 64, D), BF),
    c0_in=pltpu.VMEM((8, 2, 64, D), BF),
    c1=pltpu.VMEM((8, 2, 64, D), BF),
    a1_in=pltpu.VMEM((3, 8, 32, 256), BF),
    a2=pltpu.VMEM((8, 32, 256), BF),
    a2_in=pltpu.VMEM((3, 8, 32, 128), BF),
    b1_in=pltpu.VMEM((3, 8, 2, 32, 128), BF),
    b2=pltpu.VMEM((8, 2, 32, 128), BF),
    b2_in=pltpu.VMEM((3, 8, 32, 128), BF),
    c3=pltpu.VMEM((8, 32, 128), BF),
    c3_in=pltpu.VMEM((7, 32, 128), BF),
    m0=pltpu.VMEM((8, 2, 2, 32, 256), BF),
    m0_in=pltpu.VMEM((8, 2, 32, 256), BF),
    m1=pltpu.VMEM((8, 2, 32, 256), BF),
    m1_in=pltpu.VMEM((8, 32, 256), BF),
    m2=pltpu.VMEM((8, 32, 256), BF),
    m2_in=pltpu.VMEM((7, 32, 256), BF),
    local=pltpu.SemaphoreType.DMA((10,)),
    send=pltpu.SemaphoreType.DMA((112,)),
    recv=pltpu.SemaphoreType.DMA((112,)),
)


class Scratch:
    def __init__(self, refs):
        for name, ref in zip(SCRATCH, refs, strict=True):
            setattr(self, name, ref)


def norm_back(xhat, inverse, g):
    mean_g = jnp.mean(g, axis=-1, keepdims=True)
    mean_gx = jnp.mean(g * xhat, axis=-1, keepdims=True)
    return inverse * (g - mean_g - xhat * mean_gx)


def by_x(rows):
    low = lax.broadcasted_iota(jnp.int32, (rows.shape[0], 128), 1) < 64
    tiles = []
    for t in range(4):
        one = rows[:, (t // 2) * 128 : (t // 2) * 128 + 128]
        two = rows[:, 256 + (t // 2) * 128 : 256 + (t // 2) * 128 + 128]
        if t % 2 == 0:
            tiles.append(jnp.where(low, one, pltpu.roll(two, 64, 1)))
        else:
            tiles.append(jnp.where(low, pltpu.roll(one, 64, 1), two))
    return jnp.concatenate(tiles, axis=1)


def same_class(region, classes, lat):
    cell = lax.broadcasted_iota(jnp.int32, (12, WTOK), 1)
    column = (cell % 24) // 2
    source = lax.broadcasted_iota(jnp.int32, (12, WTOK), 0)
    from_west = f32((column + 6 == source)).astype(BF)
    from_east = f32((column - 6 == source)).astype(BF)
    row = lax.broadcasted_iota(jnp.int32, (6, WTOK), 1) // 24
    line = lax.broadcasted_iota(jnp.int32, (6, WTOK), 0)
    top = f32(row + 3 == line)
    bottom = f32(row - 3 == line)
    blocks = [f32(region[...]).astype(BF)] + [f32(classes[k]).astype(BF) for k in range(3)]
    own = (nn(blocks[0], from_west) + nn(blocks[1], from_east)) * top
    below = (nn(blocks[2], from_west) + nn(blocks[3], from_east)) * bottom
    label = 2.0 * jnp.sum(own + below, axis=0, keepdims=True)
    wraps = jnp.where(lat == 7, 1.0, 0.0)
    label = label + wraps * f32(lax.broadcasted_iota(jnp.int32, (1, WTOK), 1) >= 72)
    spread = jnp.broadcast_to(label, (8, WTOK)).astype(BF)
    down = tn(spread, jnp.full((8, WTOK), 0.125, BF))
    return down == label


def kernel(
    tokens, region, w_qkv, w_proj, w_merge, cotangent, moves,
    merged_out, tokens_out, qkv_out, proj_out, merge_out, *scratch
):
    s = Scratch(scratch)
    lat = lax.axis_index("lat")
    lon = lax.axis_index("lon")
    y_hi, x, z, y_lo, core = lat // 4, lat % 4, lon // 4, (lon // 2) % 2, lon % 2
    y = y_hi * 2 + y_lo
    south, north = (lat + 1) % 8, (lat + 7) % 8
    east, west = (lon + 1) % 32, (lon + 31) % 32

    def chip(y_hi, x, z, y_lo, core):
        return (y_hi * 4 + x, z * 4 + y_lo * 2 + core)

    back = [(lat, west), (north, lon), (north, west)]
    ahead = [(lat, east), (south, lon), (south, east)]
    ys = [(y + k) % 4 for k in range(1, 4)]
    zs = [(z + k) % 8 for k in range(1, 8)]
    xs = [(x + k) % 4 for k in range(1, 4)]
    lats = [(lat + k) % 8 for k in range(1, 8)]
    other_core = chip(y_hi, x, z, y_lo, 1 - core)
    y_chips = [chip(t // 2, x, z, t % 2, core) for t in ys]
    z_chips = [chip(y_hi, x, t, y_lo, core) for t in zs]
    x_chips = [chip(y_hi, t, z, y_lo, core) for t in xs]
    lat_chips = [(t, lon) for t in lats]
    y_lo_chip = chip(y_hi, x, z, 1 - y_lo, core)
    partners = lat_chips + [back[0], ahead[0], back[2], ahead[2], other_core, y_chips[0], y_chips[2]] + z_chips

    used = iter(range(112))

    def push(src, dst, target):
        at = next(used)
        copy = pltpu.make_async_remote_copy(
            src_ref=src,
            dst_ref=dst,
            send_sem=s.send.at[at],
            recv_sem=s.recv.at[at],
            device_id=target,
            device_id_type=MESH,
        )
        copy.start()
        return copy

    held = iter(range(10))

    def fetch(src, dst):
        copy = pltpu.make_async_copy(src, dst, s.local.at[next(held)])
        copy.start()
        return copy

    def wait(copies):
        for copy in copies:
            copy.wait()

    barrier = pltpu.get_barrier_semaphore()
    for target in partners:
        pl.semaphore_signal(barrier, inc=1, device_id=target, device_id_type=MESH)
    own_tokens = fetch(tokens.at[3:6, 6:12], s.halo.at[0])
    own_moves = fetch(moves, s.moves)
    own_cot = [
        fetch(cotangent.at[1:3, 3:6], s.cot.at[lat, 0:2, 0:3]),
        fetch(cotangent.at[0:1, 3:6], s.cot.at[north, 2:3, 0:3]),
    ]
    pl.semaphore_wait(barrier, len(partners))
    class_halos = [push(region, s.classes.at[k], back[k]) for k in range(3)]
    halos = [
        push(tokens.at[0:3, 6:12], s.halo.at[2], back[1]),
        push(tokens.at[0:3, 0:6], s.halo.at[3], back[2]),
        push(tokens.at[3:6, 0:6], s.halo.at[1], back[0]),
    ]
    cot_halos = [
        push(cotangent.at[1:3, 0:3], s.cot.at[lat, 0:2, 3:6], back[0]),
        push(cotangent.at[0:1, 0:3], s.cot.at[north, 2:3, 3:6], back[0]),
    ]
    own_qkv = fetch(w_qkv, s.w_qkv)
    own_proj = fetch(w_proj, s.w_proj)
    own_merge = fetch(w_merge, s.w_merge)
    wait(own_cot + cot_halos)

    def gather_cot(offset):
        chip_at = lat_chips[offset - 1]
        return [
            push(s.cot.at[lat, 0:2], s.cot.at[lat, 0:2], chip_at),
            push(s.cot.at[north, 2:3], s.cot.at[north, 2:3], chip_at),
        ]

    to_north = gather_cot(7)
    cot_sends = gather_cot(1) + gather_cot(4)
    wait([own_moves, own_tokens] + class_halos + halos)

    same = same_class(region, s.classes, lat)
    rolled = nn(s.moves[0:288, 0:TOK], s.halo[...].reshape(TOK, D))
    s.rolled[...] = rolled.astype(BF)
    centred = rolled - jnp.mean(rolled, axis=-1, keepdims=True)
    inverse = lax.rsqrt(jnp.mean(centred * centred, axis=-1, keepdims=True) + EPS)
    xhat = centred * inverse
    s.xhat[...] = xhat
    s.normed[...] = xhat.astype(BF)
    wait([own_qkv])
    normed = s.normed[...]
    for part in range(3):
        cols = slice(part * D, part * D + D)
        made = nn(normed, s.w_qkv[:, cols]).astype(BF)
        s.qkv[:, cols] = made * jnp.asarray(0.125, BF) if part == 0 else made

    lane = lax.broadcasted_iota(jnp.int32, (1, 128), 1)
    halves = [f32(lane < 64).astype(BF), f32(lane >= 64).astype(BF)]
    low = lax.broadcasted_iota(jnp.int32, (WTOK, 128), 1) < 64

    def scores_of(step):
        w, lo = step // 4, step % 4 * 128
        rows = slice(w * WTOK, w * WTOK + WTOK)
        query, keys = s.qkv[rows, lo : lo + 128], s.qkv[rows, D + lo : D + lo + 128]
        return [nt(keys, query * halves[half]) for half in range(2)]

    ahead_scores = scores_of(0)
    for step in range(8):
        w, lo = step // 4, step % 4 * 128
        rows = slice(w * WTOK, w * WTOK + WTOK)
        scores = ahead_scores
        if step < 7:
            ahead_scores = scores_of(step + 1)
        values = s.qkv[rows, 2 * D + lo : 2 * D + lo + 128]
        scores = [jnp.where(same, one, -1e30) for one in scores]
        expo = [jnp.exp(one - jnp.max(one, axis=0, keepdims=True)) for one in scores]
        probs = [one * (1.0 / jnp.sum(one, axis=0, keepdims=True)) for one in expo]
        for half in range(2):
            s.probs[step * 2 + half] = probs[half]
        out = [tn(one.astype(BF), values) for one in probs]
        s.attn[rows, lo : lo + 128] = jnp.where(low, out[0], out[1]).astype(BF)

    wait([own_proj])
    hidden = (f32(s.rolled[...]) + nn(s.attn[...], s.w_proj[...])).astype(BF)
    s.first_out[...] = nn(s.moves[1248:1296, 0:TOK], hidden).astype(BF)
    s.last_out[...] = nn(s.moves[1296:1344, 0:TOK], hidden).astype(BF)
    rims = [push(s.first_out, s.first_in, back[1]), push(s.last_out, s.last_in, ahead[1])]

    parts = nn(s.moves[576:960, 0:TOK], hidden)
    wait([own_merge] + to_north)
    cot_own = jnp.concatenate([s.cot[lat], s.cot[south, 0:1]], axis=0).reshape(MALL, D2)
    g = [f32(nt(cot_own, s.w_merge[r * D : r * D + D, :]).astype(BF)) for r in range(4)]
    wait(rims)
    cot_sends += gather_cot(2) + gather_cot(6) + gather_cot(3) + gather_cot(5)
    above = nn(s.moves[1536:1728, 0:RIM], s.last_in[...])
    below = nn(s.moves[1344:1536, 0:RIM], s.first_in[...])
    corner = [parts[r * MALL : r * MALL + MALL] for r in range(4)]
    corner = [corner[0] + above[:MALL], corner[1] + above[MALL:], corner[2] + below[:MALL], corner[3] + below[MALL:]]
    mean = sum(jnp.sum(c, axis=-1, keepdims=True) for c in corner) * (1.0 / 2048)
    corner = [c - mean for c in corner]
    var = sum(jnp.sum(c * c, axis=-1, keepdims=True) for c in corner) * (1.0 / 2048)
    m_inverse = lax.rsqrt(var + EPS)
    corner = [c * m_inverse for c in corner]
    for r in range(4):
        s.merge_in[:, r * D : r * D + D] = corner[r].astype(BF)
    merge_sends = [
        push(
            s.merge_in.at[0:MPAD, pl.ds(pl.multiple_of(lats[k] * 256, 256), 256)], s.merges.at[lat], lat_chips[k]
        )
        for k in range(7)
    ]
    s.merges[lat] = s.merge_in[0:MPAD, pl.ds(pl.multiple_of(lat * 256, 256), 256)]

    mean_g = sum(jnp.sum(d, axis=-1, keepdims=True) for d in g) * (1.0 / 2048)
    mean_gx = sum(jnp.sum(d * c, axis=-1, keepdims=True) for d, c in zip(g, corner)) * (1.0 / 2048)
    d_corner = jnp.concatenate([m_inverse * (d - mean_g - c * mean_gx) for d, c in zip(g, corner)], axis=0).astype(BF)
    d_hidden = nn(s.moves[960:1248], d_corner).astype(BF)
    s.d_hidden[...] = d_hidden

    s.d_attn[...] = nt(d_hidden, s.w_proj[...]).astype(BF)
    for w in range(2):
        rows = slice(w * WTOK, w * WTOK + WTOK)
        for pair in range(4):
            lo = pair * 128
            grad = s.d_attn[rows, lo : lo + 128]
            d_values = [nn(s.probs[w * 8 + pair * 2 + half].astype(BF), grad) for half in range(2)]
            s.d_qkv[rows, 2 * D + lo : 2 * D + lo + 128] = jnp.where(low, d_values[0], d_values[1]).astype(BF)

    grad_proj = by_x(tn(s.d_hidden[...], s.attn[...])).astype(BF)
    for j in range(32):
        s.c0[j // 4, (j // 2) % 2, j % 2, 48:64] = grad_proj[16 * j : 16 * j + 16]
    normed = s.normed[...]

    def grad_qkv(part):
        made = tn(s.d_qkv[:, part * D : part * D + D], normed)
        moved = by_x(made).astype(BF)
        made = made.astype(BF)
        for block in range(part * 32, part * 32 + 32):
            j, third = block // 3, block % 3
            rows = (moved if third == 2 else made)[16 * block - part * D : 16 * block - part * D + 16]
            s.c0[j // 4, (j // 2) % 2, j % 2, 16 * third : 16 * third + 16] = rows

    def to_core(span):
        return push(s.c0.at[span, :, 1 - core], s.c0_in.at[span], other_core)

    def to_axes(span, copy):
        copy.wait()

        @pl.loop(span.start, span.stop)
        def _(step):
            for row in range(2):
                s.c1[step, row] = (f32(s.c0[step, row, core]) + f32(s.c0_in[step, row])).astype(BF)

        return [
            push(
                s.c1.at[span, t % 2, 0:32, pl.ds(pl.multiple_of((t // 2) * 256, 256), 256)],
                s.a1_in.at[k, span],
                y_chips[k],
            )
            for k, t in enumerate(ys)
        ] + [
            push(
                s.c1.at[span, :, 32:64, pl.ds(pl.multiple_of(t * 128, 128), 128)], s.b1_in.at[k, span], x_chips[k]
            )
            for k, t in enumerate(xs)
        ]

    def to_other_axes(span, copies):
        wait(copies)

        @pl.loop(span.start, span.stop)
        def _(step):
            total = f32(s.c1[step, y_lo, 0:32, pl.ds(pl.multiple_of(y_hi * 256, 256), 256)])
            for k in range(3):
                total = total + f32(s.a1_in[k, step])
            s.a2[step] = total.astype(BF)
            for row in range(2):
                total = f32(s.c1[step, row, 32:64, pl.ds(pl.multiple_of(x * 128, 128), 128)])
                for k in range(3):
                    total = total + f32(s.b1_in[k, step, row])
                s.b2[step, row] = total.astype(BF)

        return [
            push(
                s.a2.at[span, :, pl.ds(pl.multiple_of((t // 2) * 128, 128), 128)], s.a2_in.at[k, span], x_chips[k]
            )
            for k, t in enumerate(xs)
        ] + [push(s.b2.at[span, t % 2], s.b2_in.at[k, span], y_chips[k]) for k, t in enumerate(ys)]

    chunks = [slice(6, 8), slice(0, 2), slice(2, 6)]
    grad_qkv(2)
    core_copies = [to_core(chunks[0])]
    axis_copies = []

    def d_probs_of(step):
        w, lo = step // 4, step % 4 * 128
        rows = slice(w * WTOK, w * WTOK + WTOK)
        values, grad = s.qkv[rows, 2 * D + lo : 2 * D + lo + 128], s.d_attn[rows, lo : lo + 128]
        return [nt(values, grad * halves[half]) for half in range(2)]

    ahead_d_probs = d_probs_of(0)
    for step in range(8):
        w, lo = step // 4, step % 4 * 128
        rows = slice(w * WTOK, w * WTOK + WTOK)
        d_probs = ahead_d_probs
        if step < 7:
            ahead_d_probs = d_probs_of(step + 1)
        query = s.qkv[rows, lo : lo + 128]
        keys = s.qkv[rows, D + lo : D + lo + 128]
        probs = [s.probs[step * 2 + half] for half in range(2)]
        dots = [jnp.sum(d * p, axis=0, keepdims=True) for d, p in zip(d_probs, probs)]
        d_scores = [(p * (d - dot)).astype(BF) for d, p, dot in zip(d_probs, probs, dots)]
        d_query = [tn(one, keys) for one in d_scores]
        d_keys = [nn(one, query) for one in d_scores]
        s.d_qkv[rows, lo : lo + 128] = (jnp.where(low, d_query[0], d_query[1]) * 0.125).astype(BF)
        s.d_qkv[rows, D + lo : D + lo + 128] = jnp.where(low, d_keys[0], d_keys[1]).astype(BF)
        if step == 3:
            axis_copies.append(to_axes(chunks[0], core_copies[0]))

    grad_qkv(0)
    core_copies.append(to_core(chunks[1]))
    grad_qkv(1)
    core_copies.append(to_core(chunks[2]))
    axis_copies.append(to_axes(chunks[1], core_copies[1]))

    for part in range(2):
        cols = slice(part * D, part * D + D)
        made = nn(s.merge_in[0:MPAD], s.w_merge[:, cols])[:MTOK].astype(BF)
        s.merged[:, :, :, cols] = made.reshape(3, 6, 4, D)

    axis_copies.append(to_axes(chunks[2], core_copies[2]))
    other_copies = [to_other_axes(chunks[0], axis_copies[0])]

    d_normed = nt(s.d_qkv[:, 0:D], s.w_qkv[:, 0:D])
    for part in range(1, 3):
        cols = slice(part * D, part * D + D)
        d_normed = d_normed + nt(s.d_qkv[:, cols], s.w_qkv[:, cols])
    d_tokens = (f32(s.d_hidden[...]) + norm_back(s.xhat[...], inverse, d_normed)).astype(BF)
    s.d_tokens[...] = nn(s.moves[288:576, 0:TOK], d_tokens).astype(BF).reshape(4, 3, 6, 4, D)

    other_copies.append(to_other_axes(chunks[1], axis_copies[1]))
    wait(cot_sends + merge_sends)
    for slot in range(8):
        rows = [f32(s.cot[slot].reshape(MTOK, D2)), jnp.zeros((MPAD - MTOK, D2), F32)]
        s.cots[slot] = jnp.concatenate(rows, axis=0).astype(BF)
    merges = s.merges[...].reshape(8 * MPAD, 256)
    for part in range(4):
        cots = s.cots[:, :, part * 256 : part * 256 + 256].reshape(8 * MPAD, 256)
        made = tn(cots, merges).astype(BF)
        s.m0[2 * part : 2 * part + 2] = made.reshape(2, 2, 2, 32, 256)
    m_copy = push(s.m0.at[:, :, 1 - core], s.m0_in, other_core)

    wait([m_copy])

    @pl.loop(0, 8)
    def _(step):
        for row in range(2):
            s.m1[step, row] = (f32(s.m0[step, row, core]) + f32(s.m0_in[step, row])).astype(BF)

    m_copy = push(s.m1.at[:, 1 - y_lo], s.m1_in, y_lo_chip)
    other_copies.append(to_other_axes(chunks[2], axis_copies[2]))
    last_sends = [
        push(s.merged.at[0:2, 3:6], merged_out.at[1:3, 0:3], ahead[0]),
        push(s.merged.at[2:3, 0:3], merged_out.at[0:1, 3:6], ahead[1]),
        push(s.merged.at[2:3, 3:6], merged_out.at[0:1, 0:3], ahead[2]),
        fetch(s.merged.at[0:2, 0:3], merged_out.at[1:3, 3:6]),
        push(s.d_tokens.at[1], tokens_out.at[3:6, 0:6], ahead[0]),
        push(s.d_tokens.at[2], tokens_out.at[0:3, 6:12], ahead[1]),
        push(s.d_tokens.at[3], tokens_out.at[0:3, 0:6], ahead[2]),
        fetch(s.d_tokens.at[0], tokens_out.at[3:6, 6:12]),
    ]
    wait([m_copy])

    @pl.loop(0, 8)
    def _(step):
        s.m2[step] = (f32(s.m1[step, y_lo]) + f32(s.m1_in[step])).astype(BF)

    m_copies = [push(s.m2.at[t], s.m2_in.at[k], z_chips[k]) for k, t in enumerate(zs)]
    for copies in other_copies:
        wait(copies)
    left = lax.broadcasted_iota(jnp.int32, (32, 128), 1) < 64

    @pl.loop(0, 8)
    def _(step):
        one = f32(s.a2[step, :, pl.ds(pl.multiple_of((x // 2) * 128, 128), 128)])
        two = f32(s.b2[step, y_lo])
        for k in range(3):
            one = one + f32(s.a2_in[k, step])
            two = two + f32(s.b2_in[k, step])
        one = jnp.where(x % 2 == 1, pltpu.roll(one, 64, 1), one)
        two = jnp.where(y_hi == 0, pltpu.roll(two, 64, 1), two)
        s.c3[step] = jnp.where(left, one, two).astype(BF)

    c_copies = [push(s.c3.at[t], s.c3_in.at[k], z_chips[k]) for k, t in enumerate(zs)]
    wait(c_copies)
    total = f32(s.c3[z])
    for k in range(7):
        total = total + f32(s.c3_in[k])
    qkv_out[0:32] = total[:, :64]
    qkv_out[32:48] = total[:16, 64:]
    proj_out[...] = total[16:, 64:]
    wait(m_copies)
    total = f32(s.m2[z])
    for k in range(7):
        total = total + f32(s.m2_in[k])
    merge_out[...] = total
    wait(last_sends)


def hand_over(*refs):
    held, done = refs[10:15], refs[15]
    into = [pltpu.make_async_copy(refs[k], held[k], done.at[k]) for k in range(5)]
    out = [pltpu.make_async_copy(held[k], refs[5 + k], done.at[5 + k]) for k in range(5)]
    for copy in into:
        copy.start()
    for one, two in zip(into, out):
        one.wait()
        two.start()
    for copy in out:
        copy.wait()


def shards(tokens, region, w_qkv, w_proj, w_merge, cotangent):
    hbm = pl.BlockSpec(memory_space=pltpu.HBM)
    vmem = pl.BlockSpec(memory_space=pltpu.VMEM)
    made = pl.pallas_call(
        kernel,
        out_shape=(
            jax.ShapeDtypeStruct((3, 6, 4, D2), BF),
            jax.ShapeDtypeStruct((6, 12, 4, D), BF),
            jax.ShapeDtypeStruct((48, 64), F32),
            jax.ShapeDtypeStruct((16, 64), F32),
            jax.ShapeDtypeStruct((32, 256), F32),
        ),
        in_specs=[hbm, vmem, hbm, hbm, hbm, hbm, hbm],
        out_specs=(hbm, hbm, vmem, vmem, vmem),
        scratch_shapes=list(SCRATCH.values()),
        compiler_params=pltpu.CompilerParams(
            collective_id=0, has_side_effects=True, vmem_limit_bytes=56 * 1024 * 1024
        ),
    )(tokens, region, w_qkv, w_proj, w_merge, cotangent, jnp.asarray(one_hot_moves()))
    merged, grad_tokens, grad_qkv, grad_proj, grad_merge = pl.pallas_call(
        hand_over,
        out_shape=tuple(jax.ShapeDtypeStruct(a.shape, a.dtype) for a in made),
        in_specs=[hbm] * 5,
        out_specs=(hbm,) * 5,
        scratch_shapes=[pltpu.VMEM(a.shape, a.dtype) for a in made] + [pltpu.SemaphoreType.DMA((10,))],
        compiler_params=pltpu.CompilerParams(vmem_limit_bytes=56 * 1024 * 1024),
    )(*made)
    return (merged, grad_tokens, grad_qkv.T, grad_proj.T, grad_merge.T)


def solution(mesh):
    return jax.shard_map(
        shards,
        mesh=mesh,
        in_specs=(
            P("lat", "lon", None, None),
            P("lat", "lon"),
            P(),
            P(),
            P(),
            P("lat", "lon", None, None),
        ),
        out_specs=(
            P("lat", "lon", None, None),
            P("lat", "lon", None, None),
            P("lat", "lon"),
            P("lat", "lon"),
            P("lat", "lon"),
        ),
        check_vma=False,
    )
```

```python
import jax
import jax.numpy as jnp
import numpy as np
from jax import lax
from jax.experimental import pallas as pl
from jax.experimental.pallas import tpu as pltpu
from jax.sharding import PartitionSpec as P

MESH = pl.DeviceIdType.MESH
BF = jnp.bfloat16
F32 = jnp.float32
D = 512
D2 = 1024
TOK = 288
WTOK = 144
MTOK = 72
MPAD = 80
MALL = 96
RIM = 48
EPS = 1e-05


def f32(x):
    return x.astype(F32)


def nn(a, b):
    return jnp.dot(a, b, preferred_element_type=F32)


def nt(a, b):
    return lax.dot_general(a, b, (((1,), (1,)), ((), ())), preferred_element_type=F32)


def tn(a, b):
    return lax.dot_general(a, b, (((0,), (0,)), ((), ())), preferred_element_type=F32)


def one_hot_moves():
    into = np.zeros((TOK, TOK))
    part = np.zeros((4 * MALL, TOK))
    first = np.zeros((RIM, TOK))
    last = np.zeros((RIM, TOK))
    late = np.zeros((2 * MALL, RIM))
    early = np.zeros((2 * MALL, RIM))
    for c in range(12):
        for l in range(4):
            patch = (c // 2) * 4 + l
            for r in range(6):
                natural = ((r // 3) * 2 + c // 6) * 72 + (r % 3) * 24 + (c % 6) * 4 + l
                window = (l // 2) * WTOK + r * 24 + c * 2 + l % 2
                into[window, natural] = 1
                a = (r + 1) // 2
                part[(((r - 1) % 2) * 2 + c % 2) * MALL + a * 24 + patch, window] = 1
                if r == 0:
                    first[c * 4 + l, window] = 1
                if r == 5:
                    last[c * 4 + l, window] = 1
            late[(c % 2) * MALL + 72 + patch, c * 4 + l] = 1
            early[(c % 2) * MALL + patch, c * 4 + l] = 1
    rows = [into, into.T, part, part.T, first, last, late, early]
    rows = [np.pad(m, ((0, 0), (0, 4 * MALL - m.shape[1]))) for m in rows]
    return np.concatenate(rows, axis=0).astype(jnp.bfloat16)


SCRATCH = dict(
    moves=pltpu.VMEM((1728, 4 * MALL), BF),
    w_qkv=pltpu.VMEM((D, 3 * D), BF),
    w_proj=pltpu.VMEM((D, D), BF),
    w_merge=pltpu.VMEM((4 * D, D2), BF),
    halo=pltpu.VMEM((4, 3, 6, 4, D), BF),
    classes=pltpu.VMEM((3, 6, 12), jnp.int32),
    cot=pltpu.VMEM((4, 3, 6, 4, D2), BF),
    cot_top=pltpu.VMEM((1, 6, 4, D2), BF),
    cot_below=pltpu.VMEM((1, 6, 4, D2), BF),
    normed=pltpu.VMEM((TOK, D), BF),
    rolled=pltpu.VMEM((TOK, D), BF),
    xhat=pltpu.VMEM((TOK, D), F32),
    qkv=pltpu.VMEM((TOK, 3 * D), BF),
    probs=pltpu.VMEM((16, WTOK, WTOK), F32),
    attn=pltpu.VMEM((TOK, D), BF),
    first_out=pltpu.VMEM((RIM, D), BF),
    first_in=pltpu.VMEM((RIM, D), BF),
    last_out=pltpu.VMEM((RIM, D), BF),
    last_in=pltpu.VMEM((RIM, D), BF),
    merge_in=pltpu.VMEM((MALL, 4 * D), BF),
    merged=pltpu.VMEM((3, 6, 4, D2), BF),
    cots=pltpu.VMEM((4, MPAD, D2), BF),
    merges=pltpu.VMEM((4, MPAD, 512), BF),
    d_hidden=pltpu.VMEM((TOK, D), BF),
    d_attn=pltpu.VMEM((TOK, D), BF),
    d_qkv=pltpu.VMEM((TOK, 3 * D), BF),
    d_tokens=pltpu.VMEM((4, 3, 6, 4, D), BF),
    c0=pltpu.VMEM((8, 2, 2, 64, D), BF),
    c0_in=pltpu.VMEM((8, 2, 64, D), BF),
    c1=pltpu.VMEM((8, 2, 64, D), BF),
    a1_in=pltpu.VMEM((3, 8, 32, 256), BF),
    a2=pltpu.VMEM((8, 32, 256), BF),
    a2_in=pltpu.VMEM((3, 8, 32, 128), BF),
    b1_in=pltpu.VMEM((3, 8, 2, 32, 128), BF),
    b2=pltpu.VMEM((8, 2, 32, 128), BF),
    b2_in=pltpu.VMEM((3, 8, 32, 128), BF),
    c3=pltpu.VMEM((8, 32, 128), BF),
    c3_in=pltpu.VMEM((7, 32, 128), BF),
    m0=pltpu.VMEM((8, 2, 2, 32, 512), BF),
    m0_in=pltpu.VMEM((8, 2, 32, 512), BF),
    m1=pltpu.VMEM((8, 2, 32, 512), BF),
    m1_in=pltpu.VMEM((7, 2, 32, 512), BF),
    m2=pltpu.VMEM((2, 32, 512), BF),
    m2_in=pltpu.VMEM((3, 32, 256), BF),
    local=pltpu.SemaphoreType.DMA((10,)),
    send=pltpu.SemaphoreType.DMA((112,)),
    recv=pltpu.SemaphoreType.DMA((112,)),
)


class Scratch:
    def __init__(self, refs):
        for name, ref in zip(SCRATCH, refs, strict=True):
            setattr(self, name, ref)


def norm_back(xhat, inverse, g):
    mean_g = jnp.mean(g, axis=-1, keepdims=True)
    mean_gx = jnp.mean(g * xhat, axis=-1, keepdims=True)
    return inverse * (g - mean_g - xhat * mean_gx)


def by_x(rows):
    low = lax.broadcasted_iota(jnp.int32, (rows.shape[0], 128), 1) < 64
    tiles = []
    for t in range(4):
        one = rows[:, (t // 2) * 128 : (t // 2) * 128 + 128]
        two = rows[:, 256 + (t // 2) * 128 : 256 + (t // 2) * 128 + 128]
        if t % 2 == 0:
            tiles.append(jnp.where(low, one, pltpu.roll(two, 64, 1)))
        else:
            tiles.append(jnp.where(low, pltpu.roll(one, 64, 1), two))
    return jnp.concatenate(tiles, axis=1)


def same_class(region, classes, lat):
    cell = lax.broadcasted_iota(jnp.int32, (12, WTOK), 1)
    column = (cell % 24) // 2
    source = lax.broadcasted_iota(jnp.int32, (12, WTOK), 0)
    from_west = f32((column + 6 == source)).astype(BF)
    from_east = f32((column - 6 == source)).astype(BF)
    row = lax.broadcasted_iota(jnp.int32, (6, WTOK), 1) // 24
    line = lax.broadcasted_iota(jnp.int32, (6, WTOK), 0)
    top = f32(row + 3 == line)
    bottom = f32(row - 3 == line)
    blocks = [f32(region[...]).astype(BF)] + [f32(classes[k]).astype(BF) for k in range(3)]
    own = (nn(blocks[0], from_west) + nn(blocks[1], from_east)) * top
    below = (nn(blocks[2], from_west) + nn(blocks[3], from_east)) * bottom
    label = 2.0 * jnp.sum(own + below, axis=0, keepdims=True)
    wraps = jnp.where(lat == 7, 1.0, 0.0)
    label = label + wraps * f32(lax.broadcasted_iota(jnp.int32, (1, WTOK), 1) >= 72)
    spread = jnp.broadcast_to(label, (8, WTOK)).astype(BF)
    down = tn(spread, jnp.full((8, WTOK), 0.125, BF))
    return down == label


def kernel(
    tokens, region, w_qkv, w_proj, w_merge, cotangent, moves,
    merged_out, tokens_out, qkv_out, proj_out, merge_out, *scratch
):
    s = Scratch(scratch)
    lat = lax.axis_index("lat")
    lon = lax.axis_index("lon")
    y_hi, x, z, y_lo, core = lat // 4, lat % 4, lon // 4, (lon // 2) % 2, lon % 2
    y = y_hi * 2 + y_lo
    south, north = (lat + 1) % 8, (lat + 7) % 8
    east, west = (lon + 1) % 32, (lon + 31) % 32

    def chip(y_hi, x, z, y_lo, core):
        return (y_hi * 4 + x, z * 4 + y_lo * 2 + core)

    back = [(lat, west), (north, lon), (north, west)]
    ahead = [(lat, east), (south, lon), (south, east)]
    ys = [(y + k) % 4 for k in range(1, 4)]
    zs = [(z + k) % 8 for k in range(1, 8)]
    xs = [(x + k) % 4 for k in range(1, 4)]
    other_core = chip(y_hi, x, z, y_lo, 1 - core)
    y_chips = [chip(t // 2, x, z, t % 2, core) for t in ys]
    z_chips = [chip(y_hi, x, t, y_lo, core) for t in zs]
    x_chips = [chip(y_hi, t, z, y_lo, core) for t in xs]
    partners = back + ahead + [other_core] + y_chips + z_chips + x_chips

    used = iter(range(112))

    def push(src, dst, target):
        at = next(used)
        copy = pltpu.make_async_remote_copy(
            src_ref=src,
            dst_ref=dst,
            send_sem=s.send.at[at],
            recv_sem=s.recv.at[at],
            device_id=target,
            device_id_type=MESH,
        )
        copy.start()
        return copy

    held = iter(range(10))

    def fetch(src, dst):
        copy = pltpu.make_async_copy(src, dst, s.local.at[next(held)])
        copy.start()
        return copy

    def wait(copies):
        for copy in copies:
            copy.wait()

    barrier = pltpu.get_barrier_semaphore()
    for target in partners:
        pl.semaphore_signal(barrier, inc=1, device_id=target, device_id_type=MESH)
    own_tokens = fetch(tokens.at[3:6, 6:12], s.halo.at[0])
    own_moves = fetch(moves, s.moves)
    own_cot = [
        fetch(cotangent.at[1:3, 3:6], s.cot.at[x, 0:2, 0:3]),
        fetch(cotangent.at[0:1, 3:6], s.cot_top.at[0:1, 0:3]),
    ]
    pl.semaphore_wait(barrier, len(partners))
    class_halos = [push(region, s.classes.at[k], back[k]) for k in range(3)]
    halos = [
        push(tokens.at[0:3, 6:12], s.halo.at[2], back[1]),
        push(tokens.at[0:3, 0:6], s.halo.at[3], back[2]),
        push(tokens.at[3:6, 0:6], s.halo.at[1], back[0]),
    ]
    cot_halos = [
        push(cotangent.at[1:3, 0:3], s.cot.at[x, 0:2, 3:6], back[0]),
        push(cotangent.at[0:1, 0:3], s.cot_top.at[0:1, 3:6], back[0]),
    ]
    own_qkv = fetch(w_qkv, s.w_qkv)
    own_proj = fetch(w_proj, s.w_proj)
    own_merge = fetch(w_merge, s.w_merge)
    wait(own_cot + cot_halos)

    def gather_cot(offset, rows):
        return [push(s.cot.at[x, rows], s.cot.at[x, rows], x_chips[offset - 1])]

    to_north = [
        push(s.cot_top, s.cot.at[(x + 3) % 4, 2:3], back[1]),
        push(s.cot.at[x, 0:1], s.cot_below, back[1]),
    ]
    cot_sends = gather_cot(1, slice(0, 2)) + gather_cot(3, slice(0, 2))
    wait([own_moves, own_tokens] + class_halos + halos)

    same = same_class(region, s.classes, lat)
    rolled = nn(s.moves[0:288, 0:TOK], s.halo[...].reshape(TOK, D))
    s.rolled[...] = rolled.astype(BF)
    centred = rolled - jnp.mean(rolled, axis=-1, keepdims=True)
    inverse = lax.rsqrt(jnp.mean(centred * centred, axis=-1, keepdims=True) + EPS)
    xhat = centred * inverse
    s.xhat[...] = xhat
    s.normed[...] = xhat.astype(BF)
    wait([own_qkv])
    normed = s.normed[...]
    for part in range(3):
        cols = slice(part * D, part * D + D)
        made = nn(normed, s.w_qkv[:, cols]).astype(BF)
        s.qkv[:, cols] = made * jnp.asarray(0.125, BF) if part == 0 else made

    lane = lax.broadcasted_iota(jnp.int32, (1, 128), 1)
    halves = [f32(lane < 64).astype(BF), f32(lane >= 64).astype(BF)]
    low = lax.broadcasted_iota(jnp.int32, (WTOK, 128), 1) < 64

    def scores_of(step):
        w, lo = step // 4, step % 4 * 128
        rows = slice(w * WTOK, w * WTOK + WTOK)
        query, keys = s.qkv[rows, lo : lo + 128], s.qkv[rows, D + lo : D + lo + 128]
        return [nt(keys, query * halves[half]) for half in range(2)]

    ahead_scores = scores_of(0)
    for step in range(8):
        w, lo = step // 4, step % 4 * 128
        rows = slice(w * WTOK, w * WTOK + WTOK)
        scores = ahead_scores
        if step < 7:
            ahead_scores = scores_of(step + 1)
        values = s.qkv[rows, 2 * D + lo : 2 * D + lo + 128]
        scores = [jnp.where(same, one, -1e30) for one in scores]
        expo = [jnp.exp(one - jnp.max(one, axis=0, keepdims=True)) for one in scores]
        probs = [one * (1.0 / jnp.sum(one, axis=0, keepdims=True)) for one in expo]
        for half in range(2):
            s.probs[step * 2 + half] = probs[half]
        out = [tn(one.astype(BF), values) for one in probs]
        s.attn[rows, lo : lo + 128] = jnp.where(low, out[0], out[1]).astype(BF)

    wait([own_proj])
    hidden = (f32(s.rolled[...]) + nn(s.attn[...], s.w_proj[...])).astype(BF)
    s.first_out[...] = nn(s.moves[1248:1296, 0:TOK], hidden).astype(BF)
    s.last_out[...] = nn(s.moves[1296:1344, 0:TOK], hidden).astype(BF)
    rims = [push(s.first_out, s.first_in, back[1]), push(s.last_out, s.last_in, ahead[1])]

    parts = nn(s.moves[576:960, 0:TOK], hidden)
    wait([own_merge] + to_north)
    cot_own = jnp.concatenate([s.cot[x], s.cot_below[...]], axis=0).reshape(MALL, D2)
    g = [f32(nt(cot_own, s.w_merge[r * D : r * D + D, :]).astype(BF)) for r in range(4)]
    wait(rims)
    cot_sends += gather_cot(2, slice(0, 3)) + gather_cot(1, slice(2, 3)) + gather_cot(3, slice(2, 3))
    above = nn(s.moves[1536:1728, 0:RIM], s.last_in[...])
    below = nn(s.moves[1344:1536, 0:RIM], s.first_in[...])
    corner = [parts[r * MALL : r * MALL + MALL] for r in range(4)]
    corner = [corner[0] + above[:MALL], corner[1] + above[MALL:], corner[2] + below[:MALL], corner[3] + below[MALL:]]
    mean = sum(jnp.sum(c, axis=-1, keepdims=True) for c in corner) * (1.0 / 2048)
    corner = [c - mean for c in corner]
    var = sum(jnp.sum(c * c, axis=-1, keepdims=True) for c in corner) * (1.0 / 2048)
    m_inverse = lax.rsqrt(var + EPS)
    corner = [c * m_inverse for c in corner]
    for r in range(4):
        s.merge_in[:, r * D : r * D + D] = corner[r].astype(BF)
    merge_sends = []
    for half in range(2):
        lanes = slice(half * 256, half * 256 + 256)
        for k, t in enumerate(xs):
            at = pl.multiple_of(half * 1024 + t * 256, 256)
            merge_sends.append(push(s.merge_in.at[0:MPAD, pl.ds(at, 256)], s.merges.at[x, :, lanes], x_chips[k]))
        s.merges[x, :, lanes] = s.merge_in[0:MPAD, pl.ds(pl.multiple_of(half * 1024 + x * 256, 256), 256)]

    mean_g = sum(jnp.sum(d, axis=-1, keepdims=True) for d in g) * (1.0 / 2048)
    mean_gx = sum(jnp.sum(d * c, axis=-1, keepdims=True) for d, c in zip(g, corner)) * (1.0 / 2048)
    d_corner = jnp.concatenate([m_inverse * (d - mean_g - c * mean_gx) for d, c in zip(g, corner)], axis=0).astype(BF)
    d_hidden = nn(s.moves[960:1248], d_corner).astype(BF)
    s.d_hidden[...] = d_hidden

    s.d_attn[...] = nt(d_hidden, s.w_proj[...]).astype(BF)
    for w in range(2):
        rows = slice(w * WTOK, w * WTOK + WTOK)
        for pair in range(4):
            lo = pair * 128
            grad = s.d_attn[rows, lo : lo + 128]
            d_values = [nn(s.probs[w * 8 + pair * 2 + half].astype(BF), grad) for half in range(2)]
            s.d_qkv[rows, 2 * D + lo : 2 * D + lo + 128] = jnp.where(low, d_values[0], d_values[1]).astype(BF)

    grad_proj = by_x(tn(s.d_hidden[...], s.attn[...])).astype(BF)
    for j in range(32):
        s.c0[j // 4, (j // 2) % 2, j % 2, 48:64] = grad_proj[16 * j : 16 * j + 16]
    normed = s.normed[...]

    def grad_qkv(part):
        made = tn(s.d_qkv[:, part * D : part * D + D], normed)
        moved = by_x(made).astype(BF)
        made = made.astype(BF)
        for block in range(part * 32, part * 32 + 32):
            j, third = block // 3, block % 3
            rows = (moved if third == 2 else made)[16 * block - part * D : 16 * block - part * D + 16]
            s.c0[j // 4, (j // 2) % 2, j % 2, 16 * third : 16 * third + 16] = rows

    def to_core(span):
        return push(s.c0.at[span, :, 1 - core], s.c0_in.at[span], other_core)

    def to_axes(span, copy):
        copy.wait()

        @pl.loop(span.start, span.stop)
        def _(step):
            for row in range(2):
                s.c1[step, row] = (f32(s.c0[step, row, core]) + f32(s.c0_in[step, row])).astype(BF)

        return [
            push(
                s.c1.at[span, t % 2, 0:32, pl.ds(pl.multiple_of((t // 2) * 256, 256), 256)],
                s.a1_in.at[k, span],
                y_chips[k],
            )
            for k, t in enumerate(ys)
        ] + [
            push(
                s.c1.at[span, :, 32:64, pl.ds(pl.multiple_of(t * 128, 128), 128)], s.b1_in.at[k, span], x_chips[k]
            )
            for k, t in enumerate(xs)
        ]

    def to_other_axes(span, copies):
        wait(copies)

        @pl.loop(span.start, span.stop)
        def _(step):
            total = f32(s.c1[step, y_lo, 0:32, pl.ds(pl.multiple_of(y_hi * 256, 256), 256)])
            for k in range(3):
                total = total + f32(s.a1_in[k, step])
            s.a2[step] = total.astype(BF)
            for row in range(2):
                total = f32(s.c1[step, row, 32:64, pl.ds(pl.multiple_of(x * 128, 128), 128)])
                for k in range(3):
                    total = total + f32(s.b1_in[k, step, row])
                s.b2[step, row] = total.astype(BF)

        return [
            push(
                s.a2.at[span, :, pl.ds(pl.multiple_of((t // 2) * 128, 128), 128)], s.a2_in.at[k, span], x_chips[k]
            )
            for k, t in enumerate(xs)
        ] + [push(s.b2.at[span, t % 2], s.b2_in.at[k, span], y_chips[k]) for k, t in enumerate(ys)]

    chunks = [slice(6, 8), slice(0, 2), slice(2, 6)]
    grad_qkv(2)
    core_copies = [to_core(chunks[0])]
    axis_copies = []

    def d_probs_of(step):
        w, lo = step // 4, step % 4 * 128
        rows = slice(w * WTOK, w * WTOK + WTOK)
        values, grad = s.qkv[rows, 2 * D + lo : 2 * D + lo + 128], s.d_attn[rows, lo : lo + 128]
        return [nt(values, grad * halves[half]) for half in range(2)]

    ahead_d_probs = d_probs_of(0)
    for step in range(8):
        w, lo = step // 4, step % 4 * 128
        rows = slice(w * WTOK, w * WTOK + WTOK)
        d_probs = ahead_d_probs
        if step < 7:
            ahead_d_probs = d_probs_of(step + 1)
        query = s.qkv[rows, lo : lo + 128]
        keys = s.qkv[rows, D + lo : D + lo + 128]
        probs = [s.probs[step * 2 + half] for half in range(2)]
        dots = [jnp.sum(d * p, axis=0, keepdims=True) for d, p in zip(d_probs, probs)]
        d_scores = [(p * (d - dot)).astype(BF) for d, p, dot in zip(d_probs, probs, dots)]
        d_query = [tn(one, keys) for one in d_scores]
        d_keys = [nn(one, query) for one in d_scores]
        s.d_qkv[rows, lo : lo + 128] = (jnp.where(low, d_query[0], d_query[1]) * 0.125).astype(BF)
        s.d_qkv[rows, D + lo : D + lo + 128] = jnp.where(low, d_keys[0], d_keys[1]).astype(BF)
        if step == 3:
            axis_copies.append(to_axes(chunks[0], core_copies[0]))

    grad_qkv(0)
    core_copies.append(to_core(chunks[1]))
    grad_qkv(1)
    core_copies.append(to_core(chunks[2]))
    axis_copies.append(to_axes(chunks[1], core_copies[1]))

    wait(cot_sends + merge_sends)
    for slot in range(4):
        rows = [f32(s.cot[slot].reshape(MTOK, D2)), jnp.zeros((MPAD - MTOK, D2), F32)]
        s.cots[slot] = jnp.concatenate(rows, axis=0).astype(BF)
    merges = s.merges[...].reshape(4 * MPAD, 512)
    for part in range(4):
        cots = s.cots[:, :, part * 256 : part * 256 + 256].reshape(4 * MPAD, 256)
        made = tn(cots, merges).astype(BF)
        s.m0[2 * part : 2 * part + 2] = made.reshape(2, 2, 2, 32, 512)
    m_copy = push(s.m0.at[:, :, 1 - core], s.m0_in, other_core)


    axis_copies.append(to_axes(chunks[2], core_copies[2]))
    other_copies = [to_other_axes(chunks[0], axis_copies[0])]
    for part in range(2):
        cols = slice(part * D, part * D + D)
        made = nn(s.merge_in[0:MPAD], s.w_merge[:, cols])[:MTOK].astype(BF)
        s.merged[:, :, :, cols] = made.reshape(3, 6, 4, D)

    wait([m_copy])

    @pl.loop(0, 8)
    def _(step):
        for row in range(2):
            s.m1[step, row] = (f32(s.m0[step, row, core]) + f32(s.m0_in[step, row])).astype(BF)

    m_copies = [push(s.m1.at[t], s.m1_in.at[k], z_chips[k]) for k, t in enumerate(zs)]
    other_copies.append(to_other_axes(chunks[1], axis_copies[1]))

    d_normed = nt(s.d_qkv[:, 0:D], s.w_qkv[:, 0:D])
    for part in range(1, 3):
        cols = slice(part * D, part * D + D)
        d_normed = d_normed + nt(s.d_qkv[:, cols], s.w_qkv[:, cols])
    d_tokens = (f32(s.d_hidden[...]) + norm_back(s.xhat[...], inverse, d_normed)).astype(BF)
    s.d_tokens[...] = nn(s.moves[288:576, 0:TOK], d_tokens).astype(BF).reshape(4, 3, 6, 4, D)

    other_copies.append(to_other_axes(chunks[2], axis_copies[2]))
    last_sends = [
        push(s.merged.at[0:2, 3:6], merged_out.at[1:3, 0:3], ahead[0]),
        push(s.merged.at[2:3, 0:3], merged_out.at[0:1, 3:6], ahead[1]),
        push(s.merged.at[2:3, 3:6], merged_out.at[0:1, 0:3], ahead[2]),
        fetch(s.merged.at[0:2, 0:3], merged_out.at[1:3, 3:6]),
        push(s.d_tokens.at[1], tokens_out.at[3:6, 0:6], ahead[0]),
        push(s.d_tokens.at[2], tokens_out.at[0:3, 6:12], ahead[1]),
        push(s.d_tokens.at[3], tokens_out.at[0:3, 0:6], ahead[2]),
        fetch(s.d_tokens.at[0], tokens_out.at[3:6, 6:12]),
    ]
    for copies in other_copies:
        wait(copies)
    left = lax.broadcasted_iota(jnp.int32, (32, 128), 1) < 64

    @pl.loop(0, 8)
    def _(step):
        one = f32(s.a2[step, :, pl.ds(pl.multiple_of((x // 2) * 128, 128), 128)])
        two = f32(s.b2[step, y_lo])
        for k in range(3):
            one = one + f32(s.a2_in[k, step])
            two = two + f32(s.b2_in[k, step])
        one = jnp.where(x % 2 == 1, pltpu.roll(one, 64, 1), one)
        two = jnp.where(y_hi == 0, pltpu.roll(two, 64, 1), two)
        s.c3[step] = jnp.where(left, one, two).astype(BF)

    c_copies = [push(s.c3.at[t], s.c3_in.at[k], z_chips[k]) for k, t in enumerate(zs)]
    wait(m_copies)
    total = f32(s.m1[z])
    for k in range(7):
        total = total + f32(s.m1_in[k])
    s.m2[...] = total.astype(BF)
    m_copies = [
        push(s.m2.at[t % 2, :, pl.ds(pl.multiple_of((t // 2) * 256, 256), 256)], s.m2_in.at[k], y_chips[k])
        for k, t in enumerate(ys)
    ]
    wait(c_copies)
    total = f32(s.c3[z])
    for k in range(7):
        total = total + f32(s.c3_in[k])
    qkv_out[0:32] = total[:, :64]
    qkv_out[32:48] = total[:16, 64:]
    proj_out[...] = total[16:, 64:]
    wait(m_copies)
    total = f32(s.m2[y_lo, :, pl.ds(pl.multiple_of(y_hi * 256, 256), 256)])
    for k in range(3):
        total = total + f32(s.m2_in[k])
    merge_out[...] = total
    wait(last_sends)


def hand_over(*refs):
    held, done = refs[10:15], refs[15]
    into = [pltpu.make_async_copy(refs[k], held[k], done.at[k]) for k in range(5)]
    out = [pltpu.make_async_copy(held[k], refs[5 + k], done.at[5 + k]) for k in range(5)]
    for copy in into:
        copy.start()
    for one, two in zip(into, out):
        one.wait()
        two.start()
    for copy in out:
        copy.wait()


def shards(tokens, region, w_qkv, w_proj, w_merge, cotangent):
    hbm = pl.BlockSpec(memory_space=pltpu.HBM)
    vmem = pl.BlockSpec(memory_space=pltpu.VMEM)
    made = pl.pallas_call(
        kernel,
        out_shape=(
            jax.ShapeDtypeStruct((3, 6, 4, D2), BF),
            jax.ShapeDtypeStruct((6, 12, 4, D), BF),
            jax.ShapeDtypeStruct((48, 64), F32),
            jax.ShapeDtypeStruct((16, 64), F32),
            jax.ShapeDtypeStruct((32, 256), F32),
        ),
        in_specs=[hbm, vmem, hbm, hbm, hbm, hbm, hbm],
        out_specs=(hbm, hbm, vmem, vmem, vmem),
        scratch_shapes=list(SCRATCH.values()),
        compiler_params=pltpu.CompilerParams(
            collective_id=0, has_side_effects=True, vmem_limit_bytes=56 * 1024 * 1024
        ),
    )(tokens, region, w_qkv, w_proj, w_merge, cotangent, jnp.asarray(one_hot_moves()))
    merged, grad_tokens, grad_qkv, grad_proj, grad_merge = pl.pallas_call(
        hand_over,
        out_shape=tuple(jax.ShapeDtypeStruct(a.shape, a.dtype) for a in made),
        in_specs=[hbm] * 5,
        out_specs=(hbm,) * 5,
        scratch_shapes=[pltpu.VMEM(a.shape, a.dtype) for a in made] + [pltpu.SemaphoreType.DMA((10,))],
        compiler_params=pltpu.CompilerParams(vmem_limit_bytes=56 * 1024 * 1024),
    )(*made)
    return (merged, grad_tokens, grad_qkv.T, grad_proj.T, grad_merge.T)


def solution(mesh):
    return jax.shard_map(
        shards,
        mesh=mesh,
        in_specs=(
            P("lat", "lon", None, None),
            P("lat", "lon"),
            P(),
            P(),
            P(),
            P("lat", "lon", None, None),
        ),
        out_specs=(
            P("lat", "lon", None, None),
            P("lat", "lon", None, None),
            P("lat", "lon"),
            P("lat", "lon"),
            P("lat", "lon"),
        ),
        check_vma=False,
    )
```

```python
import jax
import jax.numpy as jnp
import numpy as np
from jax import lax
from jax.experimental import pallas as pl
from jax.experimental.pallas import tpu as pltpu
from jax.sharding import PartitionSpec as P

MESH = pl.DeviceIdType.MESH
BF = jnp.bfloat16
F32 = jnp.float32
D = 512
D2 = 1024
TOK = 288
WTOK = 144
MTOK = 72
MPAD = 80
MALL = 96
RIM = 48
EPS = 1e-05


def f32(x):
    return x.astype(F32)


def nn(a, b):
    return jnp.dot(a, b, preferred_element_type=F32)


def nt(a, b):
    return lax.dot_general(a, b, (((1,), (1,)), ((), ())), preferred_element_type=F32)


def tn(a, b):
    return lax.dot_general(a, b, (((0,), (0,)), ((), ())), preferred_element_type=F32)


def one_hot_moves():
    into = np.zeros((TOK, TOK))
    part = np.zeros((4 * MALL, TOK))
    first = np.zeros((RIM, TOK))
    last = np.zeros((RIM, TOK))
    late = np.zeros((2 * MALL, RIM))
    early = np.zeros((2 * MALL, RIM))
    for c in range(12):
        for l in range(4):
            patch = (c // 2) * 4 + l
            for r in range(6):
                natural = ((r // 3) * 2 + c // 6) * 72 + (r % 3) * 24 + (c % 6) * 4 + l
                window = (l // 2) * WTOK + r * 24 + c * 2 + l % 2
                into[window, natural] = 1
                a = (r + 1) // 2
                part[(((r - 1) % 2) * 2 + c % 2) * MALL + a * 24 + patch, window] = 1
                if r == 0:
                    first[c * 4 + l, window] = 1
                if r == 5:
                    last[c * 4 + l, window] = 1
            late[(c % 2) * MALL + 72 + patch, c * 4 + l] = 1
            early[(c % 2) * MALL + patch, c * 4 + l] = 1
    rows = [into, into.T, part, part.T, first, last, late, early]
    rows = [np.pad(m, ((0, 0), (0, 4 * MALL - m.shape[1]))) for m in rows]
    return np.concatenate(rows, axis=0).astype(jnp.bfloat16)


SCRATCH = dict(
    moves=pltpu.VMEM((1728, 4 * MALL), BF),
    w_qkv=pltpu.VMEM((D, 3 * D), BF),
    w_proj=pltpu.VMEM((D, D), BF),
    w_merge=pltpu.VMEM((4 * D, D2), BF),
    halo=pltpu.VMEM((4, 3, 6, 4, D), BF),
    classes=pltpu.VMEM((3, 6, 12), jnp.int32),
    cot=pltpu.VMEM((4, 3, 6, 4, D2), BF),
    cot_top=pltpu.VMEM((1, 6, 4, D2), BF),
    cot_below=pltpu.VMEM((1, 6, 4, D2), BF),
    normed=pltpu.VMEM((TOK, D), BF),
    rolled=pltpu.VMEM((TOK, D), BF),
    xhat=pltpu.VMEM((TOK, D), F32),
    qkv=pltpu.VMEM((TOK, 3 * D), BF),
    probs=pltpu.VMEM((16, WTOK, WTOK), F32),
    attn=pltpu.VMEM((TOK, D), BF),
    first_out=pltpu.VMEM((RIM, D), BF),
    first_in=pltpu.VMEM((RIM, D), BF),
    last_out=pltpu.VMEM((RIM, D), BF),
    last_in=pltpu.VMEM((RIM, D), BF),
    merge_in=pltpu.VMEM((MALL, 4 * D), BF),
    merged=pltpu.VMEM((3, 6, 4, D2), BF),
    cots=pltpu.VMEM((4, MPAD, D2), BF),
    merges=pltpu.VMEM((4, MPAD, 512), BF),
    d_hidden=pltpu.VMEM((TOK, D), BF),
    d_attn=pltpu.VMEM((TOK, D), BF),
    d_qkv=pltpu.VMEM((TOK, 3 * D), BF),
    d_tokens=pltpu.VMEM((4, 3, 6, 4, D), BF),
    c0=pltpu.VMEM((8, 2, 2, 64, D), BF),
    c0_in=pltpu.VMEM((8, 2, 64, D), BF),
    c1=pltpu.VMEM((8, 2, 64, D), BF),
    a1_in=pltpu.VMEM((3, 8, 32, 256), BF),
    a2=pltpu.VMEM((8, 32, 256), BF),
    a2_in=pltpu.VMEM((3, 8, 32, 128), BF),
    b1_in=pltpu.VMEM((3, 8, 2, 32, 128), BF),
    b2=pltpu.VMEM((8, 2, 32, 128), BF),
    b2_in=pltpu.VMEM((3, 8, 32, 128), BF),
    c3=pltpu.VMEM((8, 32, 128), BF),
    c3_in=pltpu.VMEM((7, 32, 128), BF),
    m0=pltpu.VMEM((8, 2, 2, 32, 512), BF),
    m0_in=pltpu.VMEM((8, 2, 32, 512), BF),
    m1=pltpu.VMEM((8, 2, 32, 512), BF),
    m1_in=pltpu.VMEM((7, 2, 32, 512), BF),
    m2=pltpu.VMEM((2, 32, 512), BF),
    m2_in=pltpu.VMEM((3, 32, 256), BF),
    local=pltpu.SemaphoreType.DMA((10,)),
    send=pltpu.SemaphoreType.DMA((112,)),
    recv=pltpu.SemaphoreType.DMA((112,)),
)


class Scratch:
    def __init__(self, refs):
        for name, ref in zip(SCRATCH, refs, strict=True):
            setattr(self, name, ref)


def norm_back(xhat, inverse, g):
    mean_g = jnp.mean(g, axis=-1, keepdims=True)
    mean_gx = jnp.mean(g * xhat, axis=-1, keepdims=True)
    return inverse * (g - mean_g - xhat * mean_gx)


def by_x(rows):
    low = lax.broadcasted_iota(jnp.int32, (rows.shape[0], 128), 1) < 64
    tiles = []
    for t in range(4):
        one = rows[:, (t // 2) * 128 : (t // 2) * 128 + 128]
        two = rows[:, 256 + (t // 2) * 128 : 256 + (t // 2) * 128 + 128]
        if t % 2 == 0:
            tiles.append(jnp.where(low, one, pltpu.roll(two, 64, 1)))
        else:
            tiles.append(jnp.where(low, pltpu.roll(one, 64, 1), two))
    return jnp.concatenate(tiles, axis=1)


def same_class(region, classes, lat):
    cell = lax.broadcasted_iota(jnp.int32, (12, WTOK), 1)
    column = (cell % 24) // 2
    source = lax.broadcasted_iota(jnp.int32, (12, WTOK), 0)
    from_west = f32((column + 6 == source)).astype(BF)
    from_east = f32((column - 6 == source)).astype(BF)
    row = lax.broadcasted_iota(jnp.int32, (6, WTOK), 1) // 24
    line = lax.broadcasted_iota(jnp.int32, (6, WTOK), 0)
    top = f32(row + 3 == line)
    bottom = f32(row - 3 == line)
    blocks = [f32(region[...]).astype(BF)] + [f32(classes[k]).astype(BF) for k in range(3)]
    own = (nn(blocks[0], from_west) + nn(blocks[1], from_east)) * top
    below = (nn(blocks[2], from_west) + nn(blocks[3], from_east)) * bottom
    label = 2.0 * jnp.sum(own + below, axis=0, keepdims=True)
    wraps = jnp.where(lat == 7, 1.0, 0.0)
    label = label + wraps * f32(lax.broadcasted_iota(jnp.int32, (1, WTOK), 1) >= 72)
    spread = jnp.broadcast_to(label, (8, WTOK)).astype(BF)
    down = tn(spread, jnp.full((8, WTOK), 0.125, BF))
    return down == label


def kernel(
    tokens, region, w_qkv, w_proj, w_merge, cotangent, moves,
    merged_out, tokens_out, qkv_out, proj_out, merge_out, *scratch
):
    s = Scratch(scratch)
    lat = lax.axis_index("lat")
    lon = lax.axis_index("lon")
    y_hi, x, z, y_lo, core = lat // 4, lat % 4, lon // 4, (lon // 2) % 2, lon % 2
    y = y_hi * 2 + y_lo
    south, north = (lat + 1) % 8, (lat + 7) % 8
    east, west = (lon + 1) % 32, (lon + 31) % 32

    def chip(y_hi, x, z, y_lo, core):
        return (y_hi * 4 + x, z * 4 + y_lo * 2 + core)

    back = [(lat, west), (north, lon), (north, west)]
    ahead = [(lat, east), (south, lon), (south, east)]
    ys = [(y + k) % 4 for k in range(1, 4)]
    zs = [(z + k) % 8 for k in range(1, 8)]
    xs = [(x + k) % 4 for k in range(1, 4)]
    other_core = chip(y_hi, x, z, y_lo, 1 - core)
    y_chips = [chip(t // 2, x, z, t % 2, core) for t in ys]
    z_chips = [chip(y_hi, x, t, y_lo, core) for t in zs]
    x_chips = [chip(y_hi, t, z, y_lo, core) for t in xs]
    partners = back + ahead + [other_core] + y_chips + z_chips + x_chips

    used = iter(range(112))

    def push(src, dst, target):
        at = next(used)
        copy = pltpu.make_async_remote_copy(
            src_ref=src,
            dst_ref=dst,
            send_sem=s.send.at[at],
            recv_sem=s.recv.at[at],
            device_id=target,
            device_id_type=MESH,
        )
        copy.start()
        return copy

    held = iter(range(10))

    def fetch(src, dst):
        copy = pltpu.make_async_copy(src, dst, s.local.at[next(held)])
        copy.start()
        return copy

    def wait(copies):
        for copy in copies:
            copy.wait()

    barrier = pltpu.get_barrier_semaphore()
    for target in partners:
        pl.semaphore_signal(barrier, inc=1, device_id=target, device_id_type=MESH)
    own_tokens = fetch(tokens.at[3:6, 6:12], s.halo.at[0])
    own_moves = fetch(moves, s.moves)
    own_cot = [
        fetch(cotangent.at[1:3, 3:6], s.cot.at[x, 0:2, 0:3]),
        fetch(cotangent.at[0:1, 3:6], s.cot_top.at[0:1, 0:3]),
    ]
    pl.semaphore_wait(barrier, len(partners))
    class_halos = [push(region, s.classes.at[k], back[k]) for k in range(3)]
    halos = [
        push(tokens.at[0:3, 6:12], s.halo.at[2], back[1]),
        push(tokens.at[0:3, 0:6], s.halo.at[3], back[2]),
        push(tokens.at[3:6, 0:6], s.halo.at[1], back[0]),
    ]
    cot_halos = [
        push(cotangent.at[1:3, 0:3], s.cot.at[x, 0:2, 3:6], back[0]),
        push(cotangent.at[0:1, 0:3], s.cot_top.at[0:1, 3:6], back[0]),
    ]
    own_qkv = fetch(w_qkv, s.w_qkv)
    own_proj = fetch(w_proj, s.w_proj)
    own_merge = fetch(w_merge, s.w_merge)
    wait(own_cot + cot_halos)

    def gather_cot(offset, rows):
        return [push(s.cot.at[x, rows], s.cot.at[x, rows], x_chips[offset - 1])]

    to_north = [
        push(s.cot_top, s.cot.at[(x + 3) % 4, 2:3], back[1]),
        push(s.cot.at[x, 0:1], s.cot_below, back[1]),
    ]
    cot_sends = gather_cot(1, slice(0, 2)) + gather_cot(3, slice(0, 2)) + gather_cot(2, slice(0, 2))
    wait([own_moves, own_tokens] + class_halos + halos)

    same = same_class(region, s.classes, lat)
    rolled = nn(s.moves[0:288, 0:TOK], s.halo[...].reshape(TOK, D))
    s.rolled[...] = rolled.astype(BF)
    centred = rolled - jnp.mean(rolled, axis=-1, keepdims=True)
    inverse = lax.rsqrt(jnp.mean(centred * centred, axis=-1, keepdims=True) + EPS)
    xhat = centred * inverse
    s.xhat[...] = xhat
    s.normed[...] = xhat.astype(BF)
    wait([own_qkv])
    normed = s.normed[...]
    for part in range(3):
        cols = slice(part * D, part * D + D)
        made = nn(normed, s.w_qkv[:, cols]).astype(BF)
        s.qkv[:, cols] = made * jnp.asarray(0.125, BF) if part == 0 else made

    lane = lax.broadcasted_iota(jnp.int32, (1, 128), 1)
    halves = [f32(lane < 64).astype(BF), f32(lane >= 64).astype(BF)]
    low = lax.broadcasted_iota(jnp.int32, (WTOK, 128), 1) < 64

    def scores_of(step):
        w, lo = step // 4, step % 4 * 128
        rows = slice(w * WTOK, w * WTOK + WTOK)
        query, keys = s.qkv[rows, lo : lo + 128], s.qkv[rows, D + lo : D + lo + 128]
        return [nt(keys, query * halves[half]) for half in range(2)]

    ahead_scores = scores_of(0)
    for step in range(8):
        w, lo = step // 4, step % 4 * 128
        rows = slice(w * WTOK, w * WTOK + WTOK)
        scores = ahead_scores
        if step < 7:
            ahead_scores = scores_of(step + 1)
        values = s.qkv[rows, 2 * D + lo : 2 * D + lo + 128]
        scores = [jnp.where(same, one, -1e30) for one in scores]
        expo = [jnp.exp(one - jnp.max(one, axis=0, keepdims=True)) for one in scores]
        probs = [one * (1.0 / jnp.sum(one, axis=0, keepdims=True)) for one in expo]
        for half in range(2):
            s.probs[step * 2 + half] = probs[half]
        out = [tn(one.astype(BF), values) for one in probs]
        s.attn[rows, lo : lo + 128] = jnp.where(low, out[0], out[1]).astype(BF)

    wait([own_proj])
    hidden = (f32(s.rolled[...]) + nn(s.attn[...], s.w_proj[...])).astype(BF)
    s.first_out[...] = nn(s.moves[1248:1296, 0:TOK], hidden).astype(BF)
    s.last_out[...] = nn(s.moves[1296:1344, 0:TOK], hidden).astype(BF)
    rims = [push(s.first_out, s.first_in, back[1]), push(s.last_out, s.last_in, ahead[1])]

    parts = nn(s.moves[576:960, 0:TOK], hidden)
    wait([own_merge] + to_north)
    cot_own = jnp.concatenate([s.cot[x], s.cot_below[...]], axis=0).reshape(MALL, D2)
    g = [f32(nt(cot_own, s.w_merge[r * D : r * D + D, :]).astype(BF)) for r in range(4)]
    wait(rims)
    cot_sends += gather_cot(1, slice(2, 3)) + gather_cot(3, slice(2, 3)) + gather_cot(2, slice(2, 3))
    above = nn(s.moves[1536:1728, 0:RIM], s.last_in[...])
    below = nn(s.moves[1344:1536, 0:RIM], s.first_in[...])
    corner = [parts[r * MALL : r * MALL + MALL] for r in range(4)]
    corner = [corner[0] + above[:MALL], corner[1] + above[MALL:], corner[2] + below[:MALL], corner[3] + below[MALL:]]
    mean = sum(jnp.sum(c, axis=-1, keepdims=True) for c in corner) * (1.0 / 2048)
    corner = [c - mean for c in corner]
    var = sum(jnp.sum(c * c, axis=-1, keepdims=True) for c in corner) * (1.0 / 2048)
    m_inverse = lax.rsqrt(var + EPS)
    corner = [c * m_inverse for c in corner]
    for r in range(4):
        s.merge_in[:, r * D : r * D + D] = corner[r].astype(BF)
    merge_sends = []
    for half in range(2):
        lanes = slice(half * 256, half * 256 + 256)
        for k, t in enumerate(xs):
            at = pl.multiple_of(half * 1024 + t * 256, 256)
            merge_sends.append(push(s.merge_in.at[0:MPAD, pl.ds(at, 256)], s.merges.at[x, :, lanes], x_chips[k]))
        s.merges[x, :, lanes] = s.merge_in[0:MPAD, pl.ds(pl.multiple_of(half * 1024 + x * 256, 256), 256)]

    mean_g = sum(jnp.sum(d, axis=-1, keepdims=True) for d in g) * (1.0 / 2048)
    mean_gx = sum(jnp.sum(d * c, axis=-1, keepdims=True) for d, c in zip(g, corner)) * (1.0 / 2048)
    d_corner = jnp.concatenate([m_inverse * (d - mean_g - c * mean_gx) for d, c in zip(g, corner)], axis=0).astype(BF)
    d_hidden = nn(s.moves[960:1248], d_corner).astype(BF)
    s.d_hidden[...] = d_hidden

    s.d_attn[...] = nt(d_hidden, s.w_proj[...]).astype(BF)
    for w in range(2):
        rows = slice(w * WTOK, w * WTOK + WTOK)
        for pair in range(4):
            lo = pair * 128
            grad = s.d_attn[rows, lo : lo + 128]
            d_values = [nn(s.probs[w * 8 + pair * 2 + half].astype(BF), grad) for half in range(2)]
            s.d_qkv[rows, 2 * D + lo : 2 * D + lo + 128] = jnp.where(low, d_values[0], d_values[1]).astype(BF)

    grad_proj = by_x(tn(s.d_hidden[...], s.attn[...])).astype(BF)
    for j in range(32):
        s.c0[j // 4, (j // 2) % 2, j % 2, 48:64] = grad_proj[16 * j : 16 * j + 16]
    normed = s.normed[...]

    def grad_qkv(part):
        made = tn(s.d_qkv[:, part * D : part * D + D], normed)
        moved = by_x(made).astype(BF)
        made = made.astype(BF)
        for block in range(part * 32, part * 32 + 32):
            j, third = block // 3, block % 3
            rows = (moved if third == 2 else made)[16 * block - part * D : 16 * block - part * D + 16]
            s.c0[j // 4, (j // 2) % 2, j % 2, 16 * third : 16 * third + 16] = rows

    def to_core(span):
        return push(s.c0.at[span, :, 1 - core], s.c0_in.at[span], other_core)

    def to_axes(span, copy):
        copy.wait()

        @pl.loop(span.start, span.stop)
        def _(step):
            for row in range(2):
                s.c1[step, row] = (f32(s.c0[step, row, core]) + f32(s.c0_in[step, row])).astype(BF)

        return [
            push(
                s.c1.at[span, t % 2, 0:32, pl.ds(pl.multiple_of((t // 2) * 256, 256), 256)],
                s.a1_in.at[k, span],
                y_chips[k],
            )
            for k, t in enumerate(ys)
        ] + [
            push(
                s.c1.at[span, :, 32:64, pl.ds(pl.multiple_of(t * 128, 128), 128)], s.b1_in.at[k, span], x_chips[k]
            )
            for k, t in enumerate(xs)
        ]

    def to_other_axes(span, copies):
        wait(copies)

        @pl.loop(span.start, span.stop)
        def _(step):
            total = f32(s.c1[step, y_lo, 0:32, pl.ds(pl.multiple_of(y_hi * 256, 256), 256)])
            for k in range(3):
                total = total + f32(s.a1_in[k, step])
            s.a2[step] = total.astype(BF)
            for row in range(2):
                total = f32(s.c1[step, row, 32:64, pl.ds(pl.multiple_of(x * 128, 128), 128)])
                for k in range(3):
                    total = total + f32(s.b1_in[k, step, row])
                s.b2[step, row] = total.astype(BF)

        return [
            push(
                s.a2.at[span, :, pl.ds(pl.multiple_of((t // 2) * 128, 128), 128)], s.a2_in.at[k, span], x_chips[k]
            )
            for k, t in enumerate(xs)
        ] + [push(s.b2.at[span, t % 2], s.b2_in.at[k, span], y_chips[k]) for k, t in enumerate(ys)]

    chunks = [slice(6, 8), slice(0, 2), slice(2, 6)]
    grad_qkv(2)
    core_copies = [to_core(chunks[0])]
    axis_copies = []

    def d_probs_of(step):
        w, lo = step // 4, step % 4 * 128
        rows = slice(w * WTOK, w * WTOK + WTOK)
        values, grad = s.qkv[rows, 2 * D + lo : 2 * D + lo + 128], s.d_attn[rows, lo : lo + 128]
        return [nt(values, grad * halves[half]) for half in range(2)]

    ahead_d_probs = d_probs_of(0)
    for step in range(8):
        w, lo = step // 4, step % 4 * 128
        rows = slice(w * WTOK, w * WTOK + WTOK)
        d_probs = ahead_d_probs
        if step < 7:
            ahead_d_probs = d_probs_of(step + 1)
        query = s.qkv[rows, lo : lo + 128]
        keys = s.qkv[rows, D + lo : D + lo + 128]
        probs = [s.probs[step * 2 + half] for half in range(2)]
        dots = [jnp.sum(d * p, axis=0, keepdims=True) for d, p in zip(d_probs, probs)]
        d_scores = [(p * (d - dot)).astype(BF) for d, p, dot in zip(d_probs, probs, dots)]
        d_query = [tn(one, keys) for one in d_scores]
        d_keys = [nn(one, query) for one in d_scores]
        s.d_qkv[rows, lo : lo + 128] = (jnp.where(low, d_query[0], d_query[1]) * 0.125).astype(BF)
        s.d_qkv[rows, D + lo : D + lo + 128] = jnp.where(low, d_keys[0], d_keys[1]).astype(BF)
        if step == 3:
            axis_copies.append(to_axes(chunks[0], core_copies[0]))

    grad_qkv(0)
    core_copies.append(to_core(chunks[1]))
    grad_qkv(1)
    core_copies.append(to_core(chunks[2]))
    axis_copies.append(to_axes(chunks[1], core_copies[1]))

    wait(cot_sends + merge_sends)
    for slot in range(4):
        rows = [f32(s.cot[slot].reshape(MTOK, D2)), jnp.zeros((MPAD - MTOK, D2), F32)]
        s.cots[slot] = jnp.concatenate(rows, axis=0).astype(BF)
    merges = s.merges[...].reshape(4 * MPAD, 512)
    for part in range(4):
        cots = s.cots[:, :, part * 256 : part * 256 + 256].reshape(4 * MPAD, 256)
        made = tn(cots, merges).astype(BF)
        s.m0[2 * part : 2 * part + 2] = made.reshape(2, 2, 2, 32, 512)
    m_copy = push(s.m0.at[:, :, 1 - core], s.m0_in, other_core)


    axis_copies.append(to_axes(chunks[2], core_copies[2]))
    other_copies = [to_other_axes(chunks[0], axis_copies[0])]
    for part in range(2):
        cols = slice(part * D, part * D + D)
        made = nn(s.merge_in[0:MPAD], s.w_merge[:, cols])[:MTOK].astype(BF)
        s.merged[:, :, :, cols] = made.reshape(3, 6, 4, D)

    wait([m_copy])

    @pl.loop(0, 8)
    def _(step):
        for row in range(2):
            s.m1[step, row] = (f32(s.m0[step, row, core]) + f32(s.m0_in[step, row])).astype(BF)

    m_copies = [push(s.m1.at[t], s.m1_in.at[k], z_chips[k]) for k, t in enumerate(zs)]
    other_copies.append(to_other_axes(chunks[1], axis_copies[1]))

    d_normed = nt(s.d_qkv[:, 0:D], s.w_qkv[:, 0:D])
    for part in range(1, 3):
        cols = slice(part * D, part * D + D)
        d_normed = d_normed + nt(s.d_qkv[:, cols], s.w_qkv[:, cols])
    d_tokens = (f32(s.d_hidden[...]) + norm_back(s.xhat[...], inverse, d_normed)).astype(BF)
    s.d_tokens[...] = nn(s.moves[288:576, 0:TOK], d_tokens).astype(BF).reshape(4, 3, 6, 4, D)

    other_copies.append(to_other_axes(chunks[2], axis_copies[2]))
    last_sends = [
        push(s.merged.at[0:2, 3:6], merged_out.at[1:3, 0:3], ahead[0]),
        push(s.merged.at[2:3, 0:3], merged_out.at[0:1, 3:6], ahead[1]),
        push(s.merged.at[2:3, 3:6], merged_out.at[0:1, 0:3], ahead[2]),
        fetch(s.merged.at[0:2, 0:3], merged_out.at[1:3, 3:6]),
        push(s.d_tokens.at[1], tokens_out.at[3:6, 0:6], ahead[0]),
        push(s.d_tokens.at[2], tokens_out.at[0:3, 6:12], ahead[1]),
        push(s.d_tokens.at[3], tokens_out.at[0:3, 0:6], ahead[2]),
        fetch(s.d_tokens.at[0], tokens_out.at[3:6, 6:12]),
    ]
    for copies in other_copies:
        wait(copies)
    left = lax.broadcasted_iota(jnp.int32, (32, 128), 1) < 64

    @pl.loop(0, 8)
    def _(step):
        one = f32(s.a2[step, :, pl.ds(pl.multiple_of((x // 2) * 128, 128), 128)])
        two = f32(s.b2[step, y_lo])
        for k in range(3):
            one = one + f32(s.a2_in[k, step])
            two = two + f32(s.b2_in[k, step])
        one = jnp.where(x % 2 == 1, pltpu.roll(one, 64, 1), one)
        two = jnp.where(y_hi == 0, pltpu.roll(two, 64, 1), two)
        s.c3[step] = jnp.where(left, one, two).astype(BF)

    c_copies = [push(s.c3.at[t], s.c3_in.at[k], z_chips[k]) for k, t in enumerate(zs)]
    wait(m_copies)
    total = f32(s.m1[z])
    for k in range(7):
        total = total + f32(s.m1_in[k])
    s.m2[...] = total.astype(BF)
    m_copies = [
        push(s.m2.at[t % 2, :, pl.ds(pl.multiple_of((t // 2) * 256, 256), 256)], s.m2_in.at[k], y_chips[k])
        for k, t in enumerate(ys)
    ]
    wait(c_copies)
    total = f32(s.c3[z])
    for k in range(7):
        total = total + f32(s.c3_in[k])
    qkv_out[0:32] = total[:, :64]
    qkv_out[32:48] = total[:16, 64:]
    proj_out[...] = total[16:, 64:]
    wait(m_copies)
    total = f32(s.m2[y_lo, :, pl.ds(pl.multiple_of(y_hi * 256, 256), 256)])
    for k in range(3):
        total = total + f32(s.m2_in[k])
    merge_out[...] = total
    wait(last_sends)


def hand_over(*refs):
    held, done = refs[10:15], refs[15]
    into = [pltpu.make_async_copy(refs[k], held[k], done.at[k]) for k in range(5)]
    out = [pltpu.make_async_copy(held[k], refs[5 + k], done.at[5 + k]) for k in range(5)]
    for copy in into:
        copy.start()
    for one, two in zip(into, out):
        one.wait()
        two.start()
    for copy in out:
        copy.wait()


def shards(tokens, region, w_qkv, w_proj, w_merge, cotangent):
    hbm = pl.BlockSpec(memory_space=pltpu.HBM)
    vmem = pl.BlockSpec(memory_space=pltpu.VMEM)
    made = pl.pallas_call(
        kernel,
        out_shape=(
            jax.ShapeDtypeStruct((3, 6, 4, D2), BF),
            jax.ShapeDtypeStruct((6, 12, 4, D), BF),
            jax.ShapeDtypeStruct((48, 64), F32),
            jax.ShapeDtypeStruct((16, 64), F32),
            jax.ShapeDtypeStruct((32, 256), F32),
        ),
        in_specs=[hbm, vmem, hbm, hbm, hbm, hbm, hbm],
        out_specs=(hbm, hbm, vmem, vmem, vmem),
        scratch_shapes=list(SCRATCH.values()),
        compiler_params=pltpu.CompilerParams(
            collective_id=0, has_side_effects=True, vmem_limit_bytes=56 * 1024 * 1024
        ),
    )(tokens, region, w_qkv, w_proj, w_merge, cotangent, jnp.asarray(one_hot_moves()))
    merged, grad_tokens, grad_qkv, grad_proj, grad_merge = pl.pallas_call(
        hand_over,
        out_shape=tuple(jax.ShapeDtypeStruct(a.shape, a.dtype) for a in made),
        in_specs=[hbm] * 5,
        out_specs=(hbm,) * 5,
        scratch_shapes=[pltpu.VMEM(a.shape, a.dtype) for a in made] + [pltpu.SemaphoreType.DMA((10,))],
        compiler_params=pltpu.CompilerParams(vmem_limit_bytes=56 * 1024 * 1024),
    )(*made)
    return (merged, grad_tokens, grad_qkv.T, grad_proj.T, grad_merge.T)


def solution(mesh):
    return jax.shard_map(
        shards,
        mesh=mesh,
        in_specs=(
            P("lat", "lon", None, None),
            P("lat", "lon"),
            P(),
            P(),
            P(),
            P("lat", "lon", None, None),
        ),
        out_specs=(
            P("lat", "lon", None, None),
            P("lat", "lon", None, None),
            P("lat", "lon"),
            P("lat", "lon"),
            P("lat", "lon"),
        ),
        check_vma=False,
    )
```

```python
import jax
import jax.numpy as jnp
import numpy as np
from jax import lax
from jax.experimental import pallas as pl
from jax.experimental.pallas import tpu as pltpu
from jax.sharding import PartitionSpec as P

MESH = pl.DeviceIdType.MESH
BF = jnp.bfloat16
F32 = jnp.float32
D = 512
D2 = 1024
TOK = 288
WTOK = 144
MTOK = 72
MPAD = 80
MALL = 96
RIM = 48
EPS = 1e-05


def f32(x):
    return x.astype(F32)


def nn(a, b):
    return jnp.dot(a, b, preferred_element_type=F32)


def nt(a, b):
    return lax.dot_general(a, b, (((1,), (1,)), ((), ())), preferred_element_type=F32)


def tn(a, b):
    return lax.dot_general(a, b, (((0,), (0,)), ((), ())), preferred_element_type=F32)


def one_hot_moves():
    into = np.zeros((TOK, TOK))
    part = np.zeros((4 * MALL, TOK))
    first = np.zeros((RIM, TOK))
    last = np.zeros((RIM, TOK))
    late = np.zeros((2 * MALL, RIM))
    early = np.zeros((2 * MALL, RIM))
    for c in range(12):
        for l in range(4):
            patch = (c // 2) * 4 + l
            for r in range(6):
                natural = ((r // 3) * 2 + c // 6) * 72 + (r % 3) * 24 + (c % 6) * 4 + l
                window = (l // 2) * WTOK + r * 24 + c * 2 + l % 2
                into[window, natural] = 1
                a = (r + 1) // 2
                part[(((r - 1) % 2) * 2 + c % 2) * MALL + a * 24 + patch, window] = 1
                if r == 0:
                    first[c * 4 + l, window] = 1
                if r == 5:
                    last[c * 4 + l, window] = 1
            late[(c % 2) * MALL + 72 + patch, c * 4 + l] = 1
            early[(c % 2) * MALL + patch, c * 4 + l] = 1
    rows = [into, into.T, part, part.T, first, last, late, early]
    rows = [np.pad(m, ((0, 0), (0, 4 * MALL - m.shape[1]))) for m in rows]
    return np.concatenate(rows, axis=0).astype(jnp.bfloat16)


SCRATCH = dict(
    moves=pltpu.VMEM((1728, 4 * MALL), BF),
    w_qkv=pltpu.VMEM((D, 3 * D), BF),
    w_proj=pltpu.VMEM((D, D), BF),
    w_merge=pltpu.VMEM((4 * D, D2), BF),
    halo=pltpu.VMEM((4, 3, 6, 4, D), BF),
    classes=pltpu.VMEM((3, 6, 12), jnp.int32),
    cot=pltpu.VMEM((4, 3, 6, 4, D2), BF),
    cot_top=pltpu.VMEM((1, 6, 4, D2), BF),
    cot_below=pltpu.VMEM((1, 6, 4, D2), BF),
    normed=pltpu.VMEM((TOK, D), BF),
    rolled=pltpu.VMEM((TOK, D), BF),
    xhat=pltpu.VMEM((TOK, D), F32),
    qkv=pltpu.VMEM((TOK, 3 * D), BF),
    probs=pltpu.VMEM((16, WTOK, WTOK), F32),
    attn=pltpu.VMEM((TOK, D), BF),
    first_out=pltpu.VMEM((RIM, D), BF),
    first_in=pltpu.VMEM((RIM, D), BF),
    last_out=pltpu.VMEM((RIM, D), BF),
    last_in=pltpu.VMEM((RIM, D), BF),
    merge_in=pltpu.VMEM((MALL, 4 * D), BF),
    merged=pltpu.VMEM((3, 6, 4, D2), BF),
    cots=pltpu.VMEM((4, MPAD, D2), BF),
    merges=pltpu.VMEM((4, MPAD, 512), BF),
    d_hidden=pltpu.VMEM((TOK, D), BF),
    d_attn=pltpu.VMEM((TOK, D), BF),
    d_qkv=pltpu.VMEM((TOK, 3 * D), BF),
    d_tokens=pltpu.VMEM((4, 3, 6, 4, D), BF),
    c0=pltpu.VMEM((8, 2, 2, 64, D), BF),
    c0_in=pltpu.VMEM((8, 2, 64, D), BF),
    c1=pltpu.VMEM((8, 2, 64, D), BF),
    a1_in=pltpu.VMEM((3, 8, 32, 256), BF),
    a2=pltpu.VMEM((8, 32, 256), BF),
    a2_in=pltpu.VMEM((3, 8, 32, 128), BF),
    b1_in=pltpu.VMEM((3, 8, 2, 32, 128), BF),
    b2=pltpu.VMEM((8, 2, 32, 128), BF),
    b2_in=pltpu.VMEM((3, 8, 32, 128), BF),
    c3=pltpu.VMEM((8, 32, 128), BF),
    c3_in=pltpu.VMEM((7, 32, 128), BF),
    m0=pltpu.VMEM((8, 2, 2, 32, 512), BF),
    m0_in=pltpu.VMEM((8, 2, 32, 512), BF),
    m1=pltpu.VMEM((8, 2, 32, 512), BF),
    m1_in=pltpu.VMEM((7, 2, 32, 512), BF),
    m2=pltpu.VMEM((2, 32, 512), BF),
    m2_in=pltpu.VMEM((3, 32, 256), BF),
    local=pltpu.SemaphoreType.DMA((10,)),
    send=pltpu.SemaphoreType.DMA((112,)),
    recv=pltpu.SemaphoreType.DMA((112,)),
)


class Scratch:
    def __init__(self, refs):
        for name, ref in zip(SCRATCH, refs, strict=True):
            setattr(self, name, ref)


def far_first(ring):
    return sorted(enumerate(ring), key=lambda one: -min(one[0] + 1, len(ring) - one[0]))


def norm_back(xhat, inverse, g):
    mean_g = jnp.mean(g, axis=-1, keepdims=True)
    mean_gx = jnp.mean(g * xhat, axis=-1, keepdims=True)
    return inverse * (g - mean_g - xhat * mean_gx)


def by_x(rows):
    low = lax.broadcasted_iota(jnp.int32, (rows.shape[0], 128), 1) < 64
    tiles = []
    for t in range(4):
        one = rows[:, (t // 2) * 128 : (t // 2) * 128 + 128]
        two = rows[:, 256 + (t // 2) * 128 : 256 + (t // 2) * 128 + 128]
        if t % 2 == 0:
            tiles.append(jnp.where(low, one, pltpu.roll(two, 64, 1)))
        else:
            tiles.append(jnp.where(low, pltpu.roll(one, 64, 1), two))
    return jnp.concatenate(tiles, axis=1)


def same_class(region, classes, lat):
    cell = lax.broadcasted_iota(jnp.int32, (12, WTOK), 1)
    column = (cell % 24) // 2
    source = lax.broadcasted_iota(jnp.int32, (12, WTOK), 0)
    from_west = f32((column + 6 == source)).astype(BF)
    from_east = f32((column - 6 == source)).astype(BF)
    row = lax.broadcasted_iota(jnp.int32, (6, WTOK), 1) // 24
    line = lax.broadcasted_iota(jnp.int32, (6, WTOK), 0)
    top = f32(row + 3 == line)
    bottom = f32(row - 3 == line)
    blocks = [f32(region[...]).astype(BF)] + [f32(classes[k]).astype(BF) for k in range(3)]
    own = (nn(blocks[0], from_west) + nn(blocks[1], from_east)) * top
    below = (nn(blocks[2], from_west) + nn(blocks[3], from_east)) * bottom
    label = 2.0 * jnp.sum(own + below, axis=0, keepdims=True)
    wraps = jnp.where(lat == 7, 1.0, 0.0)
    label = label + wraps * f32(lax.broadcasted_iota(jnp.int32, (1, WTOK), 1) >= 72)
    spread = jnp.broadcast_to(label, (8, WTOK)).astype(BF)
    down = tn(spread, jnp.full((8, WTOK), 0.125, BF))
    return down == label


def kernel(
    tokens, region, w_qkv, w_proj, w_merge, cotangent, moves,
    merged_out, tokens_out, qkv_out, proj_out, merge_out, *scratch
):
    s = Scratch(scratch)
    lat = lax.axis_index("lat")
    lon = lax.axis_index("lon")
    y_hi, x, z, y_lo, core = lat // 4, lat % 4, lon // 4, (lon // 2) % 2, lon % 2
    y = y_hi * 2 + y_lo
    south, north = (lat + 1) % 8, (lat + 7) % 8
    east, west = (lon + 1) % 32, (lon + 31) % 32

    def chip(y_hi, x, z, y_lo, core):
        return (y_hi * 4 + x, z * 4 + y_lo * 2 + core)

    back = [(lat, west), (north, lon), (north, west)]
    ahead = [(lat, east), (south, lon), (south, east)]
    ys = [(y + k) % 4 for k in range(1, 4)]
    zs = [(z + k) % 8 for k in range(1, 8)]
    xs = [(x + k) % 4 for k in range(1, 4)]
    other_core = chip(y_hi, x, z, y_lo, 1 - core)
    y_chips = [chip(t // 2, x, z, t % 2, core) for t in ys]
    z_chips = [chip(y_hi, x, t, y_lo, core) for t in zs]
    x_chips = [chip(y_hi, t, z, y_lo, core) for t in xs]
    partners = back + ahead + [other_core] + y_chips + z_chips + x_chips

    used = iter(range(112))

    def push(src, dst, target):
        at = next(used)
        copy = pltpu.make_async_remote_copy(
            src_ref=src,
            dst_ref=dst,
            send_sem=s.send.at[at],
            recv_sem=s.recv.at[at],
            device_id=target,
            device_id_type=MESH,
        )
        copy.start()
        return copy

    held = iter(range(10))

    def fetch(src, dst):
        copy = pltpu.make_async_copy(src, dst, s.local.at[next(held)])
        copy.start()
        return copy

    def wait(copies):
        for copy in copies:
            copy.wait()

    barrier = pltpu.get_barrier_semaphore()
    for target in partners:
        pl.semaphore_signal(barrier, inc=1, device_id=target, device_id_type=MESH)
    own_tokens = fetch(tokens.at[3:6, 6:12], s.halo.at[0])
    own_moves = fetch(moves, s.moves)
    own_cot = [
        fetch(cotangent.at[1:3, 3:6], s.cot.at[x, 0:2, 0:3]),
        fetch(cotangent.at[0:1, 3:6], s.cot_top.at[0:1, 0:3]),
    ]
    pl.semaphore_wait(barrier, len(partners))
    class_halos = [push(region, s.classes.at[k], back[k]) for k in range(3)]
    halos = [
        push(tokens.at[0:3, 6:12], s.halo.at[2], back[1]),
        push(tokens.at[0:3, 0:6], s.halo.at[3], back[2]),
        push(tokens.at[3:6, 0:6], s.halo.at[1], back[0]),
    ]
    cot_halos = [
        push(cotangent.at[1:3, 0:3], s.cot.at[x, 0:2, 3:6], back[0]),
        push(cotangent.at[0:1, 0:3], s.cot_top.at[0:1, 3:6], back[0]),
    ]
    own_qkv = fetch(w_qkv, s.w_qkv)
    own_proj = fetch(w_proj, s.w_proj)
    own_merge = fetch(w_merge, s.w_merge)
    wait(own_cot + cot_halos)

    def gather_cot(offset, rows):
        return [push(s.cot.at[x, rows], s.cot.at[x, rows], x_chips[offset - 1])]

    to_north = [
        push(s.cot_top, s.cot.at[(x + 3) % 4, 2:3], back[1]),
        push(s.cot.at[x, 0:1], s.cot_below, back[1]),
    ]
    cot_sends = gather_cot(1, slice(0, 2)) + gather_cot(3, slice(0, 2)) + gather_cot(2, slice(0, 2))
    wait([own_moves, own_tokens] + class_halos + halos)

    same = same_class(region, s.classes, lat)
    rolled = nn(s.moves[0:288, 0:TOK], s.halo[...].reshape(TOK, D))
    s.rolled[...] = rolled.astype(BF)
    centred = rolled - jnp.mean(rolled, axis=-1, keepdims=True)
    inverse = lax.rsqrt(jnp.mean(centred * centred, axis=-1, keepdims=True) + EPS)
    xhat = centred * inverse
    s.xhat[...] = xhat
    s.normed[...] = xhat.astype(BF)
    wait([own_qkv])
    normed = s.normed[...]
    for part in range(3):
        cols = slice(part * D, part * D + D)
        made = nn(normed, s.w_qkv[:, cols]).astype(BF)
        s.qkv[:, cols] = made * jnp.asarray(0.125, BF) if part == 0 else made

    lane = lax.broadcasted_iota(jnp.int32, (1, 128), 1)
    halves = [f32(lane < 64).astype(BF), f32(lane >= 64).astype(BF)]
    low = lax.broadcasted_iota(jnp.int32, (WTOK, 128), 1) < 64

    def scores_of(step):
        w, lo = step // 4, step % 4 * 128
        rows = slice(w * WTOK, w * WTOK + WTOK)
        query, keys = s.qkv[rows, lo : lo + 128], s.qkv[rows, D + lo : D + lo + 128]
        return [nt(keys, query * halves[half]) for half in range(2)]

    ahead_scores = scores_of(0)
    for step in range(8):
        w, lo = step // 4, step % 4 * 128
        rows = slice(w * WTOK, w * WTOK + WTOK)
        scores = ahead_scores
        if step < 7:
            ahead_scores = scores_of(step + 1)
        values = s.qkv[rows, 2 * D + lo : 2 * D + lo + 128]
        scores = [jnp.where(same, one, -1e30) for one in scores]
        expo = [jnp.exp(one - jnp.max(one, axis=0, keepdims=True)) for one in scores]
        probs = [one * (1.0 / jnp.sum(one, axis=0, keepdims=True)) for one in expo]
        for half in range(2):
            s.probs[step * 2 + half] = probs[half]
        out = [tn(one.astype(BF), values) for one in probs]
        s.attn[rows, lo : lo + 128] = jnp.where(low, out[0], out[1]).astype(BF)

    wait([own_proj])
    hidden = (f32(s.rolled[...]) + nn(s.attn[...], s.w_proj[...])).astype(BF)
    s.first_out[...] = nn(s.moves[1248:1296, 0:TOK], hidden).astype(BF)
    s.last_out[...] = nn(s.moves[1296:1344, 0:TOK], hidden).astype(BF)
    rims = [push(s.first_out, s.first_in, back[1]), push(s.last_out, s.last_in, ahead[1])]

    parts = nn(s.moves[576:960, 0:TOK], hidden)
    wait([own_merge] + to_north)
    cot_own = jnp.concatenate([s.cot[x], s.cot_below[...]], axis=0).reshape(MALL, D2)
    g = [f32(nt(cot_own, s.w_merge[r * D : r * D + D, :]).astype(BF)) for r in range(4)]
    wait(rims)
    cot_sends += gather_cot(1, slice(2, 3)) + gather_cot(3, slice(2, 3)) + gather_cot(2, slice(2, 3))
    above = nn(s.moves[1536:1728, 0:RIM], s.last_in[...])
    below = nn(s.moves[1344:1536, 0:RIM], s.first_in[...])
    corner = [parts[r * MALL : r * MALL + MALL] for r in range(4)]
    corner = [corner[0] + above[:MALL], corner[1] + above[MALL:], corner[2] + below[:MALL], corner[3] + below[MALL:]]
    mean = sum(jnp.sum(c, axis=-1, keepdims=True) for c in corner) * (1.0 / 2048)
    corner = [c - mean for c in corner]
    var = sum(jnp.sum(c * c, axis=-1, keepdims=True) for c in corner) * (1.0 / 2048)
    m_inverse = lax.rsqrt(var + EPS)
    corner = [c * m_inverse for c in corner]
    for r in range(4):
        s.merge_in[:, r * D : r * D + D] = corner[r].astype(BF)
    merge_sends = []
    for half in range(2):
        lanes = slice(half * 256, half * 256 + 256)
        for k, t in far_first(xs):
            at = pl.multiple_of(half * 1024 + t * 256, 256)
            merge_sends.append(push(s.merge_in.at[0:MPAD, pl.ds(at, 256)], s.merges.at[x, :, lanes], x_chips[k]))
        s.merges[x, :, lanes] = s.merge_in[0:MPAD, pl.ds(pl.multiple_of(half * 1024 + x * 256, 256), 256)]

    mean_g = sum(jnp.sum(d, axis=-1, keepdims=True) for d in g) * (1.0 / 2048)
    mean_gx = sum(jnp.sum(d * c, axis=-1, keepdims=True) for d, c in zip(g, corner)) * (1.0 / 2048)
    d_corner = jnp.concatenate([m_inverse * (d - mean_g - c * mean_gx) for d, c in zip(g, corner)], axis=0).astype(BF)
    d_hidden = nn(s.moves[960:1248], d_corner).astype(BF)
    s.d_hidden[...] = d_hidden

    s.d_attn[...] = nt(d_hidden, s.w_proj[...]).astype(BF)
    for w in range(2):
        rows = slice(w * WTOK, w * WTOK + WTOK)
        for pair in range(4):
            lo = pair * 128
            grad = s.d_attn[rows, lo : lo + 128]
            d_values = [nn(s.probs[w * 8 + pair * 2 + half].astype(BF), grad) for half in range(2)]
            s.d_qkv[rows, 2 * D + lo : 2 * D + lo + 128] = jnp.where(low, d_values[0], d_values[1]).astype(BF)

    grad_proj = by_x(tn(s.d_hidden[...], s.attn[...])).astype(BF)
    for j in range(32):
        s.c0[j // 4, (j // 2) % 2, j % 2, 48:64] = grad_proj[16 * j : 16 * j + 16]
    normed = s.normed[...]

    def grad_qkv(part):
        made = tn(s.d_qkv[:, part * D : part * D + D], normed)
        moved = by_x(made).astype(BF)
        made = made.astype(BF)
        for block in range(part * 32, part * 32 + 32):
            j, third = block // 3, block % 3
            rows = (moved if third == 2 else made)[16 * block - part * D : 16 * block - part * D + 16]
            s.c0[j // 4, (j // 2) % 2, j % 2, 16 * third : 16 * third + 16] = rows

    def to_core(span):
        return push(s.c0.at[span, :, 1 - core], s.c0_in.at[span], other_core)

    def to_axes(span, copy):
        copy.wait()

        @pl.loop(span.start, span.stop)
        def _(step):
            for row in range(2):
                s.c1[step, row] = (f32(s.c0[step, row, core]) + f32(s.c0_in[step, row])).astype(BF)

        return [
            push(
                s.c1.at[span, t % 2, 0:32, pl.ds(pl.multiple_of((t // 2) * 256, 256), 256)],
                s.a1_in.at[k, span],
                y_chips[k],
            )
            for k, t in far_first(ys)
        ] + [
            push(
                s.c1.at[span, :, 32:64, pl.ds(pl.multiple_of(t * 128, 128), 128)], s.b1_in.at[k, span], x_chips[k]
            )
            for k, t in far_first(xs)
        ]

    def to_other_axes(span, copies):
        wait(copies)

        @pl.loop(span.start, span.stop)
        def _(step):
            total = f32(s.c1[step, y_lo, 0:32, pl.ds(pl.multiple_of(y_hi * 256, 256), 256)])
            for k in range(3):
                total = total + f32(s.a1_in[k, step])
            s.a2[step] = total.astype(BF)
            for row in range(2):
                total = f32(s.c1[step, row, 32:64, pl.ds(pl.multiple_of(x * 128, 128), 128)])
                for k in range(3):
                    total = total + f32(s.b1_in[k, step, row])
                s.b2[step, row] = total.astype(BF)

        return [
            push(
                s.a2.at[span, :, pl.ds(pl.multiple_of((t // 2) * 128, 128), 128)], s.a2_in.at[k, span], x_chips[k]
            )
            for k, t in far_first(xs)
        ] + [push(s.b2.at[span, t % 2], s.b2_in.at[k, span], y_chips[k]) for k, t in far_first(ys)]

    chunks = [slice(6, 8), slice(0, 2), slice(2, 6)]
    grad_qkv(2)
    core_copies = [to_core(chunks[0])]
    axis_copies = []

    def d_probs_of(step):
        w, lo = step // 4, step % 4 * 128
        rows = slice(w * WTOK, w * WTOK + WTOK)
        values, grad = s.qkv[rows, 2 * D + lo : 2 * D + lo + 128], s.d_attn[rows, lo : lo + 128]
        return [nt(values, grad * halves[half]) for half in range(2)]

    ahead_d_probs = d_probs_of(0)
    for step in range(8):
        w, lo = step // 4, step % 4 * 128
        rows = slice(w * WTOK, w * WTOK + WTOK)
        d_probs = ahead_d_probs
        if step < 7:
            ahead_d_probs = d_probs_of(step + 1)
        query = s.qkv[rows, lo : lo + 128]
        keys = s.qkv[rows, D + lo : D + lo + 128]
        probs = [s.probs[step * 2 + half] for half in range(2)]
        dots = [jnp.sum(d * p, axis=0, keepdims=True) for d, p in zip(d_probs, probs)]
        d_scores = [(p * (d - dot)).astype(BF) for d, p, dot in zip(d_probs, probs, dots)]
        d_query = [tn(one, keys) for one in d_scores]
        d_keys = [nn(one, query) for one in d_scores]
        s.d_qkv[rows, lo : lo + 128] = (jnp.where(low, d_query[0], d_query[1]) * 0.125).astype(BF)
        s.d_qkv[rows, D + lo : D + lo + 128] = jnp.where(low, d_keys[0], d_keys[1]).astype(BF)
        if step == 3:
            axis_copies.append(to_axes(chunks[0], core_copies[0]))

    grad_qkv(0)
    core_copies.append(to_core(chunks[1]))
    grad_qkv(1)
    core_copies.append(to_core(chunks[2]))
    axis_copies.append(to_axes(chunks[1], core_copies[1]))

    wait(cot_sends + merge_sends)
    for slot in range(4):
        rows = [f32(s.cot[slot].reshape(MTOK, D2)), jnp.zeros((MPAD - MTOK, D2), F32)]
        s.cots[slot] = jnp.concatenate(rows, axis=0).astype(BF)
    merges = s.merges[...].reshape(4 * MPAD, 512)
    for part in range(4):
        cots = s.cots[:, :, part * 256 : part * 256 + 256].reshape(4 * MPAD, 256)
        made = tn(cots, merges).astype(BF)
        s.m0[2 * part : 2 * part + 2] = made.reshape(2, 2, 2, 32, 512)
    m_copy = push(s.m0.at[:, :, 1 - core], s.m0_in, other_core)


    axis_copies.append(to_axes(chunks[2], core_copies[2]))
    other_copies = [to_other_axes(chunks[0], axis_copies[0])]
    for part in range(2):
        cols = slice(part * D, part * D + D)
        made = nn(s.merge_in[0:MPAD], s.w_merge[:, cols])[:MTOK].astype(BF)
        s.merged[:, :, :, cols] = made.reshape(3, 6, 4, D)

    wait([m_copy])

    @pl.loop(0, 8)
    def _(step):
        for row in range(2):
            s.m1[step, row] = (f32(s.m0[step, row, core]) + f32(s.m0_in[step, row])).astype(BF)

    m_copies = [push(s.m1.at[t], s.m1_in.at[k], z_chips[k]) for k, t in far_first(zs)]
    other_copies.append(to_other_axes(chunks[1], axis_copies[1]))

    d_normed = nt(s.d_qkv[:, 0:D], s.w_qkv[:, 0:D])
    for part in range(1, 3):
        cols = slice(part * D, part * D + D)
        d_normed = d_normed + nt(s.d_qkv[:, cols], s.w_qkv[:, cols])
    d_tokens = (f32(s.d_hidden[...]) + norm_back(s.xhat[...], inverse, d_normed)).astype(BF)
    s.d_tokens[...] = nn(s.moves[288:576, 0:TOK], d_tokens).astype(BF).reshape(4, 3, 6, 4, D)

    other_copies.append(to_other_axes(chunks[2], axis_copies[2]))
    last_sends = [
        push(s.merged.at[0:2, 3:6], merged_out.at[1:3, 0:3], ahead[0]),
        push(s.merged.at[2:3, 0:3], merged_out.at[0:1, 3:6], ahead[1]),
        push(s.merged.at[2:3, 3:6], merged_out.at[0:1, 0:3], ahead[2]),
        fetch(s.merged.at[0:2, 0:3], merged_out.at[1:3, 3:6]),
        push(s.d_tokens.at[1], tokens_out.at[3:6, 0:6], ahead[0]),
        push(s.d_tokens.at[2], tokens_out.at[0:3, 6:12], ahead[1]),
        push(s.d_tokens.at[3], tokens_out.at[0:3, 0:6], ahead[2]),
        fetch(s.d_tokens.at[0], tokens_out.at[3:6, 6:12]),
    ]
    for copies in other_copies:
        wait(copies)
    left = lax.broadcasted_iota(jnp.int32, (32, 128), 1) < 64

    @pl.loop(0, 8)
    def _(step):
        one = f32(s.a2[step, :, pl.ds(pl.multiple_of((x // 2) * 128, 128), 128)])
        two = f32(s.b2[step, y_lo])
        for k in range(3):
            one = one + f32(s.a2_in[k, step])
            two = two + f32(s.b2_in[k, step])
        one = jnp.where(x % 2 == 1, pltpu.roll(one, 64, 1), one)
        two = jnp.where(y_hi == 0, pltpu.roll(two, 64, 1), two)
        s.c3[step] = jnp.where(left, one, two).astype(BF)

    c_copies = [push(s.c3.at[t], s.c3_in.at[k], z_chips[k]) for k, t in far_first(zs)]
    wait(m_copies)
    total = f32(s.m1[z])
    for k in range(7):
        total = total + f32(s.m1_in[k])
    s.m2[...] = total.astype(BF)
    m_copies = [
        push(s.m2.at[t % 2, :, pl.ds(pl.multiple_of((t // 2) * 256, 256), 256)], s.m2_in.at[k], y_chips[k])
        for k, t in far_first(ys)
    ]
    wait(c_copies)
    total = f32(s.c3[z])
    for k in range(7):
        total = total + f32(s.c3_in[k])
    qkv_out[0:32] = total[:, :64]
    qkv_out[32:48] = total[:16, 64:]
    proj_out[...] = total[16:, 64:]
    wait(m_copies)
    total = f32(s.m2[y_lo, :, pl.ds(pl.multiple_of(y_hi * 256, 256), 256)])
    for k in range(3):
        total = total + f32(s.m2_in[k])
    merge_out[...] = total
    wait(last_sends)


def hand_over(*refs):
    held, done = refs[10:15], refs[15]
    into = [pltpu.make_async_copy(refs[k], held[k], done.at[k]) for k in range(5)]
    out = [pltpu.make_async_copy(held[k], refs[5 + k], done.at[5 + k]) for k in range(5)]
    for copy in into:
        copy.start()
    for one, two in zip(into, out):
        one.wait()
        two.start()
    for copy in out:
        copy.wait()


def shards(tokens, region, w_qkv, w_proj, w_merge, cotangent):
    hbm = pl.BlockSpec(memory_space=pltpu.HBM)
    vmem = pl.BlockSpec(memory_space=pltpu.VMEM)
    made = pl.pallas_call(
        kernel,
        out_shape=(
            jax.ShapeDtypeStruct((3, 6, 4, D2), BF),
            jax.ShapeDtypeStruct((6, 12, 4, D), BF),
            jax.ShapeDtypeStruct((48, 64), F32),
            jax.ShapeDtypeStruct((16, 64), F32),
            jax.ShapeDtypeStruct((32, 256), F32),
        ),
        in_specs=[hbm, vmem, hbm, hbm, hbm, hbm, hbm],
        out_specs=(hbm, hbm, vmem, vmem, vmem),
        scratch_shapes=list(SCRATCH.values()),
        compiler_params=pltpu.CompilerParams(
            collective_id=0, has_side_effects=True, vmem_limit_bytes=56 * 1024 * 1024
        ),
    )(tokens, region, w_qkv, w_proj, w_merge, cotangent, jnp.asarray(one_hot_moves()))
    merged, grad_tokens, grad_qkv, grad_proj, grad_merge = pl.pallas_call(
        hand_over,
        out_shape=tuple(jax.ShapeDtypeStruct(a.shape, a.dtype) for a in made),
        in_specs=[hbm] * 5,
        out_specs=(hbm,) * 5,
        scratch_shapes=[pltpu.VMEM(a.shape, a.dtype) for a in made] + [pltpu.SemaphoreType.DMA((10,))],
        compiler_params=pltpu.CompilerParams(vmem_limit_bytes=56 * 1024 * 1024),
    )(*made)
    return (merged, grad_tokens, grad_qkv.T, grad_proj.T, grad_merge.T)


def solution(mesh):
    return jax.shard_map(
        shards,
        mesh=mesh,
        in_specs=(
            P("lat", "lon", None, None),
            P("lat", "lon"),
            P(),
            P(),
            P(),
            P("lat", "lon", None, None),
        ),
        out_specs=(
            P("lat", "lon", None, None),
            P("lat", "lon", None, None),
            P("lat", "lon"),
            P("lat", "lon"),
            P("lat", "lon"),
        ),
        check_vma=False,
    )
```
